32 devices in a mesh: rows: 4 (over y, core), cols: 8 (over z, x).
Axes of the slice: x: 2, y: 2, z: 4, core: 2. Of those that a mesh axis runs over, the one named last changes fastest.
Arguments:
- kernel: float32 [4096, 16384], P('rows', 'cols'), may hold values from -0.09375 to 0.09375
- slip_delta: float32 [64, 32, 128], P('cols', 'rows'), may hold values from -6 to 6
- block_list: int32 [64, 32], P('cols', 'rows'), may hold values from 0 to 127, as said below
- live_count: int32 [64], P('cols'), may hold values from 1 to 32, 1024 in all
- direct_effect: float32 [4096], P(('rows', 'cols')), may hold values from 0.5 to 2
- load_rate: float32 [4096], P(('rows', 'cols')), may hold values from 0.02 to 0.2
- time_before: float32 [4096], P(('rows', 'cols')), may hold values from 1 to 50
Outputs:
- stress_change: float32 [4096, 64], P(('rows', 'cols'))
- log_time: float32 [4096, 64], P(('rows', 'cols'))
The draws below stay inside these ranges and needn't reach their ends.
Inputs may be any that keep to these rules, and one draw needn't show every extreme that they name: The first live_count[e] entries of row e of block_list are distinct block numbers; the rest of the row are padding.
All inputs are finite; a program needn't handle non-finite values. No bound on the sum of `live_count` on one device may be relied on, other than what follows from the above.
Results may differ from the reference program's by a relative error of at most 0.00007.
Values sent between devices are 32-bit elements; how exact they have to be, the bound alone decides.
No kernel may reach another device: no remote copies, remote signals or barrier semaphores. Data moves between devices by JAX's collectives and lax.ppermute only.
A program may use at most 64 MiB of HBM per device.

```python
import math
import jax
import jax.numpy as jnp
import numpy as np
from jax import lax

BLOCK = 128
EVENTS = 64
LIST = 32
NR = 4096
NB = 128
NS = 16384


def draw_block_list(key, part):
    event_keys = jax.random.split(jax.random.fold_in(key, 11), EVENTS)
    shuffled = jax.vmap(lambda k: jax.random.permutation(k, NB))(event_keys)[:, :LIST].astype(jnp.int32)
    inner = jax.random.permutation(jax.random.fold_in(key, 12), NB - 2)[:LIST - 2].astype(jnp.int32) + 1
    first_row = jnp.concatenate([jnp.array([0, NB - 1], jnp.int32), inner])
    first_row = jax.random.permutation(jax.random.fold_in(key, 13), first_row).astype(jnp.int32)
    return shuffled.at[0].set(first_row)


def steps_of(own_key, extent, cuts, low, top_value):
    loudness = 1.0
    for dim, shards_of in cuts:
        draws = jax.random.uniform(jax.random.fold_in(jax.random.fold_in(own_key, 6), dim), (shards_of,), jnp.float32, low / len(cuts), top_value / len(cuts))
        loudness = loudness * jnp.repeat(jnp.exp(draws), extent[dim] // shards_of).reshape((-1,) + (1,) * (len(extent) - 1 - dim))
    return loudness


def profile(count, total, limit, skew):
    weights = [(1 << 20) // math.isqrt(standing ** skew) + 1 for standing in range(2, count + 1)]
    surplus, holding = total - limit - (count - 1), [1] * (count - 1)
    while surplus > 0:
        candidates = [i for i in range(count - 1) if holding[i] < limit]
        whole, left = sum([weights[i] for i in candidates]), surplus
        for i in candidates:
            addition = min(limit - holding[i], max(1, left * weights[i] // whole), surplus)
            holding[i] = holding[i] + addition
            surplus = surplus - addition
    return np.array([limit] + holding)


def uneven(rng, number_of, total, most, lean):
    if number_of == 2:
        one = jax.random.randint(rng, (), max(1, total - most), min(most, total - 1) + 1)
        return jnp.stack([one, total - one])
    tallies = jnp.asarray(profile(number_of, total, most, lean), jnp.int32)
    twos = (number_of - 1) // 2
    source_of, sink = tallies[1:1 + 2 * twos:2], tallies[2:2 + 2 * twos:2]
    room = jnp.minimum(source_of - 1, most - sink)
    shifted = jax.random.randint(jax.random.fold_in(rng, 1), (twos,), 0, 1 << 20) % (room + 1)
    tallies = tallies.at[1:1 + 2 * twos:2].set(source_of - shifted).at[2:2 + 2 * twos:2].set(sink + shifted)
    return tallies[jax.random.permutation(jax.random.fold_in(rng, 2), number_of)]


def bell_draw(own_key, extent, spread, most, shards=(), kind=jnp.bfloat16):
    loudness = steps_of(own_key, extent, shards, -0.22, 0.18) if shards else 1.0
    values = jax.random.normal(own_key, extent, jnp.float32) * spread * loudness
    return jnp.minimum(jnp.maximum(values, -most), most).astype(kind)


def setup_inputs(seed: int = 0) -> dict:
    seeds = jax.random.split(jax.random.key(seed), 8)
    kernel = bell_draw(seeds[0], (NR, NS), (LIST * BLOCK) ** -0.5, 0.09375, ((0, 4), (1, 8)), jnp.float32)
    slip_delta = bell_draw(seeds[1], (EVENTS, LIST, BLOCK), 1.0, 6.0, ((0, 8), (1, 4)), jnp.float32)
    block_list = draw_block_list(jax.random.fold_in(seeds[7], 71), 0)
    live_count = uneven(seeds[3], EVENTS, EVENTS * LIST // 2, LIST, 2).astype(jnp.int32)
    direct_effect = jnp.clip(jnp.exp(math.log(2.0) - 1.3862944 * jax.random.uniform(seeds[4], (NR,), jnp.float32) ** steps_of(seeds[4], (NR,), ((0, 32),), -0.2, 0.2)), 0.5, 2.0)
    load_rate = jnp.clip(jnp.exp(math.log(0.2) - 2.3025851 * jax.random.uniform(seeds[5], (NR,), jnp.float32) ** steps_of(seeds[5], (NR,), ((0, 32),), -0.2, 0.2)), 0.02, 0.2)
    time_before = jnp.clip(jnp.exp(math.log(50.0) - 3.912023 * jax.random.uniform(seeds[6], (NR,), jnp.float32) ** steps_of(seeds[6], (NR,), ((0, 32),), -0.2, 0.2)), 1.0, 50.0)
    return dict(kernel=kernel, slip_delta=slip_delta, block_list=block_list, live_count=live_count, direct_effect=direct_effect, load_rate=load_rate, time_before=time_before)


def reference(kernel, slip_delta, block_list, live_count, direct_effect, load_rate, time_before):
    live_mask = (jnp.arange(LIST, dtype=jnp.int32)[None, :] < live_count[:, None]).astype(jnp.float32)
    event_rows = jnp.broadcast_to(jnp.arange(EVENTS, dtype=jnp.int32)[:, None], (EVENTS, LIST))
    dense_slip = jnp.zeros((EVENTS, NB, BLOCK), jnp.float32)
    dense_slip = dense_slip.at[event_rows, block_list].add(slip_delta * live_mask[:, :, None])
    dense_slip = dense_slip.reshape(EVENTS, NS)
    stress_change = lax.dot_general(kernel, dense_slip, (((1,), (1,)), ((), ())), precision=lax.Precision.HIGHEST, preferred_element_type=jnp.float32)
    scale = direct_effect[:, None]
    growth = jnp.expm1(load_rate * time_before / direct_effect)[:, None]
    log_time = jnp.log(scale / load_rate[:, None]) + jnp.log(jnp.log1p(jnp.exp(-stress_change / scale) * growth))
    return stress_change, log_time
```

```python
import math

import jax
import jax.numpy as jnp
import numpy as np
from jax import lax
from jax.sharding import PartitionSpec as P

BLOCK = 128


def gather_rows(block, width):
    held = block[None]
    step = width // 2
    while step:
        other = lax.ppermute(held, "rows", [(r, r ^ step) for r in range(width)])
        held = jnp.concatenate([held, other], axis=0)
        step //= 2
    bits = width.bit_length() - 1
    slot = np.array([int(f"{k:0{bits}b}"[::-1], 2) for k in range(width)], np.int32)
    mine = lax.axis_index("rows")
    return jnp.take(held, jnp.asarray(slot)[mine ^ jnp.arange(width, dtype=jnp.int32)], axis=0)


def per_device(kernel, slip_delta, block_list, live_count, direct_effect, load_rate, time_before):
    width = lax.axis_size("cols")
    height = lax.axis_size("rows")
    my_row = lax.axis_index("rows")
    events_here, entries_here = block_list.shape
    blocks_here = kernel.shape[1] // BLOCK
    split = math.gcd(events_here, height)
    parts = height // split
    blocks_part = blocks_here // parts
    group = events_here // split

    entry = my_row * entries_here + jnp.arange(entries_here, dtype=jnp.int32)
    ids = jnp.where(entry[None, :] < live_count[:, None], block_list, -1).astype(jnp.float32)
    ids = jnp.pad(ids, ((0, 0), (0, BLOCK - entries_here)))
    packed = jnp.concatenate(
        [
            slip_delta.reshape(split, group * entries_here, BLOCK),
            ids.reshape(split, group, BLOCK),
        ],
        axis=1,
    )
    packed = jnp.repeat(packed, parts, axis=0)
    packed = lax.all_to_all(packed, "rows", 0, 0, tiled=True)
    slips = packed[:, : group * entries_here].reshape(height, group, entries_here, BLOCK)
    ids = packed[:, group * entries_here :, :entries_here]
    block = jnp.arange(width * blocks_here, dtype=jnp.float32)
    onehot = (ids[..., None] == block).astype(jnp.float32)
    dense = jnp.einsum("hgbj,hgbc->jgc", onehot, slips, precision=lax.Precision.HIGHEST)
    dense = dense.reshape(width, parts, blocks_part, group, BLOCK)
    if parts > 1:
        dense = lax.dynamic_index_in_dim(dense, my_row % parts, 1, keepdims=True)
    dense = dense.reshape(width, blocks_part, group, BLOCK)
    dense = lax.all_to_all(dense, "cols", 0, 0, tiled=True)
    held = gather_rows(dense, height)
    held = held.reshape(split, parts, width, blocks_part, group, BLOCK)
    held = held.transpose(2, 0, 4, 1, 3, 5).reshape(width * events_here, blocks_here * BLOCK)
    partial_sum = lax.dot_general(
        held,
        kernel,
        (((1,), (1,)), ((), ())),
        precision=lax.Precision.HIGH,
        preferred_element_type=jnp.float32,
    )
    share_rows = kernel.shape[0] // width
    partial_sum = partial_sum.reshape(held.shape[0], width, share_rows).transpose(1, 0, 2)
    stress_change = jnp.sum(lax.all_to_all(partial_sum, "cols", 0, 0, tiled=True), axis=0)
    scale = direct_effect[None, :]
    growth = jnp.expm1(load_rate * time_before / direct_effect)[None, :]
    log_time = jnp.log(scale / load_rate[None, :]) + jnp.log(
        jnp.log1p(jnp.exp(-stress_change / scale) * growth)
    )
    return (stress_change.T, log_time.T)


def solution(mesh):
    in_specs = (
        P("rows", "cols"),
        P("cols", "rows", None),
        P("cols", "rows"),
        P("cols"),
        P(("rows", "cols")),
        P(("rows", "cols")),
        P(("rows", "cols")),
    )
    out_specs = (P(("rows", "cols"), None), P(("rows", "cols"), None))
    return jax.shard_map(
        per_device, mesh=mesh, in_specs=in_specs, out_specs=out_specs, check_vma=False
    )
```

```python
import functools
import math

import jax
import jax.numpy as jnp
from jax import lax
from jax.experimental import pallas as pl
from jax.experimental.pallas import tpu as pltpu
from jax.sharding import PartitionSpec as P

BLOCK = 128
SUB = 8
VMEM_SPEC = pl.BlockSpec(memory_space=pltpu.VMEM)
SMEM_SPEC = pl.BlockSpec(memory_space=pltpu.SMEM)
MIB = 1024 * 1024


def f32(*shape):
    return jax.ShapeDtypeStruct(shape, jnp.float32)


def send_xor(block, axis, width, k):
    return lax.ppermute(block, axis, [(r, r ^ k) for r in range(width)])


def pack_body(height, parts, group, me_ref, slip_ref, list_ref, count_ref, *refs):
    out_refs, ids = refs[:height], refs[height]
    events, entries = list_ref.shape
    row = me_ref[0]
    lane = lax.broadcasted_iota(jnp.int32, (events, entries), 1) + row * entries
    event = lax.broadcasted_iota(jnp.int32, (events, entries), 0)
    count = jnp.zeros((events, entries), jnp.int32)
    for e in range(events):
        count = jnp.where(event == e, count_ref[e], count)
    ids[...] = jnp.full(ids.shape, -1.0, jnp.float32)
    ids[0:events, 0:entries] = jnp.where(lane < count, list_ref[...], -1).astype(jnp.float32)
    placed = pltpu.roll(ids[...], row * entries, 1)
    ids[...] = placed
    for k in range(height):
        first = ((row ^ k) // parts) * group
        for i in range(group):
            out_refs[k][i, 0:entries, :] = slip_ref[first + i]
            out_refs[k][i, SUB : 2 * SUB, :] = jnp.broadcast_to(ids[pl.ds(first + i, 1), :], (SUB, BLOCK))


def densify_body(height, width, parts, blocks_here, entries, me_ref, *refs):
    ins, outs, dense = refs[:height], refs[height : height + width], refs[-1]
    group = ins[0].shape[0]
    row, col = me_ref[0], me_ref[1]
    blocks_part = blocks_here // parts
    blocks = width * blocks_here
    for i in range(group):
        ids = ins[0][i, SUB : 2 * SUB, :]
        for k in range(1, height):
            ids = jnp.maximum(ids, ins[k][i, SUB : 2 * SUB, :])
        ids = jnp.concatenate([ids] * (blocks // SUB), axis=0)[:, : height * entries]
        number = lax.broadcasted_iota(jnp.int32, ids.shape, 0).astype(jnp.float32)
        onehot = (ids == number).astype(jnp.bfloat16)
        slips = dense.at[i, 0 : height * entries, :]
        for k in range(height):
            slips[pl.ds(pl.multiple_of((row ^ k) * entries, entries), entries), :] = ins[k][i, 0:entries, :]
        slip = slips[...]
        total = jnp.zeros((blocks, BLOCK), jnp.float32)
        for _ in range(3):
            piece = slip.astype(jnp.bfloat16)
            slip = slip - piece.astype(jnp.float32)
            total = total + jnp.dot(onehot, piece, preferred_element_type=jnp.float32)
        dense[i] = total
        part = (row % parts) * blocks_part
        for k in range(width):
            start = pl.multiple_of((col ^ k) * blocks_here + part, blocks_part)
            outs[k][i] = dense[i, pl.ds(start, blocks_part), :]


def stress_body(height, width, parts, me_ref, *refs):
    slips, (kernel_ref, out_ref, dense, stacked) = refs[:-4], refs[-4:]
    events, blocks_here, _ = dense.shape
    row, col = me_ref[0], me_ref[1]
    group, blocks_part = slips[0].shape[1], slips[0].shape[2]
    split = height // parts

    @pl.when(pl.program_id(0) == 0)
    def _():
        for kr in range(height):
            source = row ^ kr
            for kc in range(width):
                first = (col ^ kc) * (events // width) + (source // parts) * group
                for i in range(group):
                    where = pl.ds(pl.multiple_of((source % parts) * blocks_part, blocks_part), blocks_part)
                    if parts == 1:
                        where = slice(None)
                    dense[first + i, where, :] = slips[kr][kc, i]
        flat = dense.reshape(events * blocks_here, BLOCK)
        for t in range(events // SUB):
            for b in range(blocks_here):
                stacked[t * SUB : (t + 1) * SUB, b * BLOCK : (b + 1) * BLOCK] = flat[
                    pl.ds(t * SUB * blocks_here + b, SUB, stride=blocks_here), :
                ]

    slip = stacked[...]
    slip_hi = slip.astype(jnp.bfloat16)
    slip_lo = (slip - slip_hi.astype(jnp.float32)).astype(jnp.bfloat16)
    both = jnp.concatenate([slip_hi, slip_lo], axis=0)
    block = kernel_ref[...]
    block_hi = block.astype(jnp.bfloat16)
    block_lo = (block - block_hi.astype(jnp.float32)).astype(jnp.bfloat16)
    dims = (((1,), (1,)), ((), ()))
    first = lax.dot_general(both, block_hi, dims, preferred_element_type=jnp.float32)
    second = lax.dot_general(slip_hi, block_lo, dims, preferred_element_type=jnp.float32)
    total = first[:events] + first[events:] + second
    share = out_ref.shape[2]
    for j in range(out_ref.shape[0]):
        out_ref[j] = total[:, j * share : (j + 1) * share]


def per_device(kernel, slip_delta, block_list, live_count, direct_effect, load_rate, time_before):
    width = lax.axis_size("cols")
    height = lax.axis_size("rows")
    events_here, entries = block_list.shape
    events = events_here * width
    receivers, sources = kernel.shape
    blocks_here = sources // BLOCK
    split = math.gcd(events_here, height)
    parts = height // split
    group = events_here // split
    blocks_part = blocks_here // parts
    me = jnp.stack([lax.axis_index("rows"), lax.axis_index("cols")]).astype(jnp.int32)

    message = f32(group, 2 * SUB, BLOCK)
    packed = pl.pallas_call(
        functools.partial(pack_body, height, parts, group),
        out_shape=[message] * height,
        in_specs=[SMEM_SPEC, VMEM_SPEC, VMEM_SPEC, SMEM_SPEC],
        out_specs=[VMEM_SPEC] * height,
        scratch_shapes=[pltpu.VMEM((SUB, BLOCK), jnp.float32)],
        compiler_params=pltpu.CompilerParams(vmem_limit_bytes=8 * MIB),
        name="pack",
    )(me, slip_delta, block_list, live_count)
    packed = [packed[0]] + [send_xor(packed[k], "rows", height, k) for k in range(1, height)]

    dense = pl.pallas_call(
        functools.partial(densify_body, height, width, parts, blocks_here, entries),
        out_shape=[f32(group, blocks_part, BLOCK)] * width,
        in_specs=[SMEM_SPEC] + [VMEM_SPEC] * height,
        out_specs=[VMEM_SPEC] * width,
        scratch_shapes=[pltpu.VMEM((group, width * blocks_here, BLOCK), jnp.float32)],
        compiler_params=pltpu.CompilerParams(vmem_limit_bytes=8 * MIB),
        name="densify",
    )(me, *packed)
    dense = [dense[0]] + [send_xor(dense[k], "cols", width, k) for k in range(1, width)]

    held = [jnp.stack(dense)]
    step = height // 2
    while step:
        sent = jnp.stack(held) if len(held) > 1 else held[0][None]
        came = send_xor(sent, "rows", height, step)
        held = [x for j in range(len(held)) for x in (held[j], came[j])]
        step //= 2

    steps = 4
    share = receivers // width
    per_step = width // steps
    partial_sum = pl.pallas_call(
        functools.partial(stress_body, height, width, parts),
        out_shape=f32(width, events, share),
        grid=(steps,),
        in_specs=[SMEM_SPEC]
        + [pl.BlockSpec(h.shape, lambda s: (0, 0, 0, 0)) for h in held]
        + [pl.BlockSpec((receivers // steps, sources), lambda s: (s, 0))],
        out_specs=pl.BlockSpec((per_step, events, share), lambda s: (s, 0, 0)),
        scratch_shapes=[
            pltpu.VMEM((events, blocks_here, BLOCK), jnp.float32),
            pltpu.VMEM((events, sources), jnp.float32),
        ],
        compiler_params=pltpu.CompilerParams(vmem_limit_bytes=32 * MIB),
        cost_estimate=pl.CostEstimate(
            flops=6 * receivers * sources * events,
            bytes_accessed=4 * receivers * sources,
            transcendentals=0,
        ),
        name="stress",
    )(me, *held, kernel)

    col = lax.axis_index("cols")
    stress_change = lax.dynamic_index_in_dim(partial_sum, col, 0, keepdims=False)
    for k in range(1, width):
        mine = lax.dynamic_index_in_dim(partial_sum, col ^ k, 0, keepdims=False)
        stress_change = stress_change + send_xor(mine, "cols", width, k)
    scale = direct_effect[None, :]
    growth = jnp.expm1(load_rate * time_before / direct_effect)[None, :]
    log_time = jnp.log(scale / load_rate[None, :]) + jnp.log(
        jnp.log1p(jnp.exp(-stress_change / scale) * growth)
    )
    return (stress_change.T, log_time.T)


def solution(mesh):
    in_specs = (
        P("rows", "cols"),
        P("cols", "rows", None),
        P("cols", "rows"),
        P("cols"),
        P(("rows", "cols")),
        P(("rows", "cols")),
        P(("rows", "cols")),
    )
    out_specs = (P(("rows", "cols"), None), P(("rows", "cols"), None))
    return jax.shard_map(
        per_device, mesh=mesh, in_specs=in_specs, out_specs=out_specs, check_vma=False
    )
```

```python
import functools

import jax
import jax.numpy as jnp
from jax import lax
from jax.experimental import pallas as pl
from jax.experimental.pallas import tpu as pltpu
from jax.sharding import PartitionSpec as P

BLOCK = 128
SUB = 8
VMEM_SPEC = pl.BlockSpec(memory_space=pltpu.VMEM)
SMEM_SPEC = pl.BlockSpec(memory_space=pltpu.SMEM)
HBM_SPEC = pl.BlockSpec(memory_space=pltpu.HBM)
MIB = 1024 * 1024
NT = (((1,), (1,)), ((), ()))


def f32(*shape):
    return jax.ShapeDtypeStruct(shape, jnp.float32)


def bf16(*shape):
    return jax.ShapeDtypeStruct(shape, jnp.bfloat16)


def params(mib):
    return pltpu.CompilerParams(vmem_limit_bytes=mib * MIB)


def send_xor(block, axis, k):
    return lax.ppermute(block, axis, [(r, r ^ k) for r in range(lax.axis_size(axis))])


def pack_body(me_ref, slip_hbm, list_hbm, count_hbm, out_ref, slip_ref, list_ref, count_ref, ids, sems):
    copies = [
        pltpu.make_async_copy(src, dst, sems.at[j])
        for j, (src, dst) in enumerate(((slip_hbm, slip_ref), (list_hbm, list_ref), (count_hbm, count_ref)))
    ]
    for copy in copies:
        copy.start()
    for copy in copies:
        copy.wait()
    events, entries = list_ref.shape
    half = events // 2
    row = me_ref[0]
    entry = lax.broadcasted_iota(jnp.int32, (events, entries), 1) + row * entries
    event = lax.broadcasted_iota(jnp.int32, (events, entries), 0)
    count = jnp.zeros((events, entries), jnp.int32)
    for e in range(events):
        count = jnp.where(event == e, count_ref[e], count)
    ids[...] = jnp.full(ids.shape, -1.0, jnp.float32)
    ids[0:events, 0:entries] = jnp.where(entry < count, list_ref[...], -1).astype(jnp.float32)
    ids[...] = pltpu.roll(ids[...], row * entries, 1)
    for h in range(2):
        first = ((row % 2) ^ h) * half
        for i in range(half):
            out_ref[h, i, 0:entries, :] = slip_ref[first + i]
            out_ref[h, half, i : i + 1, :] = ids[pl.ds(first + i, 1), :]


def densify_body(entries, me_ref, own_ref, came_ref, out_ref, slips):
    halves, half = own_ref.shape[0], own_ref.shape[1] - 1
    width, _, blocks_here, _ = out_ref.shape
    blocks = width * blocks_here
    live = 2 * halves * entries
    row = me_ref[0]
    for i in range(half):
        ids = jnp.full((1, BLOCK), -1.0, jnp.float32)
        for ref in (own_ref, came_ref):
            for j in range(halves):
                ids = jnp.maximum(ids, ref[j, half, i : i + 1, :])
        ids = jnp.broadcast_to(ids, (blocks, BLOCK))[:, :live]
        number = lax.broadcasted_iota(jnp.int32, ids.shape, 0).astype(jnp.float32)
        onehot = (ids == number).astype(jnp.bfloat16)
        for core, ref in enumerate((own_ref, came_ref)):
            for j in range(halves):
                source = row ^ (2 * j + core)
                slips[i, pl.ds(pl.multiple_of(source * entries, entries), entries), :] = ref[j, i, 0:entries, :]
        slip = slips[i]
        total = jnp.zeros((blocks, BLOCK), jnp.float32)
        for _ in range(3):
            piece = slip.astype(jnp.bfloat16)
            slip = slip - piece.astype(jnp.float32)
            total = total + jnp.dot(onehot, piece, preferred_element_type=jnp.float32)
        out_ref[:, i] = total.reshape(width, blocks_here, BLOCK)


def split_body(kernel_hbm, hi_ref, lo_ref, held, sems):
    steps = held.shape[0]
    rows = held.shape[1]
    copies = [
        pltpu.make_async_copy(kernel_hbm.at[pl.ds(s * rows, rows)], held.at[s], sems.at[s]) for s in range(steps)
    ]
    for copy in copies:
        copy.start()
    for s, copy in enumerate(copies):
        copy.wait()
        block = held[s]
        hi = block.astype(jnp.bfloat16)
        hi_ref[s * rows : (s + 1) * rows, :] = hi
        lo_ref[s * rows : (s + 1) * rows, :] = (block - hi.astype(jnp.float32)).astype(jnp.bfloat16)


def assemble_body(me_ref, own_ref, came_ref, out_ref, dense):
    width, half, blocks_here, _ = own_ref.shape
    events = dense.shape[0]
    core = me_ref[0] % 2
    for c in range(width):
        for other, ref in enumerate((own_ref, came_ref)):
            for i in range(half):
                dense[(2 * c + (core ^ other)) * half + i] = ref[c, i]
    flat = dense.reshape(events * blocks_here, BLOCK)
    for t in range(events // (2 * SUB)):
        for b in range(blocks_here):
            rows = [
                flat[pl.ds((2 * t + u) * SUB * blocks_here + b, SUB, stride=blocks_here), :] for u in range(2)
            ]
            slip = jnp.concatenate(rows, axis=0)
            hi = slip.astype(jnp.bfloat16)
            lo = (slip - hi.astype(jnp.float32)).astype(jnp.bfloat16)
            where = slice(b * BLOCK, (b + 1) * BLOCK)
            out_ref[2 * t * SUB : 2 * (t + 1) * SUB, where] = hi
            out_ref[events + 2 * t * SUB : events + 2 * (t + 1) * SUB, where] = lo


def stress_body(targets, me_ref, slip_ref, hi_ref, lo_ref, out_ref):
    events = slip_ref.shape[0] // 2
    share = out_ref.shape[2]
    col = me_ref[1]
    for j, k in enumerate(targets):
        rows = pl.ds(pl.multiple_of((col ^ k) * share, share), share)
        first = lax.dot_general(slip_ref[...], hi_ref[rows, :], NT, preferred_element_type=jnp.float32)
        second = lax.dot_general(slip_ref[:events, :], lo_ref[rows, :], NT, preferred_element_type=jnp.float32)
        out_ref[j] = first[:events] + first[events:] + second


def halving_order(width):
    bits = width.bit_length() - 1
    return [int(f"{k:0{bits}b}"[::-1], 2) for k in range(width)]


def per_device(kernel, slip_delta, block_list, live_count, direct_effect, load_rate, time_before):
    width = lax.axis_size("cols")
    height = lax.axis_size("rows")
    events_here, entries = block_list.shape
    half = events_here // 2
    events = events_here * width
    receivers, sources = kernel.shape
    blocks_here = sources // BLOCK
    me = jnp.stack([lax.axis_index("rows"), lax.axis_index("cols")]).astype(jnp.int32)

    packed = pl.pallas_call(
        pack_body,
        out_shape=f32(2, half + 1, SUB, BLOCK),
        in_specs=[SMEM_SPEC, HBM_SPEC, HBM_SPEC, HBM_SPEC],
        out_specs=VMEM_SPEC,
        scratch_shapes=[
            pltpu.VMEM(slip_delta.shape, jnp.float32),
            pltpu.VMEM(block_list.shape, jnp.int32),
            pltpu.SMEM(live_count.shape, jnp.int32),
            pltpu.VMEM((SUB, BLOCK), jnp.float32),
            pltpu.SemaphoreType.DMA((3,)),
        ],
        compiler_params=params(4),
        name="pack",
    )(me, slip_delta, block_list, live_count)
    held = packed[None]
    step = 2
    while step < height:
        held = jnp.concatenate([held, send_xor(held, "rows", step)], axis=0)
        step *= 2
    came = send_xor(held[:, 1], "rows", 1)

    dense = pl.pallas_call(
        functools.partial(densify_body, entries),
        out_shape=f32(width, half, blocks_here, BLOCK),
        in_specs=[SMEM_SPEC, VMEM_SPEC, VMEM_SPEC],
        out_specs=VMEM_SPEC,
        scratch_shapes=[pltpu.VMEM((half, height * entries, BLOCK), jnp.float32)],
        compiler_params=params(8),
        name="densify",
    )(me, held[:, 0], came)
    mine = lax.all_to_all(dense, "cols", 0, 0, tiled=True)

    steps = 8
    hi, lo = pl.pallas_call(
        split_body,
        out_shape=[bf16(receivers, sources)] * 2,
        in_specs=[HBM_SPEC],
        out_specs=[VMEM_SPEC] * 2,
        scratch_shapes=[
            pltpu.VMEM((steps, receivers // steps, sources), jnp.float32),
            pltpu.SemaphoreType.DMA((steps,)),
        ],
        compiler_params=params(24),
        cost_estimate=pl.CostEstimate(
            flops=3 * receivers * sources, bytes_accessed=8 * receivers * sources, transcendentals=0
        ),
        name="split",
    )(kernel)

    slips = pl.pallas_call(
        assemble_body,
        out_shape=bf16(2 * events, sources),
        in_specs=[SMEM_SPEC, VMEM_SPEC, VMEM_SPEC],
        out_specs=VMEM_SPEC,
        scratch_shapes=[pltpu.VMEM((events, blocks_here, BLOCK), jnp.float32)],
        compiler_params=params(8),
        name="assemble",
    )(me, mine, send_xor(mine, "rows", 1))

    share = receivers // width

    def stress(targets):
        return pl.pallas_call(
            functools.partial(stress_body, targets),
            out_shape=f32(len(targets), events, share),
            in_specs=[SMEM_SPEC] + [VMEM_SPEC] * 3,
            out_specs=VMEM_SPEC,
            compiler_params=params(8),
            cost_estimate=pl.CostEstimate(
                flops=6 * len(targets) * share * sources * events,
                bytes_accessed=4 * len(targets) * share * sources,
                transcendentals=0,
            ),
            name="stress",
        )(me, slips, hi, lo)

    order = halving_order(width)
    sent = stress(order[width // 2 :])
    came = send_xor(sent, "cols", 1)
    total = stress(order[: width // 2]) + came
    step = 2
    while step < width:
        keep = total.shape[0] // 2
        total = total[:keep] + send_xor(total[keep:], "cols", step)
        step *= 2
    stress_change = total[0]
    scale = direct_effect[None, :]
    growth = jnp.expm1(load_rate * time_before / direct_effect)[None, :]
    log_time = jnp.log(scale / load_rate[None, :]) + jnp.log(
        jnp.log1p(jnp.exp(-stress_change / scale) * growth)
    )
    return (stress_change.T, log_time.T)


def solution(mesh):
    in_specs = (
        P("rows", "cols"),
        P("cols", "rows", None),
        P("cols", "rows"),
        P("cols"),
        P(("rows", "cols")),
        P(("rows", "cols")),
        P(("rows", "cols")),
    )
    out_specs = (P(("rows", "cols"), None), P(("rows", "cols"), None))
    return jax.shard_map(
        per_device, mesh=mesh, in_specs=in_specs, out_specs=out_specs, check_vma=False
    )
```

```python
import functools

import jax
import jax.numpy as jnp
from jax import lax
from jax.experimental import pallas as pl
from jax.experimental.pallas import tpu as pltpu
from jax.sharding import PartitionSpec as P

BLOCK = 128
SUB = 8
VMEM_SPEC = pl.BlockSpec(memory_space=pltpu.VMEM)
SMEM_SPEC = pl.BlockSpec(memory_space=pltpu.SMEM)
HBM_SPEC = pl.BlockSpec(memory_space=pltpu.HBM)
MIB = 1024 * 1024
NT = (((1,), (1,)), ((), ()))


def f32(*shape):
    return jax.ShapeDtypeStruct(shape, jnp.float32)


def bf16(*shape):
    return jax.ShapeDtypeStruct(shape, jnp.bfloat16)


def params(mib):
    return pltpu.CompilerParams(vmem_limit_bytes=mib * MIB)


def send_xor(block, axis, k):
    return lax.ppermute(block, axis, [(r, r ^ k) for r in range(lax.axis_size(axis))])


def fetch(targets, col, kernel_hbm, out_ref, sems):
    share = out_ref.shape[1]
    copies = [
        pltpu.make_async_copy(
            kernel_hbm.at[pl.ds(pl.multiple_of((col ^ k) * share, share), share), :], out_ref.at[j], sems.at[j]
        )
        for j, k in enumerate(targets)
    ]
    for copy in copies:
        copy.start()
    return copies


def wait(copies):
    for copy in copies:
        copy.wait()


def pack_body(
    targets, me_ref, slip_hbm, list_hbm, count_hbm, kernel_hbm, out_ref, held_ref,
    slip_ref, list_ref, count_ref, ids, sems, held_sems,
):
    copies = [
        pltpu.make_async_copy(src, dst, sems.at[j])
        for j, (src, dst) in enumerate(((list_hbm, list_ref), (count_hbm, count_ref), (slip_hbm, slip_ref)))
    ]
    for copy in copies:
        copy.start()
    held = fetch(targets, me_ref[1], kernel_hbm, held_ref, held_sems)
    events, entries = list_ref.shape
    half = events // 2
    row = me_ref[0]
    entry = lax.broadcasted_iota(jnp.int32, (events, entries), 1) + row * entries
    event = lax.broadcasted_iota(jnp.int32, (events, entries), 0)
    ids[...] = jnp.full(ids.shape, -1.0, jnp.float32)
    wait(copies)
    count = jnp.zeros((events, entries), jnp.int32)
    for e in range(events):
        count = jnp.where(event == e, count_ref[e], count)
    ids[0:events, 0:entries] = jnp.where(entry < count, list_ref[...], -1).astype(jnp.float32)
    ids[...] = pltpu.roll(ids[...], row * entries, 1)
    for h in range(2):
        first = ((row % 2) ^ h) * half
        for i in range(half):
            out_ref[h, i, 0:entries, :] = slip_ref[first + i]
            out_ref[h, half, i : i + 1, :] = ids[pl.ds(first + i, 1), :]
    wait(held)


def densify_body(targets, entries, me_ref, own_ref, came_ref, kernel_hbm, out_ref, held_ref, slips, held_sems):
    held = fetch(targets, me_ref[1], kernel_hbm, held_ref, held_sems)
    halves, half = own_ref.shape[0], own_ref.shape[1] - 1
    width, _, blocks_here, _ = out_ref.shape
    blocks = width * blocks_here
    live = 2 * halves * entries
    row = me_ref[0]
    for i in range(half):
        ids = jnp.full((1, BLOCK), -1.0, jnp.float32)
        for ref in (own_ref, came_ref):
            for j in range(halves):
                ids = jnp.maximum(ids, ref[j, half, i : i + 1, :])
        ids = jnp.broadcast_to(ids, (blocks, BLOCK))[:, :live]
        number = lax.broadcasted_iota(jnp.int32, ids.shape, 0).astype(jnp.float32)
        onehot = (ids == number).astype(jnp.bfloat16)
        for core, ref in enumerate((own_ref, came_ref)):
            for j in range(halves):
                source = row ^ (2 * j + core)
                slips[i, pl.ds(pl.multiple_of(source * entries, entries), entries), :] = ref[j, i, 0:entries, :]
        slip = slips[i]
        total = jnp.zeros((blocks, BLOCK), jnp.float32)
        for _ in range(3):
            piece = slip.astype(jnp.bfloat16)
            slip = slip - piece.astype(jnp.float32)
            total = total + jnp.dot(onehot, piece, preferred_element_type=jnp.float32)
        out_ref[:, i] = total.reshape(width, blocks_here, BLOCK)
    wait(held)


def assemble(row, own_ref, came_ref, out_ref, dense):
    width, half, blocks_here, _ = own_ref.shape
    events = dense.shape[0]
    core = row % 2
    for c in range(width):
        for other, ref in enumerate((own_ref, came_ref)):
            for i in range(half):
                dense[(2 * c + (core ^ other)) * half + i] = ref[c, i]
    flat = dense.reshape(events * blocks_here, BLOCK)
    for t in range(events // (2 * SUB)):
        for b in range(blocks_here):
            rows = [
                flat[pl.ds((2 * t + u) * SUB * blocks_here + b, SUB, stride=blocks_here), :] for u in range(2)
            ]
            slip = jnp.concatenate(rows, axis=0)
            hi = slip.astype(jnp.bfloat16)
            lo = (slip - hi.astype(jnp.float32)).astype(jnp.bfloat16)
            where = slice(b * BLOCK, (b + 1) * BLOCK)
            out_ref[2 * t * SUB : 2 * (t + 1) * SUB, where] = hi
            out_ref[events + 2 * t * SUB : events + 2 * (t + 1) * SUB, where] = lo


def stress(slip_ref, kernel_ref, out_ref):
    events = slip_ref.shape[0] // 2
    for j in range(out_ref.shape[0]):
        block = kernel_ref[j]
        hi = block.astype(jnp.bfloat16)
        lo = (block - hi.astype(jnp.float32)).astype(jnp.bfloat16)
        first = lax.dot_general(slip_ref[...], hi, NT, preferred_element_type=jnp.float32)
        second = lax.dot_general(slip_ref[:events, :], lo, NT, preferred_element_type=jnp.float32)
        out_ref[j] = first[:events] + first[events:] + second


def first_body(
    targets, me_ref, own_ref, came_ref, kernel_ref, kernel_hbm, slip_ref, out_ref, *refs
):
    held_refs, dense, held_sems = refs[:-2], refs[-2], refs[-1]
    held = [
        fetch(t, me_ref[1], kernel_hbm, ref, held_sems.at[j]) for j, (t, ref) in enumerate(zip(targets, held_refs))
    ]
    assemble(me_ref[0], own_ref, came_ref, slip_ref, dense)
    stress(slip_ref, kernel_ref, out_ref)
    for copies in held:
        wait(copies)


def halving_order(width):
    bits = width.bit_length() - 1
    return [int(f"{k:0{bits}b}"[::-1], 2) for k in range(width)]


def per_device(kernel, slip_delta, block_list, live_count, direct_effect, load_rate, time_before):
    width = lax.axis_size("cols")
    height = lax.axis_size("rows")
    events_here, entries = block_list.shape
    half = events_here // 2
    events = events_here * width
    receivers, sources = kernel.shape
    blocks_here = sources // BLOCK
    me = jnp.stack([lax.axis_index("rows"), lax.axis_index("cols")]).astype(jnp.int32)

    order = halving_order(width)
    share = receivers // width
    quarter = width // 4
    near_keep, far_keep = order[0 : 2 * quarter : 2], order[1 : 2 * quarter : 2]
    near_send, far_send = order[2 * quarter :: 2], order[2 * quarter + 1 :: 2]
    held_shape = pltpu.VMEM((quarter, share, sources), jnp.float32)
    held_sems = pltpu.SemaphoreType.DMA((quarter,))
    in_hbm, in_vmem = (
        functools.partial(pltpu.with_memory_space_constraint, memory_space=m) for m in (pltpu.HBM, pltpu.VMEM)
    )
    packed, far_send_kernel = pl.pallas_call(
        functools.partial(pack_body, far_send),
        out_shape=[f32(2, half + 1, SUB, BLOCK), held_shape],
        in_specs=[SMEM_SPEC] + [HBM_SPEC] * 4,
        out_specs=[VMEM_SPEC] * 2,
        scratch_shapes=[
            pltpu.VMEM(slip_delta.shape, jnp.float32),
            pltpu.VMEM(block_list.shape, jnp.int32),
            pltpu.SMEM(live_count.shape, jnp.int32),
            pltpu.VMEM((SUB, BLOCK), jnp.float32),
            pltpu.SemaphoreType.DMA((3,)),
            held_sems,
        ],
        compiler_params=params(4),
        name="pack",
    )(me, in_hbm(slip_delta), in_hbm(block_list), in_hbm(live_count), in_hbm(kernel))
    held = packed[None]
    step = 2
    while step < height:
        held = jnp.concatenate([held, send_xor(held, "rows", step)], axis=0)
        step *= 2
    came = send_xor(held[:, 1], "rows", 1)

    dense, near_send_kernel = pl.pallas_call(
        functools.partial(densify_body, near_send, entries),
        out_shape=[f32(width, half, blocks_here, BLOCK), held_shape],
        in_specs=[SMEM_SPEC, VMEM_SPEC, VMEM_SPEC, HBM_SPEC],
        out_specs=[VMEM_SPEC] * 2,
        scratch_shapes=[pltpu.VMEM((half, height * entries, BLOCK), jnp.float32), held_sems],
        compiler_params=params(8),
        name="densify",
    )(me, held[:, 0], came, in_hbm(kernel))
    mine = lax.all_to_all(dense, "cols", 0, 0, tiled=True)

    cost = pl.CostEstimate(
        flops=6 * quarter * share * sources * events,
        bytes_accessed=4 * quarter * share * sources,
        transcendentals=0,
    )
    slips, far_sent, far_keep_kernel, near_keep_kernel = pl.pallas_call(
        functools.partial(first_body, (far_keep, near_keep)),
        out_shape=[bf16(2 * events, sources), f32(quarter, events, share), held_shape, held_shape],
        in_specs=[SMEM_SPEC, VMEM_SPEC, VMEM_SPEC, VMEM_SPEC, HBM_SPEC],
        out_specs=[VMEM_SPEC] * 4,
        scratch_shapes=[
            pltpu.VMEM((events, blocks_here, BLOCK), jnp.float32),
            pltpu.SemaphoreType.DMA((2, quarter)),
        ],
        compiler_params=params(8),
        cost_estimate=cost,
        name="first_stress",
    )(me, mine, send_xor(mine, "rows", 1), in_vmem(far_send_kernel), in_hbm(kernel))

    def later(held):
        return pl.pallas_call(
            stress,
            out_shape=f32(quarter, events, share),
            in_specs=[VMEM_SPEC, VMEM_SPEC],
            out_specs=VMEM_SPEC,
            compiler_params=params(8),
            cost_estimate=cost,
            name="stress",
        )(slips, in_vmem(held))

    far_came = send_xor(far_sent, "cols", 1)
    near_came = send_xor(later(near_send_kernel), "cols", 1)
    far = later(far_keep_kernel) + far_came
    near = later(near_keep_kernel) + near_came
    step = 2
    while step < width // 2:
        keep = far.shape[0] // 2
        far = far[:keep] + send_xor(far[keep:], "cols", step)
        near = near[:keep] + send_xor(near[keep:], "cols", step)
        step *= 2
    total = near + send_xor(far, "cols", step)
    stress_change = total[0]
    scale = direct_effect[None, :]
    growth = jnp.expm1(load_rate * time_before / direct_effect)[None, :]
    log_time = jnp.log(scale / load_rate[None, :]) + jnp.log(
        jnp.log1p(jnp.exp(-stress_change / scale) * growth)
    )
    return (stress_change.T, log_time.T)


def solution(mesh):
    in_specs = (
        P("rows", "cols"),
        P("cols", "rows", None),
        P("cols", "rows"),
        P("cols"),
        P(("rows", "cols")),
        P(("rows", "cols")),
        P(("rows", "cols")),
    )
    out_specs = (P(("rows", "cols"), None), P(("rows", "cols"), None))
    return jax.shard_map(
        per_device, mesh=mesh, in_specs=in_specs, out_specs=out_specs, check_vma=False
    )
```

```python
import functools

import jax
import jax.numpy as jnp
from jax import lax
from jax.experimental import pallas as pl
from jax.experimental.pallas import tpu as pltpu
from jax.sharding import PartitionSpec as P

BLOCK = 128
SUB = 8
PIECES = 4
VMEM_SPEC = pl.BlockSpec(memory_space=pltpu.VMEM)
SMEM_SPEC = pl.BlockSpec(memory_space=pltpu.SMEM)
HBM_SPEC = pl.BlockSpec(memory_space=pltpu.HBM)
MIB = 1024 * 1024
NT = (((1,), (1,)), ((), ()))


def f32(*shape):
    return jax.ShapeDtypeStruct(shape, jnp.float32)


def bf16(*shape):
    return jax.ShapeDtypeStruct(shape, jnp.bfloat16)


def params(mib):
    return pltpu.CompilerParams(vmem_limit_bytes=mib * MIB)


def send_xor(block, axis, k):
    return lax.ppermute(block, axis, [(r, r ^ k) for r in range(lax.axis_size(axis))])


def fetch(targets, col, kernel_hbm, out_ref, sems):
    share = out_ref.shape[1]
    rows = share // PIECES
    copies = []
    for j, k in enumerate(targets):
        for p in range(PIECES):
            start = pl.multiple_of((col ^ k) * share + p * rows, rows)
            copies.append(
                pltpu.make_async_copy(
                    kernel_hbm.at[pl.ds(start, rows), :],
                    out_ref.at[j, pl.ds(p * rows, rows), :],
                    sems.at[j, p],
                )
            )
    for copy in copies:
        copy.start()
    return copies


def wait(copies):
    for copy in copies:
        copy.wait()


def pack_body(
    targets, me_ref, slip_hbm, list_hbm, count_hbm, kernel_hbm, out_ref, held_ref,
    slip_ref, list_ref, count_ref, ids, sems, held_sems,
):
    copies = [
        pltpu.make_async_copy(src, dst, sems.at[j])
        for j, (src, dst) in enumerate(((list_hbm, list_ref), (count_hbm, count_ref), (slip_hbm, slip_ref)))
    ]
    for copy in copies:
        copy.start()
    held = fetch(targets, me_ref[1], kernel_hbm, held_ref, held_sems)
    events, entries = list_ref.shape
    half = events // 2
    row = me_ref[0]
    entry = lax.broadcasted_iota(jnp.int32, (events, entries), 1) + row * entries
    event = lax.broadcasted_iota(jnp.int32, (events, entries), 0)
    ids[...] = jnp.full(ids.shape, -1.0, jnp.float32)
    wait(copies)
    count = jnp.zeros((events, entries), jnp.int32)
    for e in range(events):
        count = jnp.where(event == e, count_ref[e], count)
    ids[0:events, 0:entries] = jnp.where(entry < count, list_ref[...], -1).astype(jnp.float32)
    ids[...] = pltpu.roll(ids[...], row * entries, 1)
    for h in range(2):
        first = ((row % 2) ^ h) * half
        for i in range(half):
            out_ref[h, i, 0:entries, :] = slip_ref[first + i]
            out_ref[h, half, i : i + 1, :] = ids[pl.ds(first + i, 1), :]
    wait(held)


def densify_body(targets, entries, me_ref, own_ref, came_ref, kernel_hbm, out_ref, held_ref, slips, held_sems):
    held = fetch(targets, me_ref[1], kernel_hbm, held_ref, held_sems)
    halves, half = own_ref.shape[0], own_ref.shape[1] - 1
    width, _, blocks_here, _ = out_ref.shape
    blocks = width * blocks_here
    live = 2 * halves * entries
    row = me_ref[0]
    for i in range(half):
        ids = jnp.full((1, BLOCK), -1.0, jnp.float32)
        for ref in (own_ref, came_ref):
            for j in range(halves):
                ids = jnp.maximum(ids, ref[j, half, i : i + 1, :])
        ids = jnp.broadcast_to(ids, (blocks, BLOCK))[:, :live]
        number = lax.broadcasted_iota(jnp.int32, ids.shape, 0).astype(jnp.float32)
        onehot = (ids == number).astype(jnp.bfloat16)
        for core, ref in enumerate((own_ref, came_ref)):
            for j in range(halves):
                source = row ^ (2 * j + core)
                slips[i, pl.ds(pl.multiple_of(source * entries, entries), entries), :] = ref[j, i, 0:entries, :]
        slip = slips[i]
        total = jnp.zeros((blocks, BLOCK), jnp.float32)
        for _ in range(3):
            piece = slip.astype(jnp.bfloat16)
            slip = slip - piece.astype(jnp.float32)
            total = total + jnp.dot(onehot, piece, preferred_element_type=jnp.float32)
        out_ref[:, i] = total.reshape(width, blocks_here, BLOCK)
    wait(held)


def assemble(row, own_ref, came_ref, out_ref, dense):
    width, half, blocks_here, _ = own_ref.shape
    events = dense.shape[0]
    core = row % 2
    for c in range(width):
        for other, ref in enumerate((own_ref, came_ref)):
            for i in range(half):
                dense[(2 * c + (core ^ other)) * half + i] = ref[c, i]
    flat = dense.reshape(events * blocks_here, BLOCK)
    for t in range(events // (2 * SUB)):
        for b in range(blocks_here):
            rows = [
                flat[pl.ds((2 * t + u) * SUB * blocks_here + b, SUB, stride=blocks_here), :] for u in range(2)
            ]
            slip = jnp.concatenate(rows, axis=0)
            hi = slip.astype(jnp.bfloat16)
            lo = (slip - hi.astype(jnp.float32)).astype(jnp.bfloat16)
            where = slice(b * BLOCK, (b + 1) * BLOCK)
            out_ref[2 * t * SUB : 2 * (t + 1) * SUB, where] = hi
            out_ref[events + 2 * t * SUB : events + 2 * (t + 1) * SUB, where] = lo


def stress(slip_ref, kernel_ref, out_ref):
    events = slip_ref.shape[0] // 2
    for j in range(out_ref.shape[0]):
        block = kernel_ref[j]
        hi = block.astype(jnp.bfloat16)
        lo = (block - hi.astype(jnp.float32)).astype(jnp.bfloat16)
        first = lax.dot_general(slip_ref[...], hi, NT, preferred_element_type=jnp.float32)
        second = lax.dot_general(slip_ref[:events, :], lo, NT, preferred_element_type=jnp.float32)
        out_ref[j] = first[:events] + first[events:] + second


def first_body(
    targets, me_ref, own_ref, came_ref, kernel_ref, kernel_hbm, slip_ref, out_ref, *refs
):
    held_refs, dense, held_sems = refs[:-2], refs[-2], refs[-1]
    held = [
        fetch(t, me_ref[1], kernel_hbm, ref, held_sems.at[j]) for j, (t, ref) in enumerate(zip(targets, held_refs))
    ]
    assemble(me_ref[0], own_ref, came_ref, slip_ref, dense)
    stress(slip_ref, kernel_ref, out_ref)
    for copies in held:
        wait(copies)


def halving_order(width):
    bits = width.bit_length() - 1
    return [int(f"{k:0{bits}b}"[::-1], 2) for k in range(width)]


def per_device(kernel, slip_delta, block_list, live_count, direct_effect, load_rate, time_before):
    width = lax.axis_size("cols")
    height = lax.axis_size("rows")
    events_here, entries = block_list.shape
    half = events_here // 2
    events = events_here * width
    receivers, sources = kernel.shape
    blocks_here = sources // BLOCK
    me = jnp.stack([lax.axis_index("rows"), lax.axis_index("cols")]).astype(jnp.int32)

    order = halving_order(width)
    share = receivers // width
    quarter = width // 4
    near_keep, far_keep = order[0 : 2 * quarter : 2], order[1 : 2 * quarter : 2]
    near_send, far_send = order[2 * quarter :: 2], order[2 * quarter + 1 :: 2]
    held_shape = pltpu.VMEM((quarter, share, sources), jnp.float32)
    held_sems = pltpu.SemaphoreType.DMA((quarter, PIECES))
    in_hbm, in_vmem = (
        functools.partial(pltpu.with_memory_space_constraint, memory_space=m) for m in (pltpu.HBM, pltpu.VMEM)
    )
    packed, far_send_kernel = pl.pallas_call(
        functools.partial(pack_body, far_send),
        out_shape=[f32(2, half + 1, SUB, BLOCK), held_shape],
        in_specs=[SMEM_SPEC] + [HBM_SPEC] * 4,
        out_specs=[VMEM_SPEC] * 2,
        scratch_shapes=[
            pltpu.VMEM(slip_delta.shape, jnp.float32),
            pltpu.VMEM(block_list.shape, jnp.int32),
            pltpu.SMEM(live_count.shape, jnp.int32),
            pltpu.VMEM((SUB, BLOCK), jnp.float32),
            pltpu.SemaphoreType.DMA((3,)),
            held_sems,
        ],
        compiler_params=params(4),
        name="pack",
    )(me, in_hbm(slip_delta), in_hbm(block_list), in_hbm(live_count), in_hbm(kernel))
    held = packed[None]
    step = 2
    while step < height:
        held = jnp.concatenate([held, send_xor(held, "rows", step)], axis=0)
        step *= 2
    came = send_xor(held[:, 1], "rows", 1)

    dense, near_send_kernel = pl.pallas_call(
        functools.partial(densify_body, near_send, entries),
        out_shape=[f32(width, half, blocks_here, BLOCK), held_shape],
        in_specs=[SMEM_SPEC, VMEM_SPEC, VMEM_SPEC, HBM_SPEC],
        out_specs=[VMEM_SPEC] * 2,
        scratch_shapes=[pltpu.VMEM((half, height * entries, BLOCK), jnp.float32), held_sems],
        compiler_params=params(8),
        name="densify",
    )(me, held[:, 0], came, in_hbm(kernel))
    mine = lax.all_to_all(dense, "cols", 0, 0, tiled=True)

    cost = pl.CostEstimate(
        flops=6 * quarter * share * sources * events,
        bytes_accessed=4 * quarter * share * sources,
        transcendentals=0,
    )
    slips, far_sent, far_keep_kernel, near_keep_kernel = pl.pallas_call(
        functools.partial(first_body, (far_keep, near_keep)),
        out_shape=[bf16(2 * events, sources), f32(quarter, events, share), held_shape, held_shape],
        in_specs=[SMEM_SPEC, VMEM_SPEC, VMEM_SPEC, VMEM_SPEC, HBM_SPEC],
        out_specs=[VMEM_SPEC] * 4,
        scratch_shapes=[
            pltpu.VMEM((events, blocks_here, BLOCK), jnp.float32),
            pltpu.SemaphoreType.DMA((2, quarter, PIECES)),
        ],
        compiler_params=params(8),
        cost_estimate=cost,
        name="first_stress",
    )(me, mine, send_xor(mine, "rows", 1), in_vmem(far_send_kernel), in_hbm(kernel))

    def later(held):
        return pl.pallas_call(
            stress,
            out_shape=f32(quarter, events, share),
            in_specs=[VMEM_SPEC, VMEM_SPEC],
            out_specs=VMEM_SPEC,
            compiler_params=params(8),
            cost_estimate=cost,
            name="stress",
        )(slips, in_vmem(held))

    far_came = send_xor(far_sent, "cols", 1)
    near_came = send_xor(later(near_send_kernel), "cols", 1)
    far = later(far_keep_kernel) + far_came
    near = later(near_keep_kernel) + near_came
    step = 2
    while step < width // 2:
        keep = far.shape[0] // 2
        far = far[:keep] + send_xor(far[keep:], "cols", step)
        near = near[:keep] + send_xor(near[keep:], "cols", step)
        step *= 2
    stress_change = near[0] + send_xor(far[0], "cols", step)
    scale = direct_effect[None, :]
    growth = jnp.expm1(load_rate * time_before / direct_effect)[None, :]
    log_time = jnp.log(scale / load_rate[None, :]) + jnp.log(
        jnp.log1p(jnp.exp(-stress_change / scale) * growth)
    )
    return (stress_change.T, log_time.T)


def solution(mesh):
    in_specs = (
        P("rows", "cols"),
        P("cols", "rows", None),
        P("cols", "rows"),
        P("cols"),
        P(("rows", "cols")),
        P(("rows", "cols")),
        P(("rows", "cols")),
    )
    out_specs = (P(("rows", "cols"), None), P(("rows", "cols"), None))
    return jax.shard_map(
        per_device, mesh=mesh, in_specs=in_specs, out_specs=out_specs, check_vma=False
    )
```

```python
import functools

import jax
import jax.numpy as jnp
from jax import lax
from jax.experimental import pallas as pl
from jax.experimental.pallas import tpu as pltpu
from jax.sharding import PartitionSpec as P

BLOCK = 128
SUB = 8
PIECES = 4
VMEM_SPEC = pl.BlockSpec(memory_space=pltpu.VMEM)
SMEM_SPEC = pl.BlockSpec(memory_space=pltpu.SMEM)
HBM_SPEC = pl.BlockSpec(memory_space=pltpu.HBM)
MIB = 1024 * 1024
NT = (((1,), (1,)), ((), ()))


def f32(*shape):
    return jax.ShapeDtypeStruct(shape, jnp.float32)


def bf16(*shape):
    return jax.ShapeDtypeStruct(shape, jnp.bfloat16)


def params(mib):
    return pltpu.CompilerParams(vmem_limit_bytes=mib * MIB)


def send_xor(block, axis, k):
    return lax.ppermute(block, axis, [(r, r ^ k) for r in range(lax.axis_size(axis))])


def fetch(targets, col, kernel_hbm, out_ref, sems):
    share = out_ref.shape[1]
    rows = share // PIECES
    copies = []
    for j, k in enumerate(targets):
        for p in range(PIECES):
            start = pl.multiple_of((col ^ k) * share + p * rows, rows)
            copies.append(
                pltpu.make_async_copy(
                    kernel_hbm.at[pl.ds(start, rows), :],
                    out_ref.at[j, pl.ds(p * rows, rows), :],
                    sems.at[j, p],
                )
            )
    for n, copy in enumerate(copies):
        copy.start(priority=n % 2)
    return copies


def wait(copies):
    for copy in copies:
        copy.wait()


def pack_body(
    targets, me_ref, slip_hbm, list_hbm, count_hbm, kernel_hbm, out_ref, held_ref,
    slip_ref, list_ref, count_ref, ids, sems, held_sems,
):
    copies = [
        pltpu.make_async_copy(src, dst, sems.at[j])
        for j, (src, dst) in enumerate(((list_hbm, list_ref), (count_hbm, count_ref), (slip_hbm, slip_ref)))
    ]
    for copy in copies:
        copy.start()
    held = fetch(targets, me_ref[1], kernel_hbm, held_ref, held_sems)
    events, entries = list_ref.shape
    half = events // 2
    row = me_ref[0]
    entry = lax.broadcasted_iota(jnp.int32, (events, entries), 1) + row * entries
    event = lax.broadcasted_iota(jnp.int32, (events, entries), 0)
    ids[...] = jnp.full(ids.shape, -1.0, jnp.float32)
    wait(copies)
    count = jnp.zeros((events, entries), jnp.int32)
    for e in range(events):
        count = jnp.where(event == e, count_ref[e], count)
    ids[0:events, 0:entries] = jnp.where(entry < count, list_ref[...], -1).astype(jnp.float32)
    ids[...] = pltpu.roll(ids[...], row * entries, 1)
    for h in range(2):
        first = ((row % 2) ^ h) * half
        for i in range(half):
            out_ref[h, i, 0:entries, :] = slip_ref[first + i]
            out_ref[h, half, i : i + 1, :] = ids[pl.ds(first + i, 1), :]
    wait(held)


def densify_body(targets, entries, me_ref, own_ref, came_ref, kernel_hbm, out_ref, held_ref, slips, held_sems):
    held = fetch(targets, me_ref[1], kernel_hbm, held_ref, held_sems)
    halves, half = own_ref.shape[0], own_ref.shape[1] - 1
    width, _, blocks_here, _ = out_ref.shape
    blocks = width * blocks_here
    live = 2 * halves * entries
    row = me_ref[0]
    for i in range(half):
        ids = jnp.full((1, BLOCK), -1.0, jnp.float32)
        for ref in (own_ref, came_ref):
            for j in range(halves):
                ids = jnp.maximum(ids, ref[j, half, i : i + 1, :])
        ids = jnp.broadcast_to(ids, (blocks, BLOCK))[:, :live]
        number = lax.broadcasted_iota(jnp.int32, ids.shape, 0).astype(jnp.float32)
        onehot = (ids == number).astype(jnp.bfloat16)
        for core, ref in enumerate((own_ref, came_ref)):
            for j in range(halves):
                source = row ^ (2 * j + core)
                slips[i, pl.ds(pl.multiple_of(source * entries, entries), entries), :] = ref[j, i, 0:entries, :]
        slip = slips[i]
        total = jnp.zeros((blocks, BLOCK), jnp.float32)
        for _ in range(3):
            piece = slip.astype(jnp.bfloat16)
            slip = slip - piece.astype(jnp.float32)
            total = total + jnp.dot(onehot, piece, preferred_element_type=jnp.float32)
        out_ref[:, i] = total.reshape(width, blocks_here, BLOCK)
    wait(held)


def assemble(row, own_ref, came_ref, out_ref, dense):
    width, half, blocks_here, _ = own_ref.shape
    events = dense.shape[0]
    core = row % 2
    for c in range(width):
        for other, ref in enumerate((own_ref, came_ref)):
            for i in range(half):
                dense[(2 * c + (core ^ other)) * half + i] = ref[c, i]
    flat = dense.reshape(events * blocks_here, BLOCK)
    for t in range(events // (2 * SUB)):
        for b in range(blocks_here):
            rows = [
                flat[pl.ds((2 * t + u) * SUB * blocks_here + b, SUB, stride=blocks_here), :] for u in range(2)
            ]
            slip = jnp.concatenate(rows, axis=0)
            hi = slip.astype(jnp.bfloat16)
            lo = (slip - hi.astype(jnp.float32)).astype(jnp.bfloat16)
            where = slice(b * BLOCK, (b + 1) * BLOCK)
            out_ref[2 * t * SUB : 2 * (t + 1) * SUB, where] = hi
            out_ref[events + 2 * t * SUB : events + 2 * (t + 1) * SUB, where] = lo


def stress(slip_ref, kernel_ref, out_ref):
    events = slip_ref.shape[0] // 2
    for j in range(out_ref.shape[0]):
        block = kernel_ref[j]
        hi = block.astype(jnp.bfloat16)
        lo = (block - hi.astype(jnp.float32)).astype(jnp.bfloat16)
        first = lax.dot_general(slip_ref[...], hi, NT, preferred_element_type=jnp.float32)
        second = lax.dot_general(slip_ref[:events, :], lo, NT, preferred_element_type=jnp.float32)
        out_ref[j] = first[:events] + first[events:] + second


def first_body(
    targets, me_ref, own_ref, came_ref, kernel_ref, kernel_hbm, slip_ref, out_ref, *refs
):
    held_refs, dense, held_sems = refs[:-2], refs[-2], refs[-1]
    held = [
        fetch(t, me_ref[1], kernel_hbm, ref, held_sems.at[j]) for j, (t, ref) in enumerate(zip(targets, held_refs))
    ]
    assemble(me_ref[0], own_ref, came_ref, slip_ref, dense)
    stress(slip_ref, kernel_ref, out_ref)
    for copies in held:
        wait(copies)


def halving_order(width):
    bits = width.bit_length() - 1
    return [int(f"{k:0{bits}b}"[::-1], 2) for k in range(width)]


def per_device(kernel, slip_delta, block_list, live_count, direct_effect, load_rate, time_before):
    width = lax.axis_size("cols")
    height = lax.axis_size("rows")
    events_here, entries = block_list.shape
    half = events_here // 2
    events = events_here * width
    receivers, sources = kernel.shape
    blocks_here = sources // BLOCK
    me = jnp.stack([lax.axis_index("rows"), lax.axis_index("cols")]).astype(jnp.int32)

    order = halving_order(width)
    share = receivers // width
    quarter = width // 4
    near_keep, far_keep = order[0 : 2 * quarter : 2], order[1 : 2 * quarter : 2]
    near_send, far_send = order[2 * quarter :: 2], order[2 * quarter + 1 :: 2]
    held_shape = pltpu.VMEM((quarter, share, sources), jnp.float32)
    held_sems = pltpu.SemaphoreType.DMA((quarter, PIECES))
    in_hbm, in_vmem = (
        functools.partial(pltpu.with_memory_space_constraint, memory_space=m) for m in (pltpu.HBM, pltpu.VMEM)
    )
    packed, far_send_kernel = pl.pallas_call(
        functools.partial(pack_body, far_send),
        out_shape=[f32(2, half + 1, SUB, BLOCK), held_shape],
        in_specs=[SMEM_SPEC] + [HBM_SPEC] * 4,
        out_specs=[VMEM_SPEC] * 2,
        scratch_shapes=[
            pltpu.VMEM(slip_delta.shape, jnp.float32),
            pltpu.VMEM(block_list.shape, jnp.int32),
            pltpu.SMEM(live_count.shape, jnp.int32),
            pltpu.VMEM((SUB, BLOCK), jnp.float32),
            pltpu.SemaphoreType.DMA((3,)),
            held_sems,
        ],
        compiler_params=params(4),
        name="pack",
    )(me, in_hbm(slip_delta), in_hbm(block_list), in_hbm(live_count), in_hbm(kernel))
    held = packed[None]
    step = 2
    while step < height:
        held = jnp.concatenate([held, send_xor(held, "rows", step)], axis=0)
        step *= 2
    came = send_xor(held[:, 1], "rows", 1)

    dense, near_send_kernel = pl.pallas_call(
        functools.partial(densify_body, near_send, entries),
        out_shape=[f32(width, half, blocks_here, BLOCK), held_shape],
        in_specs=[SMEM_SPEC, VMEM_SPEC, VMEM_SPEC, HBM_SPEC],
        out_specs=[VMEM_SPEC] * 2,
        scratch_shapes=[pltpu.VMEM((half, height * entries, BLOCK), jnp.float32), held_sems],
        compiler_params=params(8),
        name="densify",
    )(me, held[:, 0], came, in_hbm(kernel))
    mine = lax.all_to_all(dense, "cols", 0, 0, tiled=True)

    cost = pl.CostEstimate(
        flops=6 * quarter * share * sources * events,
        bytes_accessed=4 * quarter * share * sources,
        transcendentals=0,
    )
    slips, far_sent, far_keep_kernel, near_keep_kernel = pl.pallas_call(
        functools.partial(first_body, (far_keep, near_keep)),
        out_shape=[bf16(2 * events, sources), f32(quarter, events, share), held_shape, held_shape],
        in_specs=[SMEM_SPEC, VMEM_SPEC, VMEM_SPEC, VMEM_SPEC, HBM_SPEC],
        out_specs=[VMEM_SPEC] * 4,
        scratch_shapes=[
            pltpu.VMEM((events, blocks_here, BLOCK), jnp.float32),
            pltpu.SemaphoreType.DMA((2, quarter, PIECES)),
        ],
        compiler_params=params(8),
        cost_estimate=cost,
        name="first_stress",
    )(me, mine, send_xor(mine, "rows", 1), in_vmem(far_send_kernel), in_hbm(kernel))

    def later(held):
        return pl.pallas_call(
            stress,
            out_shape=f32(quarter, events, share),
            in_specs=[VMEM_SPEC, VMEM_SPEC],
            out_specs=VMEM_SPEC,
            compiler_params=params(8),
            cost_estimate=cost,
            name="stress",
        )(slips, in_vmem(held))

    far_came = send_xor(far_sent, "cols", 1)
    near_came = send_xor(later(near_send_kernel), "cols", 1)
    far = later(far_keep_kernel) + far_came
    near = later(near_keep_kernel) + near_came
    step = 2
    while step < width // 2:
        keep = far.shape[0] // 2
        far = far[:keep] + send_xor(far[keep:], "cols", step)
        near = near[:keep] + send_xor(near[keep:], "cols", step)
        step *= 2
    stress_change = near[0] + send_xor(far[0], "cols", step)
    scale = direct_effect[None, :]
    growth = jnp.expm1(load_rate * time_before / direct_effect)[None, :]
    log_time = jnp.log(scale / load_rate[None, :]) + jnp.log(
        jnp.log1p(jnp.exp(-stress_change / scale) * growth)
    )
    return (stress_change.T, log_time.T)


def solution(mesh):
    in_specs = (
        P("rows", "cols"),
        P("cols", "rows", None),
        P("cols", "rows"),
        P("cols"),
        P(("rows", "cols")),
        P(("rows", "cols")),
        P(("rows", "cols")),
    )
    out_specs = (P(("rows", "cols"), None), P(("rows", "cols"), None))
    return jax.shard_map(
        per_device, mesh=mesh, in_specs=in_specs, out_specs=out_specs, check_vma=False
    )
```

```python
import functools

import jax
import jax.numpy as jnp
from jax import lax
from jax.experimental import pallas as pl
from jax.experimental.pallas import tpu as pltpu
from jax.sharding import PartitionSpec as P

BLOCK = 128
SUB = 8
PIECES = 4
VMEM_SPEC = pl.BlockSpec(memory_space=pltpu.VMEM)
SMEM_SPEC = pl.BlockSpec(memory_space=pltpu.SMEM)
HBM_SPEC = pl.BlockSpec(memory_space=pltpu.HBM)
MIB = 1024 * 1024
NT = (((1,), (1,)), ((), ()))


def f32(*shape):
    return jax.ShapeDtypeStruct(shape, jnp.float32)


def bf16(*shape):
    return jax.ShapeDtypeStruct(shape, jnp.bfloat16)


def params(mib):
    return pltpu.CompilerParams(vmem_limit_bytes=mib * MIB)


def send_xor(block, axis, k):
    return lax.ppermute(block, axis, [(r, r ^ k) for r in range(lax.axis_size(axis))])


def fetch(targets, col, kernel_hbm, out_ref, sems):
    share = out_ref.shape[1]
    rows = share // PIECES
    copies = []
    for j, k in enumerate(targets):
        for p in range(PIECES):
            start = pl.multiple_of((col ^ k) * share + p * rows, rows)
            copies.append(
                pltpu.make_async_copy(
                    kernel_hbm.at[pl.ds(start, rows), :],
                    out_ref.at[j, pl.ds(p * rows, rows), :],
                    sems.at[j, p],
                )
            )
    for n, copy in enumerate(copies):
        copy.start(priority=n % 2)
    return copies


def wait(copies):
    for copy in copies:
        copy.wait()


def pack_body(me_ref, slip_hbm, list_hbm, count_hbm, out_ref, slip_ref, list_ref, count_ref, ids, sems):
    copies = [
        pltpu.make_async_copy(src, dst, sems.at[j])
        for j, (src, dst) in enumerate(((list_hbm, list_ref), (count_hbm, count_ref), (slip_hbm, slip_ref)))
    ]
    for copy in copies:
        copy.start()
    events, entries = list_ref.shape
    half = events // 2
    row = me_ref[0]
    entry = lax.broadcasted_iota(jnp.int32, (events, entries), 1) + row * entries
    event = lax.broadcasted_iota(jnp.int32, (events, entries), 0)
    ids[...] = jnp.full(ids.shape, -1.0, jnp.float32)
    wait(copies)
    count = jnp.zeros((events, entries), jnp.int32)
    for e in range(events):
        count = jnp.where(event == e, count_ref[e], count)
    ids[0:events, 0:entries] = jnp.where(entry < count, list_ref[...], -1).astype(jnp.float32)
    ids[...] = pltpu.roll(ids[...], row * entries, 1)
    for h in range(2):
        first = ((row % 2) ^ h) * half
        for i in range(half):
            out_ref[h, i, 0:entries, :] = slip_ref[first + i]
            out_ref[h, half, i : i + 1, :] = ids[pl.ds(first + i, 1), :]


def densify_body(entries, me_ref, own_ref, came_ref, out_hbm, out_ref, slips, sem):
    halves, half = own_ref.shape[0], own_ref.shape[1] - 1
    width, _, blocks_here, _ = out_ref.shape
    blocks = width * blocks_here
    live = 2 * halves * entries
    row = me_ref[0]
    for i in range(half):
        ids = jnp.full((1, BLOCK), -1.0, jnp.float32)
        for ref in (own_ref, came_ref):
            for j in range(halves):
                ids = jnp.maximum(ids, ref[j, half, i : i + 1, :])
        ids = jnp.broadcast_to(ids, (blocks, BLOCK))[:, :live]
        number = lax.broadcasted_iota(jnp.int32, ids.shape, 0).astype(jnp.float32)
        onehot = (ids == number).astype(jnp.bfloat16)
        for core, ref in enumerate((own_ref, came_ref)):
            for j in range(halves):
                source = row ^ (2 * j + core)
                slips[i, pl.ds(pl.multiple_of(source * entries, entries), entries), :] = ref[j, i, 0:entries, :]
        slip = slips[i]
        total = jnp.zeros((blocks, BLOCK), jnp.float32)
        for _ in range(3):
            piece = slip.astype(jnp.bfloat16)
            slip = slip - piece.astype(jnp.float32)
            total = total + jnp.dot(onehot, piece, preferred_element_type=jnp.float32)
        out_ref[:, i] = total.reshape(width, blocks_here, BLOCK)
    copy = pltpu.make_async_copy(out_ref, out_hbm, sem)
    copy.start()
    copy.wait()


def fetch_body(targets, me_ref, kernel_hbm, *refs):
    held_refs, held_sems = refs[:-1], refs[-1]
    held = [
        fetch(t, me_ref[1], kernel_hbm, ref, held_sems.at[j]) for j, (t, ref) in enumerate(zip(targets, held_refs))
    ]
    for copies in held:
        wait(copies)


def assemble(row, own_ref, came_ref, out_ref, dense):
    width, half, blocks_here, _ = own_ref.shape
    events = dense.shape[0]
    core = row % 2
    for c in range(width):
        for other, ref in enumerate((own_ref, came_ref)):
            for i in range(half):
                dense[(2 * c + (core ^ other)) * half + i] = ref[c, i]
    flat = dense.reshape(events * blocks_here, BLOCK)
    for t in range(events // (2 * SUB)):
        for b in range(blocks_here):
            rows = [
                flat[pl.ds((2 * t + u) * SUB * blocks_here + b, SUB, stride=blocks_here), :] for u in range(2)
            ]
            slip = jnp.concatenate(rows, axis=0)
            hi = slip.astype(jnp.bfloat16)
            lo = (slip - hi.astype(jnp.float32)).astype(jnp.bfloat16)
            where = slice(b * BLOCK, (b + 1) * BLOCK)
            out_ref[2 * t * SUB : 2 * (t + 1) * SUB, where] = hi
            out_ref[events + 2 * t * SUB : events + 2 * (t + 1) * SUB, where] = lo


def stress(slip_ref, kernel_ref, out_ref):
    events = slip_ref.shape[0] // 2
    for j in range(out_ref.shape[0]):
        block = kernel_ref[j]
        hi = block.astype(jnp.bfloat16)
        lo = (block - hi.astype(jnp.float32)).astype(jnp.bfloat16)
        first = lax.dot_general(slip_ref[...], hi, NT, preferred_element_type=jnp.float32)
        second = lax.dot_general(slip_ref[:events, :], lo, NT, preferred_element_type=jnp.float32)
        out_ref[j] = first[:events] + first[events:] + second


def first_body(
    targets, me_ref, own_ref, came_ref, kernel_ref, kernel_hbm, slip_ref, out_ref, *refs
):
    held_refs, dense, held_sems = refs[:-2], refs[-2], refs[-1]
    held = [
        fetch(t, me_ref[1], kernel_hbm, ref, held_sems.at[j]) for j, (t, ref) in enumerate(zip(targets, held_refs))
    ]
    assemble(me_ref[0], own_ref, came_ref, slip_ref, dense)
    stress(slip_ref, kernel_ref, out_ref)
    for copies in held:
        wait(copies)


def halving_order(width):
    bits = width.bit_length() - 1
    return [int(f"{k:0{bits}b}"[::-1], 2) for k in range(width)]


def per_device(kernel, slip_delta, block_list, live_count, direct_effect, load_rate, time_before):
    width = lax.axis_size("cols")
    height = lax.axis_size("rows")
    events_here, entries = block_list.shape
    half = events_here // 2
    events = events_here * width
    receivers, sources = kernel.shape
    blocks_here = sources // BLOCK
    me = jnp.stack([lax.axis_index("rows"), lax.axis_index("cols")]).astype(jnp.int32)

    order = halving_order(width)
    share = receivers // width
    quarter = width // 4
    near_keep, far_keep = order[0 : 2 * quarter : 2], order[1 : 2 * quarter : 2]
    near_send, far_send = order[2 * quarter :: 2], order[2 * quarter + 1 :: 2]
    held_shape = pltpu.VMEM((quarter, share, sources), jnp.float32)
    in_hbm, in_vmem = (
        functools.partial(pltpu.with_memory_space_constraint, memory_space=m) for m in (pltpu.HBM, pltpu.VMEM)
    )
    packed = pl.pallas_call(
        pack_body,
        out_shape=f32(2, half + 1, SUB, BLOCK),
        in_specs=[SMEM_SPEC] + [HBM_SPEC] * 3,
        out_specs=VMEM_SPEC,
        scratch_shapes=[
            pltpu.VMEM(slip_delta.shape, jnp.float32),
            pltpu.VMEM(block_list.shape, jnp.int32),
            pltpu.SMEM(live_count.shape, jnp.int32),
            pltpu.VMEM((SUB, BLOCK), jnp.float32),
            pltpu.SemaphoreType.DMA((3,)),
        ],
        compiler_params=params(4),
        name="pack",
    )(me, in_hbm(slip_delta), in_hbm(block_list), in_hbm(live_count))
    held = packed[None]
    step = 2
    while step < height:
        held = jnp.concatenate([held, send_xor(held, "rows", step)], axis=0)
        step *= 2
    came = send_xor(held[:, 1], "rows", 1)

    dense = pl.pallas_call(
        functools.partial(densify_body, entries),
        out_shape=pltpu.HBM((width, half, blocks_here, BLOCK), jnp.float32),
        in_specs=[SMEM_SPEC, VMEM_SPEC, VMEM_SPEC],
        out_specs=HBM_SPEC,
        scratch_shapes=[
            pltpu.VMEM((width, half, blocks_here, BLOCK), jnp.float32),
            pltpu.VMEM((half, height * entries, BLOCK), jnp.float32),
            pltpu.SemaphoreType.DMA,
        ],
        compiler_params=params(8),
        name="densify",
    )(me, held[:, 0], came)
    dense, after = lax.optimization_barrier((dense, me))
    mine = lax.all_to_all(dense, "cols", 0, 0, tiled=True)
    far_send_kernel, near_send_kernel, far_keep_kernel = pl.pallas_call(
        functools.partial(fetch_body, (far_send, near_send, far_keep)),
        out_shape=[held_shape] * 3,
        in_specs=[SMEM_SPEC, HBM_SPEC],
        out_specs=[VMEM_SPEC] * 3,
        scratch_shapes=[pltpu.SemaphoreType.DMA((3, quarter, PIECES))],
        compiler_params=params(4),
        cost_estimate=pl.CostEstimate(
            flops=0, bytes_accessed=6 * receivers * sources, transcendentals=0
        ),
        name="fetch",
    )(after, in_hbm(kernel))
    mine, far_send_kernel, near_send_kernel, far_keep_kernel = lax.optimization_barrier(
        (mine, far_send_kernel, near_send_kernel, far_keep_kernel)
    )

    cost = pl.CostEstimate(
        flops=6 * quarter * share * sources * events,
        bytes_accessed=4 * quarter * share * sources,
        transcendentals=0,
    )
    slips, far_sent, near_keep_kernel = pl.pallas_call(
        functools.partial(first_body, (near_keep,)),
        out_shape=[bf16(2 * events, sources), f32(quarter, events, share), held_shape],
        in_specs=[SMEM_SPEC, VMEM_SPEC, VMEM_SPEC, VMEM_SPEC, HBM_SPEC],
        out_specs=[VMEM_SPEC] * 3,
        scratch_shapes=[
            pltpu.VMEM((events, blocks_here, BLOCK), jnp.float32),
            pltpu.SemaphoreType.DMA((1, quarter, PIECES)),
        ],
        compiler_params=params(8),
        cost_estimate=cost,
        name="first_stress",
    )(me, mine, send_xor(mine, "rows", 1), in_vmem(far_send_kernel), in_hbm(kernel))

    def later(held):
        return pl.pallas_call(
            stress,
            out_shape=f32(quarter, events, share),
            in_specs=[VMEM_SPEC, VMEM_SPEC],
            out_specs=VMEM_SPEC,
            compiler_params=params(8),
            cost_estimate=cost,
            name="stress",
        )(slips, in_vmem(held))

    far_came = send_xor(far_sent, "cols", 1)
    near_came = send_xor(later(near_send_kernel), "cols", 1)
    far = later(far_keep_kernel) + far_came
    near = later(near_keep_kernel) + near_came
    step = 2
    while step < width // 2:
        keep = far.shape[0] // 2
        far = far[:keep] + send_xor(far[keep:], "cols", step)
        near = near[:keep] + send_xor(near[keep:], "cols", step)
        step *= 2
    stress_change = near[0] + send_xor(far[0], "cols", step)
    scale = direct_effect[None, :]
    growth = jnp.expm1(load_rate * time_before / direct_effect)[None, :]
    log_time = jnp.log(scale / load_rate[None, :]) + jnp.log(
        jnp.log1p(jnp.exp(-stress_change / scale) * growth)
    )
    return (stress_change.T, log_time.T)


def solution(mesh):
    in_specs = (
        P("rows", "cols"),
        P("cols", "rows", None),
        P("cols", "rows"),
        P("cols"),
        P(("rows", "cols")),
        P(("rows", "cols")),
        P(("rows", "cols")),
    )
    out_specs = (P(("rows", "cols"), None), P(("rows", "cols"), None))
    return jax.shard_map(
        per_device, mesh=mesh, in_specs=in_specs, out_specs=out_specs, check_vma=False
    )
```

```python
import functools

import jax
import jax.numpy as jnp
from jax import lax
from jax.experimental import pallas as pl
from jax.experimental.pallas import tpu as pltpu
from jax.sharding import PartitionSpec as P

BLOCK = 128
SUB = 8
PIECES = 4
VMEM_SPEC = pl.BlockSpec(memory_space=pltpu.VMEM)
SMEM_SPEC = pl.BlockSpec(memory_space=pltpu.SMEM)
HBM_SPEC = pl.BlockSpec(memory_space=pltpu.HBM)
MIB = 1024 * 1024
NT = (((1,), (1,)), ((), ()))


def f32(*shape):
    return jax.ShapeDtypeStruct(shape, jnp.float32)


def bf16(*shape):
    return jax.ShapeDtypeStruct(shape, jnp.bfloat16)


def params(mib):
    return pltpu.CompilerParams(vmem_limit_bytes=mib * MIB)


def send_xor(block, axis, k):
    return lax.ppermute(block, axis, [(r, r ^ k) for r in range(lax.axis_size(axis))])


def fetch(targets, col, kernel_hbm, out_ref, sems):
    share = out_ref.shape[1]
    rows = share // PIECES
    copies = []
    for j, k in enumerate(targets):
        for p in range(PIECES):
            start = pl.multiple_of((col ^ k) * share + p * rows, rows)
            copies.append(
                pltpu.make_async_copy(
                    kernel_hbm.at[pl.ds(start, rows), :],
                    out_ref.at[j, pl.ds(p * rows, rows), :],
                    sems.at[j, p],
                )
            )
    for n, copy in enumerate(copies):
        copy.start(priority=n % 2)
    return copies


def wait(copies):
    for copy in copies:
        copy.wait()


def pack_body(me_ref, slip_hbm, list_hbm, count_hbm, out_ref, slip_ref, list_ref, count_ref, ids, sems):
    copies = [
        pltpu.make_async_copy(src, dst, sems.at[j])
        for j, (src, dst) in enumerate(((list_hbm, list_ref), (count_hbm, count_ref), (slip_hbm, slip_ref)))
    ]
    for copy in copies:
        copy.start()
    events, entries = list_ref.shape
    half = events // 2
    row = me_ref[0]
    entry = lax.broadcasted_iota(jnp.int32, (events, entries), 1) + row * entries
    event = lax.broadcasted_iota(jnp.int32, (events, entries), 0)
    ids[...] = jnp.full(ids.shape, -1.0, jnp.float32)
    wait(copies)
    count = jnp.zeros((events, entries), jnp.int32)
    for e in range(events):
        count = jnp.where(event == e, count_ref[e], count)
    ids[0:events, 0:entries] = jnp.where(entry < count, list_ref[...], -1).astype(jnp.float32)
    ids[...] = pltpu.roll(ids[...], row * entries, 1)
    for h in range(2):
        first = ((row % 2) ^ h) * half
        for i in range(half):
            out_ref[h, i, 0:entries, :] = slip_ref[first + i]
            out_ref[h, half, i : i + 1, :] = ids[pl.ds(first + i, 1), :]


def densify_body(entries, me_ref, own_ref, came_ref, out_ref, slips):
    halves, half = own_ref.shape[0], own_ref.shape[1] - 1
    width, _, blocks_here, _ = out_ref.shape
    blocks = width * blocks_here
    live = 2 * halves * entries
    row = me_ref[0]
    for i in range(half):
        ids = jnp.full((1, BLOCK), -1.0, jnp.float32)
        for ref in (own_ref, came_ref):
            for j in range(halves):
                ids = jnp.maximum(ids, ref[j, half, i : i + 1, :])
        ids = jnp.broadcast_to(ids, (blocks, BLOCK))[:, :live]
        number = lax.broadcasted_iota(jnp.int32, ids.shape, 0).astype(jnp.float32)
        onehot = (ids == number).astype(jnp.bfloat16)
        for core, ref in enumerate((own_ref, came_ref)):
            for j in range(halves):
                source = row ^ (2 * j + core)
                slips[i, pl.ds(pl.multiple_of(source * entries, entries), entries), :] = ref[j, i, 0:entries, :]
        slip = slips[i]
        total = jnp.zeros((blocks, BLOCK), jnp.float32)
        for _ in range(3):
            piece = slip.astype(jnp.bfloat16)
            slip = slip - piece.astype(jnp.float32)
            total = total + jnp.dot(onehot, piece, preferred_element_type=jnp.float32)
        out_ref[:, i] = total.reshape(width, blocks_here, BLOCK)


def fetch_body(targets, me_ref, kernel_hbm, mark_ref, *refs):
    held_refs, held_sems = refs[:-1], refs[-1]
    mark_ref[...] = jnp.zeros(mark_ref.shape, jnp.float32)
    held = [
        fetch(t, me_ref[1], kernel_hbm, ref, held_sems.at[j]) for j, (t, ref) in enumerate(zip(targets, held_refs))
    ]
    for copies in held:
        wait(copies)


def assemble(row, own_ref, came_ref, out_ref, dense):
    width, half, blocks_here, _ = own_ref.shape
    events = dense.shape[0]
    core = row % 2
    for c in range(width):
        for other, ref in enumerate((own_ref, came_ref)):
            for i in range(half):
                dense[(2 * c + (core ^ other)) * half + i] = ref[c, i]
    flat = dense.reshape(events * blocks_here, BLOCK)
    for t in range(events // (2 * SUB)):
        for b in range(blocks_here):
            rows = [
                flat[pl.ds((2 * t + u) * SUB * blocks_here + b, SUB, stride=blocks_here), :] for u in range(2)
            ]
            slip = jnp.concatenate(rows, axis=0)
            hi = slip.astype(jnp.bfloat16)
            lo = (slip - hi.astype(jnp.float32)).astype(jnp.bfloat16)
            where = slice(b * BLOCK, (b + 1) * BLOCK)
            out_ref[2 * t * SUB : 2 * (t + 1) * SUB, where] = hi
            out_ref[events + 2 * t * SUB : events + 2 * (t + 1) * SUB, where] = lo


def stress(slip_ref, kernel_ref, out_ref):
    events = slip_ref.shape[0] // 2
    for j in range(out_ref.shape[0]):
        block = kernel_ref[j]
        hi = block.astype(jnp.bfloat16)
        lo = (block - hi.astype(jnp.float32)).astype(jnp.bfloat16)
        first = lax.dot_general(slip_ref[...], hi, NT, preferred_element_type=jnp.float32)
        second = lax.dot_general(slip_ref[:events, :], lo, NT, preferred_element_type=jnp.float32)
        out_ref[j] = first[:events] + first[events:] + second


def first_body(me_ref, own_ref, came_ref, kernel_ref, mark_ref, slip_ref, out_ref, dense):
    assemble(me_ref[0], own_ref, came_ref, slip_ref, dense)
    stress(slip_ref, kernel_ref, out_ref)


def halving_order(width):
    bits = width.bit_length() - 1
    return [int(f"{k:0{bits}b}"[::-1], 2) for k in range(width)]


def per_device(kernel, slip_delta, block_list, live_count, direct_effect, load_rate, time_before):
    width = lax.axis_size("cols")
    height = lax.axis_size("rows")
    events_here, entries = block_list.shape
    half = events_here // 2
    events = events_here * width
    receivers, sources = kernel.shape
    blocks_here = sources // BLOCK
    me = jnp.stack([lax.axis_index("rows"), lax.axis_index("cols")]).astype(jnp.int32)

    order = halving_order(width)
    share = receivers // width
    quarter = width // 4
    near_keep, far_keep = order[0 : 2 * quarter : 2], order[1 : 2 * quarter : 2]
    near_send, far_send = order[2 * quarter :: 2], order[2 * quarter + 1 :: 2]
    held_shape = pltpu.VMEM((quarter, share, sources), jnp.float32)
    in_hbm, in_vmem = (
        functools.partial(pltpu.with_memory_space_constraint, memory_space=m) for m in (pltpu.HBM, pltpu.VMEM)
    )
    packed = pl.pallas_call(
        pack_body,
        out_shape=f32(2, half + 1, SUB, BLOCK),
        in_specs=[SMEM_SPEC] + [HBM_SPEC] * 3,
        out_specs=VMEM_SPEC,
        scratch_shapes=[
            pltpu.VMEM(slip_delta.shape, jnp.float32),
            pltpu.VMEM(block_list.shape, jnp.int32),
            pltpu.SMEM(live_count.shape, jnp.int32),
            pltpu.VMEM((SUB, BLOCK), jnp.float32),
            pltpu.SemaphoreType.DMA((3,)),
        ],
        compiler_params=params(4),
        name="pack",
    )(me, in_hbm(slip_delta), in_hbm(block_list), in_hbm(live_count))
    held = packed[None]
    step = 2
    while step < height:
        held = jnp.concatenate([held, send_xor(held, "rows", step)], axis=0)
        step *= 2
    came = send_xor(held[:, 1], "rows", 1)

    dense = pl.pallas_call(
        functools.partial(densify_body, entries),
        out_shape=f32(width, half, blocks_here, BLOCK),
        in_specs=[SMEM_SPEC, VMEM_SPEC, VMEM_SPEC],
        out_specs=VMEM_SPEC,
        scratch_shapes=[pltpu.VMEM((half, height * entries, BLOCK), jnp.float32)],
        compiler_params=params(8),
        name="densify",
    )(me, held[:, 0], came)
    dense, after = lax.optimization_barrier((dense, me))
    mine = lax.all_to_all(dense, "cols", 0, 0, tiled=True)
    mark, far_send_kernel, near_send_kernel, far_keep_kernel, near_keep_kernel = pl.pallas_call(
        functools.partial(fetch_body, (far_send, near_send, far_keep, near_keep)),
        out_shape=[f32(SUB, BLOCK)] + [held_shape] * 4,
        in_specs=[SMEM_SPEC, HBM_SPEC],
        out_specs=[VMEM_SPEC] * 5,
        scratch_shapes=[pltpu.SemaphoreType.DMA((4, quarter, PIECES))],
        compiler_params=params(4),
        cost_estimate=pl.CostEstimate(flops=0, bytes_accessed=8 * receivers * sources, transcendentals=0),
        name="fetch",
    )(after, in_hbm(kernel))
    mine, mark = lax.optimization_barrier((mine, mark))

    cost = pl.CostEstimate(
        flops=6 * quarter * share * sources * events,
        bytes_accessed=4 * quarter * share * sources,
        transcendentals=0,
    )
    slips, far_sent = pl.pallas_call(
        first_body,
        out_shape=[bf16(2 * events, sources), f32(quarter, events, share)],
        in_specs=[SMEM_SPEC] + [VMEM_SPEC] * 4,
        out_specs=[VMEM_SPEC] * 2,
        scratch_shapes=[pltpu.VMEM((events, blocks_here, BLOCK), jnp.float32)],
        compiler_params=params(8),
        cost_estimate=cost,
        name="first_stress",
    )(me, mine, send_xor(mine, "rows", 1), in_vmem(far_send_kernel), mark)

    def later(held):
        return pl.pallas_call(
            stress,
            out_shape=f32(quarter, events, share),
            in_specs=[VMEM_SPEC, VMEM_SPEC],
            out_specs=VMEM_SPEC,
            compiler_params=params(8),
            cost_estimate=cost,
            name="stress",
        )(slips, in_vmem(held))

    far_came = send_xor(far_sent, "cols", 1)
    near_came = send_xor(later(near_send_kernel), "cols", 1)
    far = later(far_keep_kernel) + far_came
    near = later(near_keep_kernel) + near_came
    step = 2
    while step < width // 2:
        keep = far.shape[0] // 2
        far = far[:keep] + send_xor(far[keep:], "cols", step)
        near = near[:keep] + send_xor(near[keep:], "cols", step)
        step *= 2
    stress_change = near[0] + send_xor(far[0], "cols", step)
    scale = direct_effect[None, :]
    growth = jnp.expm1(load_rate * time_before / direct_effect)[None, :]
    log_time = jnp.log(scale / load_rate[None, :]) + jnp.log(
        jnp.log1p(jnp.exp(-stress_change / scale) * growth)
    )
    return (stress_change.T, log_time.T)


def solution(mesh):
    in_specs = (
        P("rows", "cols"),
        P("cols", "rows", None),
        P("cols", "rows"),
        P("cols"),
        P(("rows", "cols")),
        P(("rows", "cols")),
        P(("rows", "cols")),
    )
    out_specs = (P(("rows", "cols"), None), P(("rows", "cols"), None))
    return jax.shard_map(
        per_device, mesh=mesh, in_specs=in_specs, out_specs=out_specs, check_vma=False
    )
```

```python
import functools

import jax
import jax.numpy as jnp
from jax import lax
from jax.experimental import pallas as pl
from jax.experimental.pallas import tpu as pltpu
from jax.sharding import PartitionSpec as P

BLOCK = 128
SUB = 8
VMEM_SPEC = pl.BlockSpec(memory_space=pltpu.VMEM)
SMEM_SPEC = pl.BlockSpec(memory_space=pltpu.SMEM)
HBM_SPEC = pl.BlockSpec(memory_space=pltpu.HBM)
MIB = 1024 * 1024
NT = (((1,), (1,)), ((), ()))


def f32(*shape):
    return jax.ShapeDtypeStruct(shape, jnp.float32)


def bf16(*shape):
    return jax.ShapeDtypeStruct(shape, jnp.bfloat16)


def params(mib):
    return pltpu.CompilerParams(vmem_limit_bytes=mib * MIB)


def send_xor(block, axis, k):
    return lax.ppermute(block, axis, [(r, r ^ k) for r in range(lax.axis_size(axis))])


def pack_body(me_ref, slip_hbm, list_hbm, count_hbm, out_ref, slip_ref, list_ref, count_ref, ids, sems):
    copies = [
        pltpu.make_async_copy(src, dst, sems.at[j])
        for j, (src, dst) in enumerate(((list_hbm, list_ref), (count_hbm, count_ref), (slip_hbm, slip_ref)))
    ]
    for copy in copies:
        copy.start()
    events, entries = list_ref.shape
    half = events // 2
    row = me_ref[0]
    entry = lax.broadcasted_iota(jnp.int32, (events, entries), 1) + row * entries
    event = lax.broadcasted_iota(jnp.int32, (events, entries), 0)
    ids[...] = jnp.full(ids.shape, -1.0, jnp.float32)
    for copy in copies:
        copy.wait()
    count = jnp.zeros((events, entries), jnp.int32)
    for e in range(events):
        count = jnp.where(event == e, count_ref[e], count)
    ids[0:events, 0:entries] = jnp.where(entry < count, list_ref[...], -1).astype(jnp.float32)
    ids[...] = pltpu.roll(ids[...], row * entries, 1)
    for h in range(2):
        first = ((row % 2) ^ h) * half
        for i in range(half):
            out_ref[h, i, 0:entries, :] = slip_ref[first + i]
            out_ref[h, half, i : i + 1, :] = ids[pl.ds(first + i, 1), :]


def densify_body(entries, me_ref, own_ref, came_ref, _, out_ref, slips):
    halves, half = own_ref.shape[0], own_ref.shape[1] - 1
    width, _, blocks_here, _ = out_ref.shape
    blocks = width * blocks_here
    live = 2 * halves * entries
    row = me_ref[0]
    for i in range(half):
        ids = jnp.full((1, BLOCK), -1.0, jnp.float32)
        for ref in (own_ref, came_ref):
            for j in range(halves):
                ids = jnp.maximum(ids, ref[j, half, i : i + 1, :])
        ids = jnp.broadcast_to(ids, (blocks, BLOCK))[:, :live]
        number = lax.broadcasted_iota(jnp.int32, ids.shape, 0).astype(jnp.float32)
        onehot = (ids == number).astype(jnp.bfloat16)
        for core, ref in enumerate((own_ref, came_ref)):
            for j in range(halves):
                source = row ^ (2 * j + core)
                slips[i, pl.ds(pl.multiple_of(source * entries, entries), entries), :] = ref[j, i, 0:entries, :]
        slip = slips[i]
        total = jnp.zeros((blocks, BLOCK), jnp.float32)
        for _ in range(3):
            piece = slip.astype(jnp.bfloat16)
            slip = slip - piece.astype(jnp.float32)
            total = total + jnp.dot(onehot, piece, preferred_element_type=jnp.float32)
        out_ref[:, i] = total.reshape(width, blocks_here, BLOCK)


def assemble(row, own_ref, came_ref, out_ref, dense):
    width, half, blocks_here, _ = own_ref.shape
    events = dense.shape[0]
    core = row % 2
    for c in range(width):
        for other, ref in enumerate((own_ref, came_ref)):
            for i in range(half):
                dense[(2 * c + (core ^ other)) * half + i] = ref[c, i]
    flat = dense.reshape(events * blocks_here, BLOCK)
    for t in range(events // (2 * SUB)):
        for b in range(blocks_here):
            rows = [
                flat[pl.ds((2 * t + u) * SUB * blocks_here + b, SUB, stride=blocks_here), :] for u in range(2)
            ]
            slip = jnp.concatenate(rows, axis=0)
            hi = slip.astype(jnp.bfloat16)
            lo = (slip - hi.astype(jnp.float32)).astype(jnp.bfloat16)
            where = slice(b * BLOCK, (b + 1) * BLOCK)
            out_ref[2 * t * SUB : 2 * (t + 1) * SUB, where] = hi
            out_ref[events + 2 * t * SUB : events + 2 * (t + 1) * SUB, where] = lo


def stress(targets, col, slip_ref, kernel_ref, out_ref):
    events = slip_ref.shape[0] // 2
    share = out_ref.shape[2]
    for j, k in enumerate(targets):
        block = kernel_ref[pl.ds(pl.multiple_of((col ^ k) * share, share), share), :]
        hi = block.astype(jnp.bfloat16)
        lo = (block - hi.astype(jnp.float32)).astype(jnp.bfloat16)
        first = lax.dot_general(slip_ref[...], hi, NT, preferred_element_type=jnp.float32)
        second = lax.dot_general(slip_ref[:events, :], lo, NT, preferred_element_type=jnp.float32)
        out_ref[j] = first[:events] + first[events:] + second


def first_body(targets, me_ref, own_ref, came_ref, kernel_ref, slip_ref, out_ref, dense):
    assemble(me_ref[0], own_ref, came_ref, slip_ref, dense)
    stress(targets, me_ref[1], slip_ref, kernel_ref, out_ref)


def later_body(targets, me_ref, slip_ref, kernel_ref, out_ref):
    stress(targets, me_ref[1], slip_ref, kernel_ref, out_ref)


def halving_order(width):
    bits = width.bit_length() - 1
    return [int(f"{k:0{bits}b}"[::-1], 2) for k in range(width)]


def per_device(kernel, slip_delta, block_list, live_count, direct_effect, load_rate, time_before):
    width = lax.axis_size("cols")
    height = lax.axis_size("rows")
    events_here, entries = block_list.shape
    half = events_here // 2
    events = events_here * width
    receivers, sources = kernel.shape
    blocks_here = sources // BLOCK
    me = jnp.stack([lax.axis_index("rows"), lax.axis_index("cols")]).astype(jnp.int32)

    order = halving_order(width)
    share = receivers // width
    quarter = width // 4
    near_keep, far_keep = order[0 : 2 * quarter : 2], order[1 : 2 * quarter : 2]
    near_send, far_send = order[2 * quarter :: 2], order[2 * quarter + 1 :: 2]
    in_hbm = functools.partial(pltpu.with_memory_space_constraint, memory_space=pltpu.HBM)
    packed = pl.pallas_call(
        pack_body,
        out_shape=f32(2, half + 1, SUB, BLOCK),
        in_specs=[SMEM_SPEC] + [HBM_SPEC] * 3,
        out_specs=VMEM_SPEC,
        scratch_shapes=[
            pltpu.VMEM(slip_delta.shape, jnp.float32),
            pltpu.VMEM(block_list.shape, jnp.int32),
            pltpu.SMEM(live_count.shape, jnp.int32),
            pltpu.VMEM((SUB, BLOCK), jnp.float32),
            pltpu.SemaphoreType.DMA((3,)),
        ],
        compiler_params=params(4),
        name="pack",
    )(me, in_hbm(slip_delta), in_hbm(block_list), in_hbm(live_count))
    held = packed[None]
    step = 2
    while step < height:
        held = jnp.concatenate([held, send_xor(held, "rows", step)], axis=0)
        step *= 2
    came = send_xor(held[:, 1], "rows", 1)

    dense = pl.pallas_call(
        functools.partial(densify_body, entries),
        out_shape=f32(width, half, blocks_here, BLOCK),
        in_specs=[SMEM_SPEC, VMEM_SPEC, VMEM_SPEC, HBM_SPEC],
        out_specs=VMEM_SPEC,
        scratch_shapes=[pltpu.VMEM((half, height * entries, BLOCK), jnp.float32)],
        compiler_params=params(8),
        name="densify",
    )(me, held[:, 0], came, in_hbm(kernel))
    mine = lax.all_to_all(dense, "cols", 0, 0, tiled=True)

    cost = pl.CostEstimate(
        flops=6 * quarter * share * sources * events,
        bytes_accessed=4 * quarter * share * sources,
        transcendentals=0,
    )
    slips, far_sent = pl.pallas_call(
        functools.partial(first_body, far_send),
        out_shape=[bf16(2 * events, sources), f32(quarter, events, share)],
        in_specs=[SMEM_SPEC] + [VMEM_SPEC] * 3,
        out_specs=[VMEM_SPEC] * 2,
        scratch_shapes=[pltpu.VMEM((events, blocks_here, BLOCK), jnp.float32)],
        compiler_params=params(8),
        cost_estimate=cost,
        name="first_stress",
    )(me, mine, send_xor(mine, "rows", 1), kernel)

    def later(targets):
        return pl.pallas_call(
            functools.partial(later_body, targets),
            out_shape=f32(quarter, events, share),
            in_specs=[SMEM_SPEC, VMEM_SPEC, VMEM_SPEC],
            out_specs=VMEM_SPEC,
            compiler_params=params(8),
            cost_estimate=cost,
            name="stress",
        )(me, slips, kernel)

    far_came = send_xor(far_sent, "cols", 1)
    near_came = send_xor(later(near_send), "cols", 1)
    far = later(far_keep) + far_came
    near = later(near_keep) + near_came
    step = 2
    while step < width // 2:
        keep = far.shape[0] // 2
        far = far[:keep] + send_xor(far[keep:], "cols", step)
        near = near[:keep] + send_xor(near[keep:], "cols", step)
        step *= 2
    stress_change = near[0] + send_xor(far[0], "cols", step)
    scale = direct_effect[None, :]
    growth = jnp.expm1(load_rate * time_before / direct_effect)[None, :]
    log_time = jnp.log(scale / load_rate[None, :]) + jnp.log(
        jnp.log1p(jnp.exp(-stress_change / scale) * growth)
    )
    return (stress_change.T, log_time.T)


def solution(mesh):
    in_specs = (
        P("rows", "cols"),
        P("cols", "rows", None),
        P("cols", "rows"),
        P("cols"),
        P(("rows", "cols")),
        P(("rows", "cols")),
        P(("rows", "cols")),
    )
    out_specs = (P(("rows", "cols"), None), P(("rows", "cols"), None))
    return jax.shard_map(
        per_device, mesh=mesh, in_specs=in_specs, out_specs=out_specs, check_vma=False
    )
```

```python
import functools

import jax
import jax.numpy as jnp
from jax import lax
from jax.experimental import pallas as pl
from jax.experimental.pallas import tpu as pltpu
from jax.sharding import PartitionSpec as P

BLOCK = 128
SUB = 8
VMEM_SPEC = pl.BlockSpec(memory_space=pltpu.VMEM)
SMEM_SPEC = pl.BlockSpec(memory_space=pltpu.SMEM)
HBM_SPEC = pl.BlockSpec(memory_space=pltpu.HBM)
MIB = 1024 * 1024
NT = (((1,), (1,)), ((), ()))


def f32(*shape):
    return jax.ShapeDtypeStruct(shape, jnp.float32)


def bf16(*shape):
    return jax.ShapeDtypeStruct(shape, jnp.bfloat16)


def params(mib):
    return pltpu.CompilerParams(vmem_limit_bytes=mib * MIB)


def send_xor(block, axis, k):
    return lax.ppermute(block, axis, [(r, r ^ k) for r in range(lax.axis_size(axis))])


def pack_body(me_ref, slip_hbm, list_hbm, count_hbm, out_ref, slip_ref, list_ref, count_ref, ids, sems):
    copies = [
        pltpu.make_async_copy(src, dst, sems.at[j])
        for j, (src, dst) in enumerate(((list_hbm, list_ref), (count_hbm, count_ref), (slip_hbm, slip_ref)))
    ]
    for copy in copies:
        copy.start()
    events, entries = list_ref.shape
    row = me_ref[0]
    entry = lax.broadcasted_iota(jnp.int32, (events, entries), 1) + row * entries
    event = lax.broadcasted_iota(jnp.int32, (events, entries), 0)
    ids[...] = jnp.full(ids.shape, -1.0, jnp.float32)
    for copy in copies:
        copy.wait()
    count = jnp.zeros((events, entries), jnp.int32)
    for e in range(events):
        count = jnp.where(event == e, count_ref[e], count)
    ids[0:events, 0:entries] = jnp.where(entry < count, list_ref[...], -1).astype(jnp.float32)
    out_ref[events] = pltpu.roll(ids[...], row * entries, 1)
    for e in range(events):
        out_ref[e, 0:entries, :] = slip_ref[e]


def densify_body(entries, me_ref, own_ref, came_ref, _, out_ref, slips):
    halves, events = own_ref.shape[0], own_ref.shape[1] - 1
    width, _, blocks, _ = out_ref.shape
    live = 2 * halves * entries
    row = me_ref[0]
    line = lax.broadcasted_iota(jnp.int32, (width * blocks, live), 0)
    number = ((line // blocks * 2 + row % 2) * blocks + line % blocks).astype(jnp.float32)
    for e in range(events):
        ids = jnp.full((1, BLOCK), -1.0, jnp.float32)
        for ref in (own_ref, came_ref):
            for j in range(halves):
                ids = jnp.maximum(ids, ref[j, events, e : e + 1, :])
        ids = jnp.broadcast_to(ids, (width * blocks, BLOCK))[:, :live]
        onehot = (ids == number).astype(jnp.bfloat16)
        for core, ref in enumerate((own_ref, came_ref)):
            for j in range(halves):
                source = row ^ (2 * j + core)
                slips[e, pl.ds(pl.multiple_of(source * entries, entries), entries), :] = ref[j, e, 0:entries, :]
        slip = slips[e]
        total = jnp.zeros((width * blocks, BLOCK), jnp.float32)
        for _ in range(3):
            piece = slip.astype(jnp.bfloat16)
            slip = slip - piece.astype(jnp.float32)
            total = total + jnp.dot(onehot, piece, preferred_element_type=jnp.float32)
        out_ref[:, e] = total.reshape(width, blocks, BLOCK)


def assemble(dense_ref, out_ref):
    events, blocks = out_ref.shape[0] // 2, dense_ref.shape[2]
    flat = dense_ref.reshape(events * blocks, BLOCK)
    for t in range(events // (2 * SUB)):
        for b in range(blocks):
            rows = [flat[pl.ds((2 * t + u) * SUB * blocks + b, SUB, stride=blocks), :] for u in range(2)]
            slip = jnp.concatenate(rows, axis=0)
            hi = slip.astype(jnp.bfloat16)
            lo = (slip - hi.astype(jnp.float32)).astype(jnp.bfloat16)
            where = slice(b * BLOCK, (b + 1) * BLOCK)
            out_ref[2 * t * SUB : 2 * (t + 1) * SUB, where] = hi
            out_ref[events + 2 * t * SUB : events + 2 * (t + 1) * SUB, where] = lo


def stress(k, core, col, slip_ref, kernel_ref):
    events, patches = slip_ref.shape[0] // 2, slip_ref.shape[1]
    block = kernel_ref[col ^ k, :, pl.ds(pl.multiple_of(core * patches, patches), patches)]
    hi = block.astype(jnp.bfloat16)
    lo = (block - hi.astype(jnp.float32)).astype(jnp.bfloat16)
    first = lax.dot_general(slip_ref[...], hi, NT, preferred_element_type=jnp.float32)
    second = lax.dot_general(slip_ref[:events, :], lo, NT, preferred_element_type=jnp.float32)
    return first[:events] + first[events:] + second


def own_body(targets, me_ref, dense_ref, kernel_ref, slip_ref, out_ref):
    assemble(dense_ref, slip_ref)
    for j, k in enumerate(targets):
        out_ref[j] = stress(k, me_ref[0] % 2, me_ref[1], slip_ref, kernel_ref)


def other_body(targets, me_ref, dense_ref, kernel_ref, sum_ref, slip_ref, out_ref):
    assemble(dense_ref, slip_ref)
    for j, k in enumerate(targets):
        out_ref[j] = sum_ref[j] + stress(k, 1 - me_ref[0] % 2, me_ref[1], slip_ref, kernel_ref)


def both_body(targets, me_ref, own_ref, other_ref, kernel_ref, out_ref):
    core = me_ref[0] % 2
    for j, k in enumerate(targets):
        out_ref[j] = stress(k, core, me_ref[1], own_ref, kernel_ref) + stress(
            k, 1 - core, me_ref[1], other_ref, kernel_ref
        )


def halving_order(width):
    bits = width.bit_length() - 1
    return [int(f"{k:0{bits}b}"[::-1], 2) for k in range(width)]


def per_device(kernel, slip_delta, block_list, live_count, direct_effect, load_rate, time_before):
    width = lax.axis_size("cols")
    height = lax.axis_size("rows")
    events_here, entries = block_list.shape
    events = events_here * width
    receivers, sources = kernel.shape
    blocks_here = sources // BLOCK
    me = jnp.stack([lax.axis_index("rows"), lax.axis_index("cols")]).astype(jnp.int32)

    order = halving_order(width)
    share = receivers // width
    quarter = width // 4
    near_keep, far_keep = order[0 : 2 * quarter : 2], order[1 : 2 * quarter : 2]
    near_send, far_send = order[2 * quarter :: 2], order[2 * quarter + 1 :: 2]
    in_hbm = functools.partial(pltpu.with_memory_space_constraint, memory_space=pltpu.HBM)
    kernel = kernel.reshape(width, share, sources)
    packed = pl.pallas_call(
        pack_body,
        out_shape=f32(events_here + 1, SUB, BLOCK),
        in_specs=[SMEM_SPEC] + [HBM_SPEC] * 3,
        out_specs=VMEM_SPEC,
        scratch_shapes=[
            pltpu.VMEM(slip_delta.shape, jnp.float32),
            pltpu.VMEM(block_list.shape, jnp.int32),
            pltpu.SMEM(live_count.shape, jnp.int32),
            pltpu.VMEM((SUB, BLOCK), jnp.float32),
            pltpu.SemaphoreType.DMA((3,)),
        ],
        compiler_params=params(4),
        name="pack",
    )(me, in_hbm(slip_delta), in_hbm(block_list), in_hbm(live_count))
    held = packed[None]
    step = 2
    while step < height:
        held = jnp.concatenate([held, send_xor(held, "rows", step)], axis=0)
        step *= 2

    blocks_half = blocks_here // 2
    dense = pl.pallas_call(
        functools.partial(densify_body, entries),
        out_shape=f32(width, events_here, blocks_half, BLOCK),
        in_specs=[SMEM_SPEC, VMEM_SPEC, VMEM_SPEC, HBM_SPEC],
        out_specs=VMEM_SPEC,
        scratch_shapes=[pltpu.VMEM((events_here, height * entries, BLOCK), jnp.float32)],
        compiler_params=params(8),
        name="densify",
    )(me, held, send_xor(held, "rows", 1), in_hbm(kernel))
    mine = lax.all_to_all(dense, "cols", 0, 0, tiled=True)

    def call(body, targets, outs, *args):
        return pl.pallas_call(
            functools.partial(body, targets),
            out_shape=outs,
            in_specs=[SMEM_SPEC] + [VMEM_SPEC] * len(args),
            out_specs=jax.tree.map(lambda _: VMEM_SPEC, outs),
            compiler_params=params(8),
            cost_estimate=pl.CostEstimate(
                flops=6 * quarter * share * sources * events,
                bytes_accessed=4 * quarter * share * sources,
                transcendentals=0,
            ),
            name=body.__name__.removesuffix("_body") + "_stress",
        )(me, *args)

    slips = bf16(2 * events, blocks_half * BLOCK)
    sums = f32(quarter, events, share)
    came = send_xor(mine, "rows", 1)
    own, own_sum = call(own_body, far_send, [slips, sums], mine, kernel)
    other, far_sent = call(other_body, far_send, [slips, sums], came, kernel, own_sum)

    def later(targets):
        return call(both_body, targets, sums, own, other, kernel)

    far_came = send_xor(far_sent, "cols", 1)
    near_came = send_xor(later(near_send), "cols", 1)
    far = later(far_keep) + far_came
    near = later(near_keep) + near_came
    step = 2
    while step < width // 2:
        keep = far.shape[0] // 2
        far = far[:keep] + send_xor(far[keep:], "cols", step)
        near = near[:keep] + send_xor(near[keep:], "cols", step)
        step *= 2
    stress_change = near[0] + send_xor(far[0], "cols", step)
    scale = direct_effect[None, :]
    growth = jnp.expm1(load_rate * time_before / direct_effect)[None, :]
    log_time = jnp.log(scale / load_rate[None, :]) + jnp.log(
        jnp.log1p(jnp.exp(-stress_change / scale) * growth)
    )
    return (stress_change.T, log_time.T)


def solution(mesh):
    in_specs = (
        P("rows", "cols"),
        P("cols", "rows", None),
        P("cols", "rows"),
        P("cols"),
        P(("rows", "cols")),
        P(("rows", "cols")),
        P(("rows", "cols")),
    )
    out_specs = (P(("rows", "cols"), None), P(("rows", "cols"), None))
    return jax.shard_map(
        per_device, mesh=mesh, in_specs=in_specs, out_specs=out_specs, check_vma=False
    )
```

```python
import functools

import jax
import jax.numpy as jnp
from jax import lax
from jax.experimental import pallas as pl
from jax.experimental.pallas import tpu as pltpu
from jax.sharding import PartitionSpec as P

BLOCK = 128
SUB = 8
CHUNK = 256
VMEM_SPEC = pl.BlockSpec(memory_space=pltpu.VMEM)
SMEM_SPEC = pl.BlockSpec(memory_space=pltpu.SMEM)
HBM_SPEC = pl.BlockSpec(memory_space=pltpu.HBM)
MIB = 1024 * 1024
NT = (((1,), (1,)), ((), ()))


def f32(*shape):
    return jax.ShapeDtypeStruct(shape, jnp.float32)


def bf16(*shape):
    return jax.ShapeDtypeStruct(shape, jnp.bfloat16)


def params(mib):
    return pltpu.CompilerParams(vmem_limit_bytes=mib * MIB)


def send_xor(block, axis, k):
    return lax.ppermute(block, axis, [(r, r ^ k) for r in range(lax.axis_size(axis))])


def pack_body(me_ref, slip_hbm, list_hbm, count_hbm, out_ref, slip_ref, list_ref, count_ref, ids, sems):
    copies = [
        pltpu.make_async_copy(src, dst, sems.at[j])
        for j, (src, dst) in enumerate(((list_hbm, list_ref), (count_hbm, count_ref), (slip_hbm, slip_ref)))
    ]
    for copy in copies:
        copy.start()
    events, entries = list_ref.shape
    row = me_ref[0]
    entry = lax.broadcasted_iota(jnp.int32, (events, entries), 1) + row * entries
    event = lax.broadcasted_iota(jnp.int32, (events, entries), 0)
    ids[...] = jnp.full(ids.shape, -1.0, jnp.float32)
    for copy in copies:
        copy.wait()
    count = jnp.zeros((events, entries), jnp.int32)
    for e in range(events):
        count = jnp.where(event == e, count_ref[e], count)
    ids[0:events, 0:entries] = jnp.where(entry < count, list_ref[...], -1).astype(jnp.float32)
    out_ref[events] = pltpu.roll(ids[...], row * entries, 1)
    for e in range(events):
        out_ref[e, 0:entries, :] = slip_ref[e]


def densify_body(entries, me_ref, own_ref, came_ref, _, out_ref, slips):
    halves, events = own_ref.shape[0], own_ref.shape[1] - 1
    width, _, blocks, _ = out_ref.shape
    live = 2 * halves * entries
    row = me_ref[0]
    line = lax.broadcasted_iota(jnp.int32, (width * blocks, live), 0)
    number = ((line // blocks * 2 + row % 2) * blocks + line % blocks).astype(jnp.float32)
    for e in range(events):
        ids = jnp.full((1, BLOCK), -1.0, jnp.float32)
        for ref in (own_ref, came_ref):
            for j in range(halves):
                ids = jnp.maximum(ids, ref[j, events, e : e + 1, :])
        ids = jnp.broadcast_to(ids, (width * blocks, BLOCK))[:, :live]
        onehot = (ids == number).astype(jnp.bfloat16)
        for core, ref in enumerate((own_ref, came_ref)):
            for j in range(halves):
                source = row ^ (2 * j + core)
                slips[e, pl.ds(pl.multiple_of(source * entries, entries), entries), :] = ref[j, e, 0:entries, :]
        slip = slips[e]
        total = jnp.zeros((width * blocks, BLOCK), jnp.float32)
        for _ in range(3):
            piece = slip.astype(jnp.bfloat16)
            slip = slip - piece.astype(jnp.float32)
            total = total + jnp.dot(onehot, piece, preferred_element_type=jnp.float32)
        out_ref[:, e] = total.reshape(width, blocks, BLOCK)


def assemble(dense_ref, out_ref):
    events, blocks = out_ref.shape[0] // 2, dense_ref.shape[2]
    flat = dense_ref.reshape(events * blocks, BLOCK)
    for t in range(events // (2 * SUB)):
        for b in range(blocks):
            rows = [flat[pl.ds((2 * t + u) * SUB * blocks + b, SUB, stride=blocks), :] for u in range(2)]
            slip = jnp.concatenate(rows, axis=0)
            hi = slip.astype(jnp.bfloat16)
            lo = (slip - hi.astype(jnp.float32)).astype(jnp.bfloat16)
            where = slice(b * BLOCK, (b + 1) * BLOCK)
            out_ref[2 * t * SUB : 2 * (t + 1) * SUB, where] = hi
            out_ref[events + 2 * t * SUB : events + 2 * (t + 1) * SUB, where] = lo


def stress(k, core, col, slip_ref, kernel_ref):
    events, patches = slip_ref.shape[0] // 2, slip_ref.shape[1]
    rows = kernel_ref.at[col ^ k]
    both = low = 0.0
    for t in range(0, patches, CHUNK):
        block = rows[:, pl.ds(pl.multiple_of(core * patches + t, CHUNK), CHUNK)]
        hi = block.astype(jnp.bfloat16)
        lo = (block - hi.astype(jnp.float32)).astype(jnp.bfloat16)
        both += lax.dot_general(slip_ref[:, t : t + CHUNK], hi, NT, preferred_element_type=jnp.float32)
        low += lax.dot_general(slip_ref[:events, t : t + CHUNK], lo, NT, preferred_element_type=jnp.float32)
    return both[:events] + both[events:] + low


def own_body(targets, me_ref, dense_ref, kernel_ref, slip_ref, out_ref):
    assemble(dense_ref, slip_ref)
    for j, k in enumerate(targets):
        out_ref[j] = stress(k, me_ref[0] % 2, me_ref[1], slip_ref, kernel_ref)


def other_body(targets, me_ref, dense_ref, kernel_ref, sum_ref, slip_ref, out_ref):
    assemble(dense_ref, slip_ref)
    for j, k in enumerate(targets):
        out_ref[j] = sum_ref[j] + stress(k, 1 - me_ref[0] % 2, me_ref[1], slip_ref, kernel_ref)


def both_body(targets, me_ref, own_ref, other_ref, kernel_ref, out_ref):
    core = me_ref[0] % 2
    for j, k in enumerate(targets):
        out_ref[j] = stress(k, core, me_ref[1], own_ref, kernel_ref) + stress(
            k, 1 - core, me_ref[1], other_ref, kernel_ref
        )


def halving_order(width):
    bits = width.bit_length() - 1
    return [int(f"{k:0{bits}b}"[::-1], 2) for k in range(width)]


def per_device(kernel, slip_delta, block_list, live_count, direct_effect, load_rate, time_before):
    width = lax.axis_size("cols")
    height = lax.axis_size("rows")
    events_here, entries = block_list.shape
    events = events_here * width
    receivers, sources = kernel.shape
    blocks_here = sources // BLOCK
    me = jnp.stack([lax.axis_index("rows"), lax.axis_index("cols")]).astype(jnp.int32)

    order = halving_order(width)
    share = receivers // width
    quarter = width // 4
    near_keep, far_keep = order[0 : 2 * quarter : 2], order[1 : 2 * quarter : 2]
    near_send, far_send = order[2 * quarter :: 2], order[2 * quarter + 1 :: 2]
    in_hbm = functools.partial(pltpu.with_memory_space_constraint, memory_space=pltpu.HBM)
    kernel = kernel.reshape(width, share, sources)
    packed = pl.pallas_call(
        pack_body,
        out_shape=f32(events_here + 1, SUB, BLOCK),
        in_specs=[SMEM_SPEC] + [HBM_SPEC] * 3,
        out_specs=VMEM_SPEC,
        scratch_shapes=[
            pltpu.VMEM(slip_delta.shape, jnp.float32),
            pltpu.VMEM(block_list.shape, jnp.int32),
            pltpu.SMEM(live_count.shape, jnp.int32),
            pltpu.VMEM((SUB, BLOCK), jnp.float32),
            pltpu.SemaphoreType.DMA((3,)),
        ],
        compiler_params=params(4),
        name="pack",
    )(me, in_hbm(slip_delta), in_hbm(block_list), in_hbm(live_count))
    held = packed[None]
    step = 2
    while step < height:
        held = jnp.concatenate([held, send_xor(held, "rows", step)], axis=0)
        step *= 2

    blocks_half = blocks_here // 2
    dense = pl.pallas_call(
        functools.partial(densify_body, entries),
        out_shape=f32(width, events_here, blocks_half, BLOCK),
        in_specs=[SMEM_SPEC, VMEM_SPEC, VMEM_SPEC, HBM_SPEC],
        out_specs=VMEM_SPEC,
        scratch_shapes=[pltpu.VMEM((events_here, height * entries, BLOCK), jnp.float32)],
        compiler_params=params(8),
        name="densify",
    )(me, held, send_xor(held, "rows", 1), in_hbm(kernel))
    mine = lax.all_to_all(dense, "cols", 0, 0, tiled=True)

    def call(body, targets, outs, *args):
        return pl.pallas_call(
            functools.partial(body, targets),
            out_shape=outs,
            in_specs=[SMEM_SPEC] + [VMEM_SPEC] * len(args),
            out_specs=jax.tree.map(lambda _: VMEM_SPEC, outs),
            compiler_params=params(8),
            cost_estimate=pl.CostEstimate(
                flops=6 * quarter * share * sources * events,
                bytes_accessed=4 * quarter * share * sources,
                transcendentals=0,
            ),
            name=body.__name__.removesuffix("_body") + "_stress",
        )(me, *args)

    slips = bf16(2 * events, blocks_half * BLOCK)
    sums = f32(quarter, events, share)
    came = send_xor(mine, "rows", 1)
    own, own_sum = call(own_body, far_send, [slips, sums], mine, kernel)
    other, far_sent = call(other_body, far_send, [slips, sums], came, kernel, own_sum)

    def later(targets):
        return call(both_body, targets, sums, own, other, kernel)

    far_came = send_xor(far_sent, "cols", 1)
    near_sent = later(near_send)
    far = later(far_keep) + far_came
    near_sent, far = lax.optimization_barrier((near_sent, far))
    near_came = send_xor(near_sent, "cols", 1)
    near = later(near_keep) + near_came
    step = 2
    while step < width // 2:
        keep = far.shape[0] // 2
        far = far[:keep] + send_xor(far[keep:], "cols", step)
        near = near[:keep] + send_xor(near[keep:], "cols", step)
        step *= 2
    stress_change = near[0] + send_xor(far[0], "cols", step)
    scale = direct_effect[None, :]
    growth = jnp.expm1(load_rate * time_before / direct_effect)[None, :]
    log_time = jnp.log(scale / load_rate[None, :]) + jnp.log(
        jnp.log1p(jnp.exp(-stress_change / scale) * growth)
    )
    return (stress_change.T, log_time.T)


def solution(mesh):
    in_specs = (
        P("rows", "cols"),
        P("cols", "rows", None),
        P("cols", "rows"),
        P("cols"),
        P(("rows", "cols")),
        P(("rows", "cols")),
        P(("rows", "cols")),
    )
    out_specs = (P(("rows", "cols"), None), P(("rows", "cols"), None))
    return jax.shard_map(
        per_device, mesh=mesh, in_specs=in_specs, out_specs=out_specs, check_vma=False
    )
```

```python
import functools

import jax
import jax.numpy as jnp
from jax import lax
from jax.experimental import pallas as pl
from jax.experimental.pallas import tpu as pltpu
from jax.sharding import PartitionSpec as P

BLOCK = 128
SUB = 8
CHUNK = 256
VMEM_SPEC = pl.BlockSpec(memory_space=pltpu.VMEM)
HBM_SPEC = pl.BlockSpec(memory_space=pltpu.HBM)
MIB = 1024 * 1024
NT = (((1,), (1,)), ((), ()))


def f32(*shape):
    return jax.ShapeDtypeStruct(shape, jnp.float32)


def bf16(*shape):
    return jax.ShapeDtypeStruct(shape, jnp.bfloat16)


def params(mib):
    return pltpu.CompilerParams(vmem_limit_bytes=mib * MIB)


def send_xor(block, axis, k):
    return lax.ppermute(block, axis, [(r, r ^ k) for r in range(lax.axis_size(axis))])


def pack_body(slip_hbm, list_hbm, count_hbm, out_ref, slip_ref, list_ref, count_ref, ids, sems):
    copies = [
        pltpu.make_async_copy(src, dst, sems.at[j])
        for j, (src, dst) in enumerate(((list_hbm, list_ref), (count_hbm, count_ref), (slip_hbm, slip_ref)))
    ]
    for copy in copies:
        copy.start()
    events, entries = list_ref.shape
    row = lax.axis_index("rows")
    entry = lax.broadcasted_iota(jnp.int32, (events, entries), 1) + row * entries
    event = lax.broadcasted_iota(jnp.int32, (events, entries), 0)
    ids[...] = jnp.full(ids.shape, -1.0, jnp.float32)
    for copy in copies:
        copy.wait()
    count = jnp.zeros((events, entries), jnp.int32)
    for e in range(events):
        count = jnp.where(event == e, count_ref[e], count)
    ids[0:events, 0:entries] = jnp.where(entry < count, list_ref[...], -1).astype(jnp.float32)
    out_ref[events] = pltpu.roll(ids[...], row * entries, 1)
    for e in range(events):
        out_ref[e, 0:entries, :] = slip_ref[e]


def densify_body(entries, own_ref, came_ref, _, out_ref, slips):
    halves, events = own_ref.shape[0], own_ref.shape[1] - 1
    width, _, blocks, _ = out_ref.shape
    live = 2 * halves * entries
    row = lax.axis_index("rows")
    line = lax.broadcasted_iota(jnp.int32, (width * blocks, live), 0)
    number = ((line // blocks * 2 + row % 2) * blocks + line % blocks).astype(jnp.float32)
    for e in range(events):
        ids = jnp.full((1, BLOCK), -1.0, jnp.float32)
        for ref in (own_ref, came_ref):
            for j in range(halves):
                ids = jnp.maximum(ids, ref[j, events, e : e + 1, :])
        ids = jnp.broadcast_to(ids, (width * blocks, BLOCK))[:, :live]
        onehot = (ids == number).astype(jnp.bfloat16)
        for core, ref in enumerate((own_ref, came_ref)):
            for j in range(halves):
                source = row ^ (2 * j + core)
                slips[e, pl.ds(pl.multiple_of(source * entries, entries), entries), :] = ref[j, e, 0:entries, :]
        slip = slips[e]
        total = jnp.zeros((width * blocks, BLOCK), jnp.float32)
        for _ in range(3):
            piece = slip.astype(jnp.bfloat16)
            slip = slip - piece.astype(jnp.float32)
            total = total + jnp.dot(onehot, piece, preferred_element_type=jnp.float32)
        out_ref[:, e] = total.reshape(width, blocks, BLOCK)


def assemble(dense_ref, out_ref):
    events, blocks = out_ref.shape[0] // 2, dense_ref.shape[2]
    flat = dense_ref.reshape(events * blocks, BLOCK)
    for t in range(events // (2 * SUB)):
        for b in range(blocks):
            rows = [flat[pl.ds((2 * t + u) * SUB * blocks + b, SUB, stride=blocks), :] for u in range(2)]
            slip = jnp.concatenate(rows, axis=0)
            hi = slip.astype(jnp.bfloat16)
            lo = (slip - hi.astype(jnp.float32)).astype(jnp.bfloat16)
            where = slice(b * BLOCK, (b + 1) * BLOCK)
            out_ref[2 * t * SUB : 2 * (t + 1) * SUB, where] = hi
            out_ref[events + 2 * t * SUB : events + 2 * (t + 1) * SUB, where] = lo


def stress(k, other, slip_ref, kernel_ref):
    core = lax.axis_index("rows") % 2 ^ other
    events, patches = slip_ref.shape[0] // 2, slip_ref.shape[1]
    rows = kernel_ref.at[lax.axis_index("cols") ^ k]
    both = low = 0.0
    for t in range(0, patches, CHUNK):
        block = rows[:, pl.ds(pl.multiple_of(core * patches + t, CHUNK), CHUNK)]
        hi = block.astype(jnp.bfloat16)
        lo = (block - hi.astype(jnp.float32)).astype(jnp.bfloat16)
        both += lax.dot_general(slip_ref[:, t : t + CHUNK], hi, NT, preferred_element_type=jnp.float32)
        low += lax.dot_general(slip_ref[:events, t : t + CHUNK], lo, NT, preferred_element_type=jnp.float32)
    return both[:events] + both[events:] + low


def own_body(targets, dense_ref, kernel_ref, slip_ref, out_ref):
    assemble(dense_ref, slip_ref)
    for j, k in enumerate(targets):
        out_ref[j] = stress(k, 0, slip_ref, kernel_ref)


def other_body(targets, dense_ref, kernel_ref, sum_ref, slip_ref, out_ref):
    assemble(dense_ref, slip_ref)
    for j, k in enumerate(targets):
        out_ref[j] = sum_ref[j] + stress(k, 1, slip_ref, kernel_ref)


def both_body(targets, own_ref, other_ref, kernel_ref, out_ref):
    for j, k in enumerate(targets):
        out_ref[j] = stress(k, 0, own_ref, kernel_ref) + stress(k, 1, other_ref, kernel_ref)


def halving_order(width):
    bits = width.bit_length() - 1
    return [int(f"{k:0{bits}b}"[::-1], 2) for k in range(width)]


def per_device(kernel, slip_delta, block_list, live_count, direct_effect, load_rate, time_before):
    width = lax.axis_size("cols")
    height = lax.axis_size("rows")
    events_here, entries = block_list.shape
    events = events_here * width
    receivers, sources = kernel.shape
    blocks_here = sources // BLOCK

    order = halving_order(width)
    share = receivers // width
    quarter = width // 4
    near_keep, far_keep = order[0 : 2 * quarter : 2], order[1 : 2 * quarter : 2]
    near_send, far_send = order[2 * quarter :: 2], order[2 * quarter + 1 :: 2]
    in_hbm = functools.partial(pltpu.with_memory_space_constraint, memory_space=pltpu.HBM)
    kernel = kernel.reshape(width, share, sources)
    packed = pl.pallas_call(
        pack_body,
        out_shape=f32(events_here + 1, SUB, BLOCK),
        in_specs=[HBM_SPEC] * 3,
        out_specs=VMEM_SPEC,
        scratch_shapes=[
            pltpu.VMEM(slip_delta.shape, jnp.float32),
            pltpu.VMEM(block_list.shape, jnp.int32),
            pltpu.SMEM(live_count.shape, jnp.int32),
            pltpu.VMEM((SUB, BLOCK), jnp.float32),
            pltpu.SemaphoreType.DMA((3,)),
        ],
        compiler_params=params(4),
        name="pack",
    )(in_hbm(slip_delta), in_hbm(block_list), in_hbm(live_count))
    held = packed[None]
    step = 2
    while step < height:
        held = jnp.concatenate([held, send_xor(held, "rows", step)], axis=0)
        step *= 2

    blocks_half = blocks_here // 2
    dense = pl.pallas_call(
        functools.partial(densify_body, entries),
        out_shape=f32(width, events_here, blocks_half, BLOCK),
        in_specs=[VMEM_SPEC, VMEM_SPEC, HBM_SPEC],
        out_specs=VMEM_SPEC,
        scratch_shapes=[pltpu.VMEM((events_here, height * entries, BLOCK), jnp.float32)],
        compiler_params=params(8),
        name="densify",
    )(held, send_xor(held, "rows", 1), in_hbm(kernel))
    mine = lax.all_to_all(dense, "cols", 0, 0, tiled=True)

    def call(body, targets, outs, *args):
        return pl.pallas_call(
            functools.partial(body, targets),
            out_shape=outs,
            in_specs=[VMEM_SPEC] * len(args),
            out_specs=jax.tree.map(lambda _: VMEM_SPEC, outs),
            compiler_params=params(8),
            cost_estimate=pl.CostEstimate(
                flops=6 * quarter * share * sources * events,
                bytes_accessed=4 * quarter * share * sources,
                transcendentals=0,
            ),
            name=body.__name__.removesuffix("_body") + "_stress",
        )(*args)

    slips = bf16(2 * events, blocks_half * BLOCK)
    sums = f32(quarter, events, share)
    came = send_xor(mine, "rows", 1)
    own, own_sum = call(own_body, far_send, [slips, sums], mine, kernel)
    other, far_sent = call(other_body, far_send, [slips, sums], came, kernel, own_sum)

    def later(targets):
        return call(both_body, targets, sums, own, other, kernel)

    far_came = send_xor(far_sent, "cols", 1)
    near_came = send_xor(later(near_send), "cols", 1)
    far = later(far_keep) + far_came
    near = later(near_keep) + near_came
    step = 2
    while step < width // 2:
        keep = far.shape[0] // 2
        far = far[:keep] + send_xor(far[keep:], "cols", step)
        near = near[:keep] + send_xor(near[keep:], "cols", step)
        step *= 2
    stress_change = near[0] + send_xor(far[0], "cols", step)
    scale = direct_effect[None, :]
    growth = jnp.expm1(load_rate * time_before / direct_effect)[None, :]
    log_time = jnp.log(scale / load_rate[None, :]) + jnp.log(
        jnp.log1p(jnp.exp(-stress_change / scale) * growth)
    )
    return (stress_change.T, log_time.T)


def solution(mesh):
    in_specs = (
        P("rows", "cols"),
        P("cols", "rows", None),
        P("cols", "rows"),
        P("cols"),
        P(("rows", "cols")),
        P(("rows", "cols")),
        P(("rows", "cols")),
    )
    out_specs = (P(("rows", "cols"), None), P(("rows", "cols"), None))
    return jax.shard_map(
        per_device, mesh=mesh, in_specs=in_specs, out_specs=out_specs, check_vma=False
    )
```

```python
import functools

import jax
import jax.numpy as jnp
from jax import lax
from jax.experimental import pallas as pl
from jax.experimental.pallas import tpu as pltpu
from jax.sharding import PartitionSpec as P

BLOCK = 128
SUB = 8
CHUNK = 256
VMEM_SPEC = pl.BlockSpec(memory_space=pltpu.VMEM)
HBM_SPEC = pl.BlockSpec(memory_space=pltpu.HBM)
MIB = 1024 * 1024
NT = (((1,), (1,)), ((), ()))


def f32(*shape):
    return jax.ShapeDtypeStruct(shape, jnp.float32)


def bf16(*shape):
    return jax.ShapeDtypeStruct(shape, jnp.bfloat16)


def params(mib):
    return pltpu.CompilerParams(vmem_limit_bytes=mib * MIB)


def send_xor(block, axis, k):
    return lax.ppermute(block, axis, [(r, r ^ k) for r in range(lax.axis_size(axis))])


def pack_body(slip_hbm, list_hbm, count_hbm, out_ref, slip_ref, list_ref, count_ref, ids, sems):
    copies = [
        pltpu.make_async_copy(src, dst, sems.at[j])
        for j, (src, dst) in enumerate(((list_hbm, list_ref), (count_hbm, count_ref), (slip_hbm, slip_ref)))
    ]
    for copy in copies:
        copy.start()
    events, entries = list_ref.shape
    row = lax.axis_index("rows")
    entry = lax.broadcasted_iota(jnp.int32, (events, entries), 1) + row * entries
    event = lax.broadcasted_iota(jnp.int32, (events, entries), 0)
    ids[...] = jnp.full(ids.shape, -1.0, jnp.float32)
    for copy in copies:
        copy.wait()
    count = jnp.zeros((events, entries), jnp.int32)
    for e in range(events):
        count = jnp.where(event == e, count_ref[e], count)
    ids[0:events, 0:entries] = jnp.where(entry < count, list_ref[...], -1).astype(jnp.float32)
    out_ref[events] = pltpu.roll(ids[...], row * entries, 1)
    for e in range(events):
        out_ref[e, 0:entries, :] = slip_ref[e]


def densify_body(entries, *refs):
    ins, (_, out_ref, slips) = refs[:-3], refs[-3:]
    events = ins[0].shape[0] - 1
    width, _, blocks, _ = out_ref.shape
    live = len(ins) * entries
    row = lax.axis_index("rows")
    line = lax.broadcasted_iota(jnp.int32, (width * blocks, live), 0)
    number = ((line // blocks * 2 + row % 2) * blocks + line % blocks).astype(jnp.float32)
    for e in range(events):
        ids = jnp.full((1, BLOCK), -1.0, jnp.float32)
        for ref in ins:
            ids = jnp.maximum(ids, ref[events, e : e + 1, :])
        ids = jnp.broadcast_to(ids, (width * blocks, BLOCK))[:, :live]
        onehot = (ids == number).astype(jnp.bfloat16)
        for k, ref in enumerate(ins):
            where = pl.ds(pl.multiple_of((row ^ k) * entries, entries), entries)
            slips[e, where, :] = ref[e, 0:entries, :]
        slip = slips[e]
        total = jnp.zeros((width * blocks, BLOCK), jnp.float32)
        for _ in range(3):
            piece = slip.astype(jnp.bfloat16)
            slip = slip - piece.astype(jnp.float32)
            total = total + jnp.dot(onehot, piece, preferred_element_type=jnp.float32)
        out_ref[:, e] = total.reshape(width, blocks, BLOCK)


def assemble(dense_ref, out_ref):
    events, blocks = out_ref.shape[0] // 2, dense_ref.shape[2]
    flat = dense_ref.reshape(events * blocks, BLOCK)
    for t in range(events // (2 * SUB)):
        for b in range(blocks):
            rows = [flat[pl.ds((2 * t + u) * SUB * blocks + b, SUB, stride=blocks), :] for u in range(2)]
            slip = jnp.concatenate(rows, axis=0)
            hi = slip.astype(jnp.bfloat16)
            lo = (slip - hi.astype(jnp.float32)).astype(jnp.bfloat16)
            where = slice(b * BLOCK, (b + 1) * BLOCK)
            out_ref[2 * t * SUB : 2 * (t + 1) * SUB, where] = hi
            out_ref[events + 2 * t * SUB : events + 2 * (t + 1) * SUB, where] = lo


def stress(k, other, slip_ref, kernel_ref):
    core = lax.axis_index("rows") % 2 ^ other
    events, patches = slip_ref.shape[0] // 2, slip_ref.shape[1]
    rows = kernel_ref.at[lax.axis_index("cols") ^ k]
    both = low = 0.0
    for t in range(0, patches, CHUNK):
        block = rows[:, pl.ds(pl.multiple_of(core * patches + t, CHUNK), CHUNK)]
        hi = block.astype(jnp.bfloat16)
        lo = (block - hi.astype(jnp.float32)).astype(jnp.bfloat16)
        both += lax.dot_general(slip_ref[:, t : t + CHUNK], hi, NT, preferred_element_type=jnp.float32)
        low += lax.dot_general(slip_ref[:events, t : t + CHUNK], lo, NT, preferred_element_type=jnp.float32)
    return both[:events] + both[events:] + low


def own_body(targets, dense_ref, kernel_ref, slip_ref, *out_refs):
    assemble(dense_ref, slip_ref)
    for group, out_ref in zip(targets, out_refs):
        for j, k in enumerate(group):
            out_ref[j] = stress(k, 0, slip_ref, kernel_ref)


def other_body(targets, dense_ref, kernel_ref, sum_ref, slip_ref, out_ref):
    assemble(dense_ref, slip_ref)
    rest_body(targets, slip_ref, kernel_ref, sum_ref, out_ref)


def rest_body(targets, slip_ref, kernel_ref, sum_ref, out_ref):
    for j, k in enumerate(targets):
        out_ref[j] = sum_ref[j] + stress(k, 1, slip_ref, kernel_ref)


def both_body(targets, own_ref, other_ref, kernel_ref, out_ref):
    for j, k in enumerate(targets):
        out_ref[j] = stress(k, 0, own_ref, kernel_ref) + stress(k, 1, other_ref, kernel_ref)


def halving_order(width):
    bits = width.bit_length() - 1
    return [int(f"{k:0{bits}b}"[::-1], 2) for k in range(width)]


def per_device(kernel, slip_delta, block_list, live_count, direct_effect, load_rate, time_before):
    width = lax.axis_size("cols")
    height = lax.axis_size("rows")
    events_here, entries = block_list.shape
    events = events_here * width
    receivers, sources = kernel.shape
    blocks_here = sources // BLOCK

    order = halving_order(width)
    share = receivers // width
    quarter = width // 4
    near_keep, far_keep = order[0 : 2 * quarter : 2], order[1 : 2 * quarter : 2]
    near_send, far_send = order[2 * quarter :: 2], order[2 * quarter + 1 :: 2]
    in_hbm = functools.partial(pltpu.with_memory_space_constraint, memory_space=pltpu.HBM)
    kernel = kernel.reshape(width, share, sources)
    packed = pl.pallas_call(
        pack_body,
        out_shape=f32(events_here + 1, SUB, BLOCK),
        in_specs=[HBM_SPEC] * 3,
        out_specs=VMEM_SPEC,
        scratch_shapes=[
            pltpu.VMEM(slip_delta.shape, jnp.float32),
            pltpu.VMEM(block_list.shape, jnp.int32),
            pltpu.SMEM(live_count.shape, jnp.int32),
            pltpu.VMEM((SUB, BLOCK), jnp.float32),
            pltpu.SemaphoreType.DMA((3,)),
        ],
        compiler_params=params(4),
        name="pack",
    )(in_hbm(slip_delta), in_hbm(block_list), in_hbm(live_count))
    came = {k: send_xor(packed, "rows", k) for k in sorted(range(1, height), key=lambda k: (k < 2, k))}
    blocks_half = blocks_here // 2
    dense = pl.pallas_call(
        functools.partial(densify_body, entries),
        out_shape=f32(width, events_here, blocks_half, BLOCK),
        in_specs=[VMEM_SPEC] * height + [HBM_SPEC],
        out_specs=VMEM_SPEC,
        scratch_shapes=[pltpu.VMEM((events_here, height * entries, BLOCK), jnp.float32)],
        compiler_params=params(8),
        name="densify",
    )(packed, *(came[k] for k in range(1, height)), in_hbm(kernel))
    mine = lax.all_to_all(dense, "cols", 0, 0, tiled=True)

    def call(body, targets, outs, *args):
        return pl.pallas_call(
            functools.partial(body, targets),
            out_shape=outs,
            in_specs=[VMEM_SPEC] * len(args),
            out_specs=jax.tree.map(lambda _: VMEM_SPEC, outs),
            compiler_params=params(8),
            cost_estimate=pl.CostEstimate(
                flops=6 * quarter * share * sources * events,
                bytes_accessed=4 * quarter * share * sources,
                transcendentals=0,
            ),
            name=body.__name__.removesuffix("_body") + "_stress",
        )(*args)

    slips = bf16(2 * events, blocks_half * BLOCK)
    sums = f32(quarter, events, share)
    came = send_xor(mine, "rows", 1)
    own, far_own, near_own = call(own_body, (far_send, near_send), [slips, sums, sums], mine, kernel)
    other, far_sent = call(other_body, far_send, [slips, sums], came, kernel, far_own)

    def later(targets):
        return call(both_body, targets, sums, own, other, kernel)

    far_came = send_xor(far_sent, "cols", 1)
    near_came = send_xor(call(rest_body, near_send, sums, other, kernel, near_own), "cols", 1)
    far = later(far_keep) + far_came
    near = later(near_keep) + near_came
    step = 2
    while step < width // 2:
        keep = far.shape[0] // 2
        far = far[:keep] + send_xor(far[keep:], "cols", step)
        near = near[:keep] + send_xor(near[keep:], "cols", step)
        step *= 2
    stress_change = near[0] + send_xor(far[0], "cols", step)
    scale = direct_effect[None, :]
    growth = jnp.expm1(load_rate * time_before / direct_effect)[None, :]
    log_time = jnp.log(scale / load_rate[None, :]) + jnp.log(
        jnp.log1p(jnp.exp(-stress_change / scale) * growth)
    )
    return (stress_change.T, log_time.T)


def solution(mesh):
    in_specs = (
        P("rows", "cols"),
        P("cols", "rows", None),
        P("cols", "rows"),
        P("cols"),
        P(("rows", "cols")),
        P(("rows", "cols")),
        P(("rows", "cols")),
    )
    out_specs = (P(("rows", "cols"), None), P(("rows", "cols"), None))
    return jax.shard_map(
        per_device, mesh=mesh, in_specs=in_specs, out_specs=out_specs, check_vma=False
    )
```

```python
import functools

import jax
import jax.numpy as jnp
from jax import lax
from jax.experimental import pallas as pl
from jax.experimental.pallas import tpu as pltpu
from jax.sharding import PartitionSpec as P

BLOCK = 128
SUB = 8
CHUNK = 256
ROWS = 256
VMEM_SPEC = pl.BlockSpec(memory_space=pltpu.VMEM)
HBM_SPEC = pl.BlockSpec(memory_space=pltpu.HBM)
MIB = 1024 * 1024
NT = (((1,), (1,)), ((), ()))


def f32(*shape):
    return jax.ShapeDtypeStruct(shape, jnp.float32)


def bf16(*shape):
    return jax.ShapeDtypeStruct(shape, jnp.bfloat16)


def params(mib):
    return pltpu.CompilerParams(vmem_limit_bytes=mib * MIB)


def send_xor(block, axis, k):
    return lax.ppermute(block, axis, [(r, r ^ k) for r in range(lax.axis_size(axis))])


def pack_body(slip_hbm, list_hbm, count_hbm, out_ref, slip_ref, list_ref, count_ref, ids, sems):
    copies = [
        pltpu.make_async_copy(src, dst, sems.at[j])
        for j, (src, dst) in enumerate(((list_hbm, list_ref), (count_hbm, count_ref), (slip_hbm, slip_ref)))
    ]
    for copy in copies:
        copy.start()
    events, entries = list_ref.shape
    row = lax.axis_index("rows")
    entry = lax.broadcasted_iota(jnp.int32, (events, entries), 1) + row * entries
    event = lax.broadcasted_iota(jnp.int32, (events, entries), 0)
    ids[...] = jnp.full(ids.shape, -1.0, jnp.float32)
    for copy in copies:
        copy.wait()
    count = jnp.zeros((events, entries), jnp.int32)
    for e in range(events):
        count = jnp.where(event == e, count_ref[e], count)
    ids[0:events, 0:entries] = jnp.where(entry < count, list_ref[...], -1).astype(jnp.float32)
    out_ref[events] = pltpu.roll(ids[...], row * entries, 1)
    for e in range(events):
        out_ref[e, 0:entries, :] = slip_ref[e]


def densify_body(entries, *refs):
    ins, (_, out_ref, slips) = refs[:-3], refs[-3:]
    events = ins[0].shape[0] - 1
    width, _, blocks, _ = out_ref.shape
    live = len(ins) * entries
    row = lax.axis_index("rows")
    line = lax.broadcasted_iota(jnp.int32, (width * blocks, live), 0)
    number = ((line // blocks * 2 + row % 2) * blocks + line % blocks).astype(jnp.float32)
    for e in range(events):
        ids = jnp.full((1, BLOCK), -1.0, jnp.float32)
        for ref in ins:
            ids = jnp.maximum(ids, ref[events, e : e + 1, :])
        ids = jnp.broadcast_to(ids, (width * blocks, BLOCK))[:, :live]
        onehot = (ids == number).astype(jnp.bfloat16)
        for k, ref in enumerate(ins):
            where = pl.ds(pl.multiple_of((row ^ k) * entries, entries), entries)
            slips[e, where, :] = ref[e, 0:entries, :]
        slip = slips[e]
        total = jnp.zeros((width * blocks, BLOCK), jnp.float32)
        for _ in range(3):
            piece = slip.astype(jnp.bfloat16)
            slip = slip - piece.astype(jnp.float32)
            total = total + jnp.dot(onehot, piece, preferred_element_type=jnp.float32)
        out_ref[:, e] = total.reshape(width, blocks, BLOCK)


def assemble(dense_ref, out_ref):
    events, blocks = out_ref.shape[0] // 2, dense_ref.shape[2]
    flat = dense_ref.reshape(events * blocks, BLOCK)
    for t in range(events // (2 * SUB)):
        for b in range(blocks):
            rows = [flat[pl.ds((2 * t + u) * SUB * blocks + b, SUB, stride=blocks), :] for u in range(2)]
            slip = jnp.concatenate(rows, axis=0)
            hi = slip.astype(jnp.bfloat16)
            lo = (slip - hi.astype(jnp.float32)).astype(jnp.bfloat16)
            where = slice(b * BLOCK, (b + 1) * BLOCK)
            out_ref[2 * t * SUB : 2 * (t + 1) * SUB, where] = hi
            out_ref[events + 2 * t * SUB : events + 2 * (t + 1) * SUB, where] = lo


def stress(other, slip_ref, kernel_ref, add):
    events, patches = slip_ref.shape[0] // 2, slip_ref.shape[1]
    core = lax.axis_index("rows") % 2 ^ other
    for r in range(0, kernel_ref.shape[0], ROWS):
        both = low = 0.0
        for t in range(0, patches, CHUNK):
            block = kernel_ref[r : r + ROWS, pl.ds(pl.multiple_of(core * patches + t, CHUNK), CHUNK)]
            hi = block.astype(jnp.bfloat16)
            lo = (block - hi.astype(jnp.float32)).astype(jnp.bfloat16)
            both += lax.dot_general(slip_ref[:, t : t + CHUNK], hi, NT, preferred_element_type=jnp.float32)
            low += lax.dot_general(slip_ref[:events, t : t + CHUNK], lo, NT, preferred_element_type=jnp.float32)
        add(r, both[:events] + both[events:] + low)


def own_body(dense_ref, kernel_ref, out_ref, slip_ref):
    assemble(dense_ref, slip_ref)

    def add(r, part):
        out_ref[:, r : r + ROWS] = part

    stress(0, slip_ref, kernel_ref, add)


def other_body(dense_ref, kernel_ref, sum_ref, out_ref, slip_ref):
    assemble(dense_ref, slip_ref)
    share = out_ref.shape[2]

    def add(r, part):
        total = sum_ref[:, r : r + ROWS] + part
        for c in range(ROWS // share):
            out_ref[r // share + c] = total[:, c * share : (c + 1) * share]

    stress(1, slip_ref, kernel_ref, add)


def per_device(kernel, slip_delta, block_list, live_count, direct_effect, load_rate, time_before):
    width = lax.axis_size("cols")
    height = lax.axis_size("rows")
    events_here, entries = block_list.shape
    events = events_here * width
    receivers, sources = kernel.shape
    blocks_here = sources // BLOCK

    share = receivers // width
    in_hbm = functools.partial(pltpu.with_memory_space_constraint, memory_space=pltpu.HBM)
    packed = pl.pallas_call(
        pack_body,
        out_shape=f32(events_here + 1, SUB, BLOCK),
        in_specs=[HBM_SPEC] * 3,
        out_specs=VMEM_SPEC,
        scratch_shapes=[
            pltpu.VMEM(slip_delta.shape, jnp.float32),
            pltpu.VMEM(block_list.shape, jnp.int32),
            pltpu.SMEM(live_count.shape, jnp.int32),
            pltpu.VMEM((SUB, BLOCK), jnp.float32),
            pltpu.SemaphoreType.DMA((3,)),
        ],
        compiler_params=params(4),
        name="pack",
    )(in_hbm(slip_delta), in_hbm(block_list), in_hbm(live_count))
    came = {k: send_xor(packed, "rows", k) for k in sorted(range(1, height), key=lambda k: (k < 2, k))}
    blocks_half = blocks_here // 2
    dense = pl.pallas_call(
        functools.partial(densify_body, entries),
        out_shape=f32(width, events_here, blocks_half, BLOCK),
        in_specs=[VMEM_SPEC] * height + [HBM_SPEC],
        out_specs=VMEM_SPEC,
        scratch_shapes=[pltpu.VMEM((events_here, height * entries, BLOCK), jnp.float32)],
        compiler_params=params(8),
        name="densify",
    )(packed, *(came[k] for k in range(1, height)), in_hbm(kernel))
    mine = lax.all_to_all(dense, "cols", 0, 0, tiled=True)

    def stress_call(body, out, *args):
        return pl.pallas_call(
            body,
            out_shape=out,
            in_specs=[VMEM_SPEC] * len(args),
            out_specs=VMEM_SPEC,
            scratch_shapes=[pltpu.VMEM((2 * events, blocks_half * BLOCK), jnp.bfloat16)],
            compiler_params=params(8),
            cost_estimate=pl.CostEstimate(
                flops=3 * receivers * sources * events,
                bytes_accessed=2 * receivers * sources,
                transcendentals=0,
            ),
            name=body.__name__.removesuffix("_body") + "_stress",
        )(*args)

    came = send_xor(mine, "rows", 1)
    partial_sum = stress_call(own_body, f32(events, receivers), mine, kernel)
    partial_sum = stress_call(other_body, f32(width, events, share), came, kernel, partial_sum)
    stress_change = jnp.sum(lax.all_to_all(partial_sum, "cols", 0, 0, tiled=True), axis=0)
    scale = direct_effect[None, :]
    growth = jnp.expm1(load_rate * time_before / direct_effect)[None, :]
    log_time = jnp.log(scale / load_rate[None, :]) + jnp.log(
        jnp.log1p(jnp.exp(-stress_change / scale) * growth)
    )
    return (stress_change.T, log_time.T)


def solution(mesh):
    in_specs = (
        P("rows", "cols"),
        P("cols", "rows", None),
        P("cols", "rows"),
        P("cols"),
        P(("rows", "cols")),
        P(("rows", "cols")),
        P(("rows", "cols")),
    )
    out_specs = (P(("rows", "cols"), None), P(("rows", "cols"), None))
    return jax.shard_map(
        per_device, mesh=mesh, in_specs=in_specs, out_specs=out_specs, check_vma=False
    )
```

```python
import functools

import jax
import jax.numpy as jnp
from jax import lax
from jax.experimental import pallas as pl
from jax.experimental.pallas import tpu as pltpu
from jax.sharding import PartitionSpec as P

BLOCK = 128
SUB = 8
CHUNK = 256
ROWS = 256
VMEM_SPEC = pl.BlockSpec(memory_space=pltpu.VMEM)
HBM_SPEC = pl.BlockSpec(memory_space=pltpu.HBM)
MIB = 1024 * 1024
NT = (((1,), (1,)), ((), ()))


def f32(*shape):
    return jax.ShapeDtypeStruct(shape, jnp.float32)


def bf16(*shape):
    return jax.ShapeDtypeStruct(shape, jnp.bfloat16)


def params(mib):
    return pltpu.CompilerParams(vmem_limit_bytes=mib * MIB)


def send_xor(block, axis, k):
    return lax.ppermute(block, axis, [(r, r ^ k) for r in range(lax.axis_size(axis))])


def pack_body(slip_hbm, list_hbm, count_hbm, out_ref, slip_ref, list_ref, count_ref, ids, sems):
    copies = [
        pltpu.make_async_copy(src, dst, sems.at[j])
        for j, (src, dst) in enumerate(((list_hbm, list_ref), (count_hbm, count_ref), (slip_hbm, slip_ref)))
    ]
    for copy in copies:
        copy.start()
    events, entries = list_ref.shape
    row = lax.axis_index("rows")
    entry = lax.broadcasted_iota(jnp.int32, (events, entries), 1) + row * entries
    event = lax.broadcasted_iota(jnp.int32, (events, entries), 0)
    ids[...] = jnp.full(ids.shape, -1.0, jnp.float32)
    for copy in copies:
        copy.wait()
    count = jnp.zeros((events, entries), jnp.int32)
    for e in range(events):
        count = jnp.where(event == e, count_ref[e], count)
    ids[0:events, 0:entries] = jnp.where(entry < count, list_ref[...], -1).astype(jnp.float32)
    out_ref[events] = pltpu.roll(ids[...], row * entries, 1)
    for e in range(events):
        out_ref[e, 0:entries, :] = slip_ref[e]


def densify_body(entries, *refs):
    ins, (_, out_ref, slips) = refs[:-3], refs[-3:]
    events = ins[0].shape[0] - 1
    width, _, blocks, _ = out_ref.shape
    live = len(ins) * entries
    row = lax.axis_index("rows")
    line = lax.broadcasted_iota(jnp.int32, (width * blocks, live), 0)
    number = ((line // blocks * 2 + row % 2) * blocks + line % blocks).astype(jnp.float32)
    for e in range(events):
        ids = jnp.full((1, BLOCK), -1.0, jnp.float32)
        for ref in ins:
            ids = jnp.maximum(ids, ref[events, e : e + 1, :])
        ids = jnp.broadcast_to(ids, (width * blocks, BLOCK))[:, :live]
        onehot = (ids == number).astype(jnp.bfloat16)
        for k, ref in enumerate(ins):
            where = pl.ds(pl.multiple_of((row ^ k) * entries, entries), entries)
            slips[e, where, :] = ref[e, 0:entries, :]
        slip = slips[e]
        total = jnp.zeros((width * blocks, BLOCK), jnp.float32)
        for _ in range(3):
            piece = slip.astype(jnp.bfloat16)
            slip = slip - piece.astype(jnp.float32)
            total = total + jnp.dot(onehot, piece, preferred_element_type=jnp.float32)
        out_ref[:, e] = total.reshape(width, blocks, BLOCK)


def assemble(dense_ref, out_ref):
    events, blocks = out_ref.shape[0] // 2, dense_ref.shape[2]
    flat = dense_ref.reshape(events * blocks, BLOCK)
    for t in range(events // (2 * SUB)):
        for b in range(blocks):
            rows = [flat[pl.ds((2 * t + u) * SUB * blocks + b, SUB, stride=blocks), :] for u in range(2)]
            slip = jnp.concatenate(rows, axis=0)
            hi = slip.astype(jnp.bfloat16)
            lo = (slip - hi.astype(jnp.float32)).astype(jnp.bfloat16)
            where = slice(b * BLOCK, (b + 1) * BLOCK)
            out_ref[2 * t * SUB : 2 * (t + 1) * SUB, where] = hi
            out_ref[events + 2 * t * SUB : events + 2 * (t + 1) * SUB, where] = lo


def stress(other, slip_ref, kernel_ref, add):
    events, patches = slip_ref.shape[0] // 2, slip_ref.shape[1]
    core = lax.axis_index("rows") % 2 ^ other
    for r in range(0, kernel_ref.shape[0], ROWS):
        both = low = 0.0
        for t in range(0, patches, CHUNK):
            block = kernel_ref[r : r + ROWS, pl.ds(pl.multiple_of(core * patches + t, CHUNK), CHUNK)]
            hi = block.astype(jnp.bfloat16)
            lo = (block - hi.astype(jnp.float32)).astype(jnp.bfloat16)
            both += lax.dot_general(slip_ref[:, t : t + CHUNK], hi, NT, preferred_element_type=jnp.float32)
            low += lax.dot_general(slip_ref[:events, t : t + CHUNK], lo, NT, preferred_element_type=jnp.float32)
        add(r, both[:events] + both[events:] + low)


def own_body(dense_ref, kernel_ref, out_ref, slip_ref):
    assemble(dense_ref, slip_ref)

    def add(r, part):
        out_ref[:, r : r + ROWS] = part

    stress(0, slip_ref, kernel_ref, add)


def other_body(dense_ref, kernel_ref, sum_ref, out_ref, slip_ref):
    assemble(dense_ref, slip_ref)
    share = out_ref.shape[2]

    def add(r, part):
        total = sum_ref[:, r : r + ROWS] + part
        for c in range(ROWS // share):
            out_ref[r // share + c] = total[:, c * share : (c + 1) * share]

    stress(1, slip_ref, kernel_ref, add)


def per_device(kernel, slip_delta, block_list, live_count, direct_effect, load_rate, time_before):
    width = lax.axis_size("cols")
    height = lax.axis_size("rows")
    events_here, entries = block_list.shape
    events = events_here * width
    receivers, sources = kernel.shape
    blocks_here = sources // BLOCK

    share = receivers // width
    in_hbm = functools.partial(pltpu.with_memory_space_constraint, memory_space=pltpu.HBM)
    packed = pl.pallas_call(
        pack_body,
        out_shape=f32(events_here + 1, SUB, BLOCK),
        in_specs=[HBM_SPEC] * 3,
        out_specs=VMEM_SPEC,
        scratch_shapes=[
            pltpu.VMEM(slip_delta.shape, jnp.float32),
            pltpu.VMEM(block_list.shape, jnp.int32),
            pltpu.SMEM(live_count.shape, jnp.int32),
            pltpu.VMEM((SUB, BLOCK), jnp.float32),
            pltpu.SemaphoreType.DMA((3,)),
        ],
        compiler_params=params(4),
        name="pack",
    )(in_hbm(slip_delta), in_hbm(block_list), in_hbm(live_count))
    came = {k: send_xor(packed, "rows", k) for k in sorted(range(1, height), key=lambda k: (k < 2, k))}
    blocks_half = blocks_here // 2
    dense = pl.pallas_call(
        functools.partial(densify_body, entries),
        out_shape=f32(width, events_here, blocks_half, BLOCK),
        in_specs=[VMEM_SPEC] * height + [HBM_SPEC],
        out_specs=VMEM_SPEC,
        scratch_shapes=[pltpu.VMEM((events_here, height * entries, BLOCK), jnp.float32)],
        compiler_params=params(8),
        name="densify",
    )(packed, *(came[k] for k in range(1, height)), in_hbm(kernel))
    mine = lax.all_to_all(dense, "cols", 0, 0, tiled=True)

    def stress_call(body, out, *args):
        return pl.pallas_call(
            body,
            out_shape=out,
            in_specs=[VMEM_SPEC] * len(args),
            out_specs=VMEM_SPEC,
            scratch_shapes=[pltpu.VMEM((2 * events, blocks_half * BLOCK), jnp.bfloat16)],
            compiler_params=params(8),
            cost_estimate=pl.CostEstimate(
                flops=3 * receivers * sources * events,
                bytes_accessed=2 * receivers * sources,
                transcendentals=0,
            ),
            name=body.__name__.removesuffix("_body") + "_stress",
        )(*args)

    came = send_xor(mine, "rows", 1)
    partial_sum = stress_call(own_body, f32(events, receivers), mine, kernel)
    partial_sum = stress_call(other_body, f32(width, events, share), came, kernel, partial_sum)
    scale = direct_effect[None, :]
    growth = jnp.expm1(load_rate * time_before / direct_effect)[None, :]
    base = jnp.log(scale / load_rate[None, :])
    partial_sum, growth, base = lax.optimization_barrier((partial_sum, growth, base))
    stress_change = jnp.sum(lax.all_to_all(partial_sum, "cols", 0, 0, tiled=True), axis=0)
    log_time = base + jnp.log(jnp.log1p(jnp.exp(-stress_change / scale) * growth))
    return (stress_change.T, log_time.T)


def solution(mesh):
    in_specs = (
        P("rows", "cols"),
        P("cols", "rows", None),
        P("cols", "rows"),
        P("cols"),
        P(("rows", "cols")),
        P(("rows", "cols")),
        P(("rows", "cols")),
    )
    out_specs = (P(("rows", "cols"), None), P(("rows", "cols"), None))
    return jax.shard_map(
        per_device, mesh=mesh, in_specs=in_specs, out_specs=out_specs, check_vma=False
    )
```

```python
import functools

import jax
import jax.numpy as jnp
from jax import lax
from jax.experimental import pallas as pl
from jax.experimental.pallas import tpu as pltpu
from jax.sharding import PartitionSpec as P

BLOCK = 128
SUB = 8
CHUNK = 256
VMEM_SPEC = pl.BlockSpec(memory_space=pltpu.VMEM)
HBM_SPEC = pl.BlockSpec(memory_space=pltpu.HBM)
MIB = 1024 * 1024
NT = (((1,), (1,)), ((), ()))


def f32(*shape):
    return jax.ShapeDtypeStruct(shape, jnp.float32)


def bf16(*shape):
    return jax.ShapeDtypeStruct(shape, jnp.bfloat16)


def params(mib):
    return pltpu.CompilerParams(vmem_limit_bytes=mib * MIB)


def send_xor(block, axis, k):
    return lax.ppermute(block, axis, [(r, r ^ k) for r in range(lax.axis_size(axis))])


def pack_body(slip_hbm, list_hbm, count_hbm, out_ref, slip_ref, list_ref, count_ref, ids, sems):
    copies = [
        pltpu.make_async_copy(src, dst, sems.at[j])
        for j, (src, dst) in enumerate(((list_hbm, list_ref), (count_hbm, count_ref), (slip_hbm, slip_ref)))
    ]
    for copy in copies:
        copy.start()
    events, entries = list_ref.shape
    row = lax.axis_index("rows")
    entry = lax.broadcasted_iota(jnp.int32, (events, entries), 1) + row * entries
    event = lax.broadcasted_iota(jnp.int32, (events, entries), 0)
    ids[...] = jnp.full(ids.shape, -1.0, jnp.float32)
    for copy in copies:
        copy.wait()
    count = jnp.zeros((events, entries), jnp.int32)
    for e in range(events):
        count = jnp.where(event == e, count_ref[e], count)
    ids[0:events, 0:entries] = jnp.where(entry < count, list_ref[...], -1).astype(jnp.float32)
    out_ref[events] = pltpu.roll(ids[...], row * entries, 1)
    for e in range(events):
        out_ref[e, 0:entries, :] = slip_ref[e]


def densify_body(entries, *refs):
    ins, (_, out_ref, slips) = refs[:-3], refs[-3:]
    events = ins[0].shape[0] - 1
    width, _, blocks, _ = out_ref.shape
    live = len(ins) * entries
    row = lax.axis_index("rows")
    line = lax.broadcasted_iota(jnp.int32, (width * blocks, live), 0)
    number = ((line // blocks * 2 + row % 2) * blocks + line % blocks).astype(jnp.float32)
    for e in range(events):
        ids = jnp.full((1, BLOCK), -1.0, jnp.float32)
        for ref in ins:
            ids = jnp.maximum(ids, ref[events, e : e + 1, :])
        ids = jnp.broadcast_to(ids, (width * blocks, BLOCK))[:, :live]
        onehot = (ids == number).astype(jnp.bfloat16)
        for k, ref in enumerate(ins):
            where = pl.ds(pl.multiple_of((row ^ k) * entries, entries), entries)
            slips[e, where, :] = ref[e, 0:entries, :]
        slip = slips[e]
        total = jnp.zeros((width * blocks, BLOCK), jnp.float32)
        for _ in range(3):
            piece = slip.astype(jnp.bfloat16)
            slip = slip - piece.astype(jnp.float32)
            total = total + jnp.dot(onehot, piece, preferred_element_type=jnp.float32)
        out_ref[:, e] = total.reshape(width, blocks, BLOCK)


def assemble(dense_ref, out_ref):
    events, blocks = out_ref.shape[0] // 2, dense_ref.shape[2]
    flat = dense_ref.reshape(events * blocks, BLOCK)
    for t in range(events // (2 * SUB)):
        for b in range(blocks):
            rows = [flat[pl.ds((2 * t + u) * SUB * blocks + b, SUB, stride=blocks), :] for u in range(2)]
            slip = jnp.concatenate(rows, axis=0)
            hi = slip.astype(jnp.bfloat16)
            lo = (slip - hi.astype(jnp.float32)).astype(jnp.bfloat16)
            where = slice(b * BLOCK, (b + 1) * BLOCK)
            out_ref[2 * t * SUB : 2 * (t + 1) * SUB, where] = hi
            out_ref[events + 2 * t * SUB : events + 2 * (t + 1) * SUB, where] = lo


def stress(k, other, slip_ref, kernel_ref):
    core = lax.axis_index("rows") % 2 ^ other
    events, patches = slip_ref.shape[0] // 2, slip_ref.shape[1]
    rows = kernel_ref.at[lax.axis_index("cols") ^ k]
    both = low = 0.0
    for t in range(0, patches, CHUNK):
        block = rows[:, pl.ds(pl.multiple_of(core * patches + t, CHUNK), CHUNK)]
        hi = block.astype(jnp.bfloat16)
        lo = (block - hi.astype(jnp.float32)).astype(jnp.bfloat16)
        both += lax.dot_general(slip_ref[:, t : t + CHUNK], hi, NT, preferred_element_type=jnp.float32)
        low += lax.dot_general(slip_ref[:events, t : t + CHUNK], lo, NT, preferred_element_type=jnp.float32)
    return both[:events] + both[events:] + low


def own_body(targets, dense_ref, kernel_ref, slip_ref, *out_refs):
    assemble(dense_ref, slip_ref)
    for group, out_ref in zip(targets, out_refs):
        for j, k in enumerate(group):
            out_ref[j] = stress(k, 0, slip_ref, kernel_ref)


def other_body(targets, dense_ref, kernel_ref, sum_ref, slip_ref, out_ref):
    assemble(dense_ref, slip_ref)
    rest_body(targets, slip_ref, kernel_ref, sum_ref, out_ref)


def rest_body(targets, slip_ref, kernel_ref, sum_ref, out_ref):
    for j, k in enumerate(targets):
        out_ref[j] = sum_ref[j] + stress(k, 1, slip_ref, kernel_ref)


def both_body(targets, own_ref, other_ref, kernel_ref, out_ref):
    for j, k in enumerate(targets):
        out_ref[j] = stress(k, 0, own_ref, kernel_ref) + stress(k, 1, other_ref, kernel_ref)


def halving_order(width):
    bits = width.bit_length() - 1
    return [int(f"{k:0{bits}b}"[::-1], 2) for k in range(width)]


def per_device(kernel, slip_delta, block_list, live_count, direct_effect, load_rate, time_before):
    width = lax.axis_size("cols")
    height = lax.axis_size("rows")
    events_here, entries = block_list.shape
    events = events_here * width
    receivers, sources = kernel.shape
    blocks_here = sources // BLOCK

    order = halving_order(width)
    share = receivers // width
    quarter = width // 4
    near_keep, far_keep = order[0 : 2 * quarter : 2], order[1 : 2 * quarter : 2]
    near_send, far_send = order[2 * quarter :: 2], order[2 * quarter + 1 :: 2]
    in_hbm = functools.partial(pltpu.with_memory_space_constraint, memory_space=pltpu.HBM)
    kernel = kernel.reshape(width, share, sources)
    packed = pl.pallas_call(
        pack_body,
        out_shape=f32(events_here + 1, SUB, BLOCK),
        in_specs=[HBM_SPEC] * 3,
        out_specs=VMEM_SPEC,
        scratch_shapes=[
            pltpu.VMEM(slip_delta.shape, jnp.float32),
            pltpu.VMEM(block_list.shape, jnp.int32),
            pltpu.SMEM(live_count.shape, jnp.int32),
            pltpu.VMEM((SUB, BLOCK), jnp.float32),
            pltpu.SemaphoreType.DMA((3,)),
        ],
        compiler_params=params(4),
        name="pack",
    )(in_hbm(slip_delta), in_hbm(block_list), in_hbm(live_count))
    came = {k: send_xor(packed, "rows", k) for k in sorted(range(1, height), key=lambda k: (k < 2, k))}
    blocks_half = blocks_here // 2
    dense = pl.pallas_call(
        functools.partial(densify_body, entries),
        out_shape=f32(width, events_here, blocks_half, BLOCK),
        in_specs=[VMEM_SPEC] * height + [HBM_SPEC],
        out_specs=VMEM_SPEC,
        scratch_shapes=[pltpu.VMEM((events_here, height * entries, BLOCK), jnp.float32)],
        compiler_params=params(8),
        name="densify",
    )(packed, *(came[k] for k in range(1, height)), in_hbm(kernel))
    mine = lax.all_to_all(dense, "cols", 0, 0, tiled=True)

    def call(body, targets, outs, *args):
        return pl.pallas_call(
            functools.partial(body, targets),
            out_shape=outs,
            in_specs=[VMEM_SPEC] * len(args),
            out_specs=jax.tree.map(lambda _: VMEM_SPEC, outs),
            compiler_params=params(8),
            cost_estimate=pl.CostEstimate(
                flops=6 * quarter * share * sources * events,
                bytes_accessed=4 * quarter * share * sources,
                transcendentals=0,
            ),
            name=body.__name__.removesuffix("_body") + "_stress",
        )(*args)

    slips = bf16(2 * events, blocks_half * BLOCK)
    sums = f32(quarter, events, share)
    came = send_xor(mine, "rows", 1)
    own, far_own, near_own = call(own_body, (far_send, near_send), [slips, sums, sums], mine, kernel)
    other, far_sent = call(other_body, far_send, [slips, sums], came, kernel, far_own)

    def later(targets):
        return call(both_body, targets, sums, own, other, kernel)

    far_came = send_xor(far_sent, "cols", 1)
    near_came = send_xor(call(rest_body, near_send, sums, other, kernel, near_own), "cols", 1)
    far = later(far_keep) + far_came
    near = later(near_keep) + near_came
    parts = [send_xor(far[j], "cols", k) for j, k in reversed(list(enumerate(far_keep)))]
    parts += [send_xor(near[j], "cols", k) for j, k in enumerate(near_keep) if k]
    stress_change = sum(parts, near[0])
    scale = direct_effect[None, :]
    growth = jnp.expm1(load_rate * time_before / direct_effect)[None, :]
    log_time = jnp.log(scale / load_rate[None, :]) + jnp.log(
        jnp.log1p(jnp.exp(-stress_change / scale) * growth)
    )
    return (stress_change.T, log_time.T)


def solution(mesh):
    in_specs = (
        P("rows", "cols"),
        P("cols", "rows", None),
        P("cols", "rows"),
        P("cols"),
        P(("rows", "cols")),
        P(("rows", "cols")),
        P(("rows", "cols")),
    )
    out_specs = (P(("rows", "cols"), None), P(("rows", "cols"), None))
    return jax.shard_map(
        per_device, mesh=mesh, in_specs=in_specs, out_specs=out_specs, check_vma=False
    )
```

```python
import functools

import jax
import jax.numpy as jnp
from jax import lax
from jax.experimental import pallas as pl
from jax.experimental.pallas import tpu as pltpu
from jax.sharding import PartitionSpec as P

BLOCK = 128
SUB = 8
CHUNK = 256
VMEM_SPEC = pl.BlockSpec(memory_space=pltpu.VMEM)
HBM_SPEC = pl.BlockSpec(memory_space=pltpu.HBM)
MIB = 1024 * 1024
NT = (((1,), (1,)), ((), ()))


def f32(*shape):
    return jax.ShapeDtypeStruct(shape, jnp.float32)


def bf16(*shape):
    return jax.ShapeDtypeStruct(shape, jnp.bfloat16)


def params(mib):
    return pltpu.CompilerParams(vmem_limit_bytes=mib * MIB)


def send_xor(block, axis, k):
    return lax.ppermute(block, axis, [(r, r ^ k) for r in range(lax.axis_size(axis))])


def pack_body(slip_hbm, list_hbm, count_hbm, out_ref, list_ref, count_ref, ids, sems):
    events, entries = list_ref.shape
    slips = out_ref.at[pl.ds(0, events), pl.ds(0, entries)]
    copies = [
        pltpu.make_async_copy(src, dst, sems.at[j])
        for j, (src, dst) in enumerate(((list_hbm, list_ref), (count_hbm, count_ref), (slip_hbm, slips)))
    ]
    for copy in copies:
        copy.start()
    row = lax.axis_index("rows")
    entry = lax.broadcasted_iota(jnp.int32, (events, entries), 1) + row * entries
    event = lax.broadcasted_iota(jnp.int32, (events, entries), 0)
    ids[...] = jnp.full(ids.shape, -1.0, jnp.float32)
    for copy in copies[:2]:
        copy.wait()
    count = jnp.zeros((events, entries), jnp.int32)
    for e in range(events):
        count = jnp.where(event == e, count_ref[e], count)
    ids[0:events, 0:entries] = jnp.where(entry < count, list_ref[...], -1).astype(jnp.float32)
    out_ref[events] = pltpu.roll(ids[...], row * entries, 1)
    copies[2].wait()


def densify_body(entries, sources, *refs):
    ins, (_, out_ref, slips) = refs[:-3], refs[-3:]
    events = ins[0].shape[0] - 1
    width, _, blocks, _ = out_ref.shape
    live = len(ins) * entries
    row = lax.axis_index("rows")
    line = lax.broadcasted_iota(jnp.int32, (width * blocks, live), 0)
    number = ((line // blocks * 2 + row % 2) * blocks + line % blocks).astype(jnp.float32)
    for e in range(events):
        ids = jnp.full((1, BLOCK), -1.0, jnp.float32)
        for ref in ins:
            ids = jnp.maximum(ids, ref[events, e : e + 1, :])
        ids = jnp.broadcast_to(ids, (width * blocks, BLOCK))[:, :live]
        onehot = (ids == number).astype(jnp.bfloat16)
        for k, ref in zip(sources, ins):
            where = pl.ds(pl.multiple_of((row ^ k) * entries, entries), entries)
            slips[e, where, :] = ref[e, 0:entries, :]
        slip = slips[e]
        total = jnp.zeros((width * blocks, BLOCK), jnp.float32)
        for _ in range(3):
            piece = slip.astype(jnp.bfloat16)
            slip = slip - piece.astype(jnp.float32)
            total = total + jnp.dot(onehot, piece, preferred_element_type=jnp.float32)
        out_ref[:, e] = total.reshape(width, blocks, BLOCK)


def assemble(dense_ref, out_ref):
    events, blocks = out_ref.shape[0] // 2, dense_ref.shape[2]
    flat = dense_ref.reshape(events * blocks, BLOCK)
    for t in range(events // (2 * SUB)):
        for b in range(blocks):
            rows = [flat[pl.ds((2 * t + u) * SUB * blocks + b, SUB, stride=blocks), :] for u in range(2)]
            slip = jnp.concatenate(rows, axis=0)
            hi = slip.astype(jnp.bfloat16)
            lo = (slip - hi.astype(jnp.float32)).astype(jnp.bfloat16)
            where = slice(b * BLOCK, (b + 1) * BLOCK)
            out_ref[2 * t * SUB : 2 * (t + 1) * SUB, where] = hi
            out_ref[events + 2 * t * SUB : events + 2 * (t + 1) * SUB, where] = lo


def stress(k, other, slip_ref, kernel_ref):
    core = lax.axis_index("rows") % 2 ^ other
    events, patches = slip_ref.shape[0] // 2, slip_ref.shape[1]
    rows = kernel_ref.at[lax.axis_index("cols") ^ k]
    both = low = 0.0
    for t in range(0, patches, CHUNK):
        block = rows[:, pl.ds(pl.multiple_of(core * patches + t, CHUNK), CHUNK)]
        hi = block.astype(jnp.bfloat16)
        lo = (block - hi.astype(jnp.float32)).astype(jnp.bfloat16)
        both += lax.dot_general(slip_ref[:, t : t + CHUNK], hi, NT, preferred_element_type=jnp.float32)
        low += lax.dot_general(slip_ref[:events, t : t + CHUNK], lo, NT, preferred_element_type=jnp.float32)
    return both[:events] + both[events:] + low


def own_body(targets, dense_ref, kernel_ref, slip_ref, *out_refs):
    assemble(dense_ref, slip_ref)
    for group, out_ref in zip(targets, out_refs):
        for j, k in enumerate(group):
            out_ref[j] = stress(k, 0, slip_ref, kernel_ref)


def other_body(targets, dense_ref, kernel_ref, sum_ref, slip_ref, out_ref):
    assemble(dense_ref, slip_ref)
    rest_body(targets, slip_ref, kernel_ref, sum_ref, out_ref)


def rest_body(targets, slip_ref, kernel_ref, sum_ref, out_ref):
    for j, k in enumerate(targets):
        out_ref[j] = sum_ref[j] + stress(k, 1, slip_ref, kernel_ref)


def both_body(targets, own_ref, other_ref, kernel_ref, out_ref):
    for j, k in enumerate(targets):
        out_ref[j] = stress(k, 0, own_ref, kernel_ref) + stress(k, 1, other_ref, kernel_ref)


def halving_order(width):
    bits = width.bit_length() - 1
    return [int(f"{k:0{bits}b}"[::-1], 2) for k in range(width)]


def per_device(kernel, slip_delta, block_list, live_count, direct_effect, load_rate, time_before):
    width = lax.axis_size("cols")
    height = lax.axis_size("rows")
    events_here, entries = block_list.shape
    events = events_here * width
    receivers, sources = kernel.shape
    blocks_here = sources // BLOCK

    order = halving_order(width)
    share = receivers // width
    quarter = width // 4
    near_keep, far_keep = order[0 : 2 * quarter : 2], order[1 : 2 * quarter : 2]
    near_send, far_send = order[2 * quarter :: 2], order[2 * quarter + 1 :: 2]
    in_hbm = functools.partial(pltpu.with_memory_space_constraint, memory_space=pltpu.HBM)
    kernel = kernel.reshape(width, share, sources)
    packed = pl.pallas_call(
        pack_body,
        out_shape=f32(events_here + 1, SUB, BLOCK),
        in_specs=[HBM_SPEC] * 3,
        out_specs=VMEM_SPEC,
        scratch_shapes=[
            pltpu.VMEM(block_list.shape, jnp.int32),
            pltpu.SMEM(live_count.shape, jnp.int32),
            pltpu.VMEM((SUB, BLOCK), jnp.float32),
            pltpu.SemaphoreType.DMA((3,)),
        ],
        compiler_params=params(4),
        name="pack",
    )(in_hbm(slip_delta), in_hbm(block_list), in_hbm(live_count))
    others = sorted(range(1, height), key=lambda k: (k < 2, k))
    came = [send_xor(packed, "rows", k) for k in others]
    blocks_half = blocks_here // 2
    dense = pl.pallas_call(
        functools.partial(densify_body, entries, [0] + others),
        out_shape=f32(width, events_here, blocks_half, BLOCK),
        in_specs=[VMEM_SPEC] * height + [HBM_SPEC],
        out_specs=VMEM_SPEC,
        scratch_shapes=[pltpu.VMEM((events_here, height * entries, BLOCK), jnp.float32)],
        compiler_params=params(8),
        name="densify",
    )(packed, *came, in_hbm(kernel))
    mine = lax.all_to_all(dense, "cols", 0, 0, tiled=True)

    def call(body, targets, outs, *args):
        return pl.pallas_call(
            functools.partial(body, targets),
            out_shape=outs,
            in_specs=[VMEM_SPEC] * len(args),
            out_specs=jax.tree.map(lambda _: VMEM_SPEC, outs),
            compiler_params=params(8),
            cost_estimate=pl.CostEstimate(
                flops=6 * quarter * share * sources * events,
                bytes_accessed=4 * quarter * share * sources,
                transcendentals=0,
            ),
            name=body.__name__.removesuffix("_body") + "_stress",
        )(*args)

    slips = bf16(2 * events, blocks_half * BLOCK)
    sums = f32(quarter, events, share)
    came = send_xor(mine, "rows", 1)
    own, far_own, near_own = call(own_body, (far_send, near_send), [slips, sums, sums], mine, kernel)
    other, far_sent = call(other_body, far_send, [slips, sums], came, kernel, far_own)

    def later(targets):
        return call(both_body, targets, sums, own, other, kernel)

    far_came = send_xor(far_sent, "cols", 1)
    near_came = send_xor(call(rest_body, near_send, sums, other, kernel, near_own), "cols", 1)
    far = later(far_keep) + far_came
    near = later(near_keep) + near_came
    parts = [send_xor(far[j], "cols", k) for j, k in reversed(list(enumerate(far_keep)))]
    parts += [send_xor(near[j], "cols", k) for j, k in enumerate(near_keep) if k]
    stress_change = sum(parts, near[0])
    scale = direct_effect[None, :]
    growth = jnp.expm1(load_rate * time_before / direct_effect)[None, :]
    log_time = jnp.log(scale / load_rate[None, :]) + jnp.log(
        jnp.log1p(jnp.exp(-stress_change / scale) * growth)
    )
    return (stress_change.T, log_time.T)


def solution(mesh):
    in_specs = (
        P("rows", "cols"),
        P("cols", "rows", None),
        P("cols", "rows"),
        P("cols"),
        P(("rows", "cols")),
        P(("rows", "cols")),
        P(("rows", "cols")),
    )
    out_specs = (P(("rows", "cols"), None), P(("rows", "cols"), None))
    return jax.shard_map(
        per_device, mesh=mesh, in_specs=in_specs, out_specs=out_specs, check_vma=False
    )
```

```python
import functools

import jax
import jax.numpy as jnp
from jax import lax
from jax.experimental import pallas as pl
from jax.experimental.pallas import tpu as pltpu
from jax.sharding import PartitionSpec as P

BLOCK = 128
SUB = 8
CHUNK = 256
VMEM_SPEC = pl.BlockSpec(memory_space=pltpu.VMEM)
HBM_SPEC = pl.BlockSpec(memory_space=pltpu.HBM)
MIB = 1024 * 1024
NT = (((1,), (1,)), ((), ()))


def f32(*shape):
    return jax.ShapeDtypeStruct(shape, jnp.float32)


def bf16(*shape):
    return jax.ShapeDtypeStruct(shape, jnp.bfloat16)


def params(mib):
    return pltpu.CompilerParams(vmem_limit_bytes=mib * MIB)


def send_xor(block, axis, k):
    return lax.ppermute(block, axis, [(r, r ^ k) for r in range(lax.axis_size(axis))])


def pack_body(slip_hbm, list_hbm, count_hbm, out_ref, list_ref, count_ref, ids, sems):
    events, entries = list_ref.shape
    slips = out_ref.at[pl.ds(0, events), pl.ds(0, entries)]
    copies = [
        pltpu.make_async_copy(src, dst, sems.at[j])
        for j, (src, dst) in enumerate(((list_hbm, list_ref), (count_hbm, count_ref), (slip_hbm, slips)))
    ]
    for copy in copies:
        copy.start()
    row = lax.axis_index("rows")
    entry = lax.broadcasted_iota(jnp.int32, (events, entries), 1) + row * entries
    event = lax.broadcasted_iota(jnp.int32, (events, entries), 0)
    ids[...] = jnp.full(ids.shape, -1.0, jnp.float32)
    for copy in copies[:2]:
        copy.wait()
    count = jnp.zeros((events, entries), jnp.int32)
    for e in range(events):
        count = jnp.where(event == e, count_ref[e], count)
    ids[0:events, 0:entries] = jnp.where(entry < count, list_ref[...], -1).astype(jnp.float32)
    out_ref[events] = pltpu.roll(ids[...], row * entries, 1)
    copies[2].wait()


def densify_body(entries, sources, *refs):
    ins, (_, out_ref, slips) = refs[:-3], refs[-3:]
    events = ins[0].shape[0] - 1
    width, _, blocks, _ = out_ref.shape
    live = len(ins) * entries
    row = lax.axis_index("rows")
    line = lax.broadcasted_iota(jnp.int32, (width * blocks, live), 0)
    number = ((line // blocks * 2 + row % 2) * blocks + line % blocks).astype(jnp.float32)
    for e in range(events):
        ids = jnp.full((1, BLOCK), -1.0, jnp.float32)
        for ref in ins:
            ids = jnp.maximum(ids, ref[events, e : e + 1, :])
        ids = jnp.broadcast_to(ids, (width * blocks, BLOCK))[:, :live]
        onehot = (ids == number).astype(jnp.bfloat16)
        for k, ref in zip(sources, ins):
            where = pl.ds(pl.multiple_of((row ^ k) * entries, entries), entries)
            slips[e, where, :] = ref[e, 0:entries, :]
        slip = slips[e]
        total = jnp.zeros((width * blocks, BLOCK), jnp.float32)
        for _ in range(3):
            piece = slip.astype(jnp.bfloat16)
            slip = slip - piece.astype(jnp.float32)
            total = total + jnp.dot(onehot, piece, preferred_element_type=jnp.float32)
        out_ref[:, e] = total.reshape(width, blocks, BLOCK)


def assemble(dense_ref, out_ref):
    events, blocks = out_ref.shape[0] // 2, dense_ref.shape[2]
    flat = dense_ref.reshape(events * blocks, BLOCK)
    for t in range(events // (2 * SUB)):
        for b in range(blocks):
            rows = [flat[pl.ds((2 * t + u) * SUB * blocks + b, SUB, stride=blocks), :] for u in range(2)]
            slip = jnp.concatenate(rows, axis=0)
            hi = slip.astype(jnp.bfloat16)
            lo = (slip - hi.astype(jnp.float32)).astype(jnp.bfloat16)
            where = slice(b * BLOCK, (b + 1) * BLOCK)
            out_ref[2 * t * SUB : 2 * (t + 1) * SUB, where] = hi
            out_ref[events + 2 * t * SUB : events + 2 * (t + 1) * SUB, where] = lo


def stress(k, other, slip_ref, kernel_ref):
    core = lax.axis_index("rows") % 2 ^ other
    events, patches = slip_ref.shape[0] // 2, slip_ref.shape[1]
    rows = kernel_ref.at[lax.axis_index("cols") ^ k]
    both = low = 0.0
    for t in range(0, patches, CHUNK):
        block = rows[:, pl.ds(pl.multiple_of(core * patches + t, CHUNK), CHUNK)]
        hi = block.astype(jnp.bfloat16)
        lo = (block - hi.astype(jnp.float32)).astype(jnp.bfloat16)
        both += lax.dot_general(slip_ref[:, t : t + CHUNK], hi, NT, preferred_element_type=jnp.float32)
        low += lax.dot_general(slip_ref[:events, t : t + CHUNK], lo, NT, preferred_element_type=jnp.float32)
    return both[:events] + both[events:] + low


def own_body(targets, dense_ref, kernel_ref, slip_ref, *out_refs):
    assemble(dense_ref, slip_ref)
    for group, out_ref in zip(targets, out_refs):
        for j, k in enumerate(group):
            out_ref[j] = stress(k, 0, slip_ref, kernel_ref)


def other_body(targets, dense_ref, kernel_ref, sum_ref, slip_ref, out_ref):
    assemble(dense_ref, slip_ref)
    rest_body(targets, slip_ref, kernel_ref, sum_ref, out_ref)


def rest_body(targets, slip_ref, kernel_ref, sum_ref, out_ref):
    for j, k in enumerate(targets):
        out_ref[j] = sum_ref[j] + stress(k, 1, slip_ref, kernel_ref)


def halving_order(width):
    bits = width.bit_length() - 1
    return [int(f"{k:0{bits}b}"[::-1], 2) for k in range(width)]


def per_device(kernel, slip_delta, block_list, live_count, direct_effect, load_rate, time_before):
    width = lax.axis_size("cols")
    height = lax.axis_size("rows")
    events_here, entries = block_list.shape
    events = events_here * width
    receivers, sources = kernel.shape
    blocks_here = sources // BLOCK

    order = halving_order(width)
    share = receivers // width
    quarter = width // 4
    near_keep, far_keep = order[0 : 2 * quarter : 2], order[1 : 2 * quarter : 2]
    near_send, far_send = order[2 * quarter :: 2], order[2 * quarter + 1 :: 2]
    in_hbm = functools.partial(pltpu.with_memory_space_constraint, memory_space=pltpu.HBM)
    kernel = kernel.reshape(width, share, sources)
    packed = pl.pallas_call(
        pack_body,
        out_shape=f32(events_here + 1, SUB, BLOCK),
        in_specs=[HBM_SPEC] * 3,
        out_specs=VMEM_SPEC,
        scratch_shapes=[
            pltpu.VMEM(block_list.shape, jnp.int32),
            pltpu.SMEM(live_count.shape, jnp.int32),
            pltpu.VMEM((SUB, BLOCK), jnp.float32),
            pltpu.SemaphoreType.DMA((3,)),
        ],
        compiler_params=params(4),
        name="pack",
    )(in_hbm(slip_delta), in_hbm(block_list), in_hbm(live_count))
    others = sorted(range(1, height), key=lambda k: (k < 2, k))
    came = [send_xor(packed, "rows", k) for k in others]
    blocks_half = blocks_here // 2
    dense = pl.pallas_call(
        functools.partial(densify_body, entries, [0] + others),
        out_shape=f32(width, events_here, blocks_half, BLOCK),
        in_specs=[VMEM_SPEC] * height + [HBM_SPEC],
        out_specs=VMEM_SPEC,
        scratch_shapes=[pltpu.VMEM((events_here, height * entries, BLOCK), jnp.float32)],
        compiler_params=params(8),
        name="densify",
    )(packed, *came, in_hbm(kernel))
    mine = lax.all_to_all(dense, "cols", 0, 0, tiled=True)

    def call(body, targets, outs, *args):
        return pl.pallas_call(
            functools.partial(body, targets),
            out_shape=outs,
            in_specs=[VMEM_SPEC] * len(args),
            out_specs=jax.tree.map(lambda _: VMEM_SPEC, outs),
            compiler_params=params(8),
            cost_estimate=pl.CostEstimate(
                flops=6 * quarter * share * sources * events,
                bytes_accessed=4 * quarter * share * sources,
                transcendentals=0,
            ),
            name=body.__name__.removesuffix("_body") + "_stress",
        )(*args)

    slips = bf16(2 * events, blocks_half * BLOCK)
    sums = f32(quarter, events, share)
    came = send_xor(mine, "rows", 1)
    groups = (far_send, near_send, far_keep, near_keep)
    _, *own_sums = call(own_body, groups, [slips] + [sums] * 4, mine, kernel)
    other, far_sent = call(other_body, far_send, [slips, sums], came, kernel, own_sums[0])

    def rest(g):
        return call(rest_body, groups[g], sums, other, kernel, own_sums[g])

    far_came = send_xor(far_sent, "cols", 1)
    near_came = send_xor(rest(1), "cols", 1)
    far = rest(2) + far_came
    near = rest(3) + near_came
    parts = [send_xor(far[j], "cols", k) for j, k in reversed(list(enumerate(far_keep)))]
    parts += [send_xor(near[j], "cols", k) for j, k in enumerate(near_keep) if k]
    stress_change = sum(parts, near[0])
    scale = direct_effect[None, :]
    growth = jnp.expm1(load_rate * time_before / direct_effect)[None, :]
    log_time = jnp.log(scale / load_rate[None, :]) + jnp.log(
        jnp.log1p(jnp.exp(-stress_change / scale) * growth)
    )
    return (stress_change.T, log_time.T)


def solution(mesh):
    in_specs = (
        P("rows", "cols"),
        P("cols", "rows", None),
        P("cols", "rows"),
        P("cols"),
        P(("rows", "cols")),
        P(("rows", "cols")),
        P(("rows", "cols")),
    )
    out_specs = (P(("rows", "cols"), None), P(("rows", "cols"), None))
    return jax.shard_map(
        per_device, mesh=mesh, in_specs=in_specs, out_specs=out_specs, check_vma=False
    )
```

```python
import functools

import jax
import jax.numpy as jnp
from jax import lax
from jax.experimental import pallas as pl
from jax.experimental.pallas import tpu as pltpu
from jax.sharding import PartitionSpec as P

BLOCK = 128
SUB = 8
CHUNK = 256
VMEM_SPEC = pl.BlockSpec(memory_space=pltpu.VMEM)
HBM_SPEC = pl.BlockSpec(memory_space=pltpu.HBM)
MIB = 1024 * 1024
NT = (((1,), (1,)), ((), ()))


def f32(*shape):
    return jax.ShapeDtypeStruct(shape, jnp.float32)


def bf16(*shape):
    return jax.ShapeDtypeStruct(shape, jnp.bfloat16)


def params(mib):
    return pltpu.CompilerParams(vmem_limit_bytes=mib * MIB)


def send_xor(block, axis, k):
    return lax.ppermute(block, axis, [(r, r ^ k) for r in range(lax.axis_size(axis))])


def pack_body(slip_hbm, list_hbm, count_hbm, out_ref, list_ref, count_ref, ids, sems):
    events, entries = list_ref.shape
    slips = out_ref.at[pl.ds(0, events), pl.ds(0, entries)]
    copies = [
        pltpu.make_async_copy(src, dst, sems.at[j])
        for j, (src, dst) in enumerate(((list_hbm, list_ref), (count_hbm, count_ref), (slip_hbm, slips)))
    ]
    for copy in copies:
        copy.start()
    row = lax.axis_index("rows")
    entry = lax.broadcasted_iota(jnp.int32, (events, entries), 1) + row * entries
    event = lax.broadcasted_iota(jnp.int32, (events, entries), 0)
    ids[...] = jnp.full(ids.shape, -1.0, jnp.float32)
    for copy in copies[:2]:
        copy.wait()
    count = jnp.zeros((events, entries), jnp.int32)
    for e in range(events):
        count = jnp.where(event == e, count_ref[e], count)
    ids[0:events, 0:entries] = jnp.where(entry < count, list_ref[...], -1).astype(jnp.float32)
    out_ref[events] = pltpu.roll(ids[...], row * entries, 1)
    copies[2].wait()


def densify_body(entries, sources, *refs):
    ins, (_, out_ref, slips) = refs[:-3], refs[-3:]
    events = ins[0].shape[0] - 1
    width, _, blocks, _ = out_ref.shape
    live = len(ins) * entries
    row = lax.axis_index("rows")
    line = lax.broadcasted_iota(jnp.int32, (width * blocks, live), 0)
    number = ((line // blocks * 2 + row % 2) * blocks + line % blocks).astype(jnp.float32)
    for e in range(events):
        ids = jnp.full((1, BLOCK), -1.0, jnp.float32)
        for ref in ins:
            ids = jnp.maximum(ids, ref[events, e : e + 1, :])
        ids = jnp.broadcast_to(ids, (width * blocks, BLOCK))[:, :live]
        onehot = (ids == number).astype(jnp.bfloat16)
        for k, ref in zip(sources, ins):
            where = pl.ds(pl.multiple_of((row ^ k) * entries, entries), entries)
            slips[e, where, :] = ref[e, 0:entries, :]
        slip = slips[e]
        total = jnp.zeros((width * blocks, BLOCK), jnp.float32)
        for _ in range(3):
            piece = slip.astype(jnp.bfloat16)
            slip = slip - piece.astype(jnp.float32)
            total = total + jnp.dot(onehot, piece, preferred_element_type=jnp.float32)
        out_ref[:, e] = total.reshape(width, blocks, BLOCK)


def assemble(dense_ref, out_ref):
    events, blocks = out_ref.shape[0] // 2, dense_ref.shape[2]
    flat = dense_ref.reshape(events * blocks, BLOCK)
    for t in range(events // (2 * SUB)):
        for b in range(blocks):
            rows = [flat[pl.ds((2 * t + u) * SUB * blocks + b, SUB, stride=blocks), :] for u in range(2)]
            slip = jnp.concatenate(rows, axis=0)
            hi = slip.astype(jnp.bfloat16)
            lo = (slip - hi.astype(jnp.float32)).astype(jnp.bfloat16)
            where = slice(b * BLOCK, (b + 1) * BLOCK)
            out_ref[2 * t * SUB : 2 * (t + 1) * SUB, where] = hi
            out_ref[events + 2 * t * SUB : events + 2 * (t + 1) * SUB, where] = lo


def stress(k, other, slip_ref, kernel_ref):
    core = lax.axis_index("rows") % 2 ^ other
    events, patches = slip_ref.shape[0] // 2, slip_ref.shape[1]
    rows = kernel_ref.at[lax.axis_index("cols") ^ k]
    both = low = 0.0
    for t in range(0, patches, CHUNK):
        block = rows[:, pl.ds(pl.multiple_of(core * patches + t, CHUNK), CHUNK)]
        hi = block.astype(jnp.bfloat16)
        lo = (block - hi.astype(jnp.float32)).astype(jnp.bfloat16)
        both += lax.dot_general(slip_ref[:, t : t + CHUNK], hi, NT, preferred_element_type=jnp.float32)
        low += lax.dot_general(slip_ref[:events, t : t + CHUNK], lo, NT, preferred_element_type=jnp.float32)
    return both[:events] + both[events:] + low


def own_body(targets, dense_ref, kernel_ref, slip_ref, *out_refs):
    assemble(dense_ref, slip_ref)
    for group, out_ref in zip(targets, out_refs):
        for j, k in enumerate(group):
            out_ref[j] = stress(k, 0, slip_ref, kernel_ref)


def other_body(targets, dense_ref, kernel_ref, sum_ref, slip_ref, out_ref):
    assemble(dense_ref, slip_ref)
    rest_body(targets, slip_ref, kernel_ref, sum_ref, out_ref)


def rest_body(targets, slip_ref, kernel_ref, sum_ref, out_ref):
    for j, k in enumerate(targets):
        out_ref[j] = sum_ref[j] + stress(k, 1, slip_ref, kernel_ref)


def both_body(targets, own_ref, other_ref, kernel_ref, out_ref):
    for j, k in enumerate(targets):
        out_ref[j] = stress(k, 0, own_ref, kernel_ref) + stress(k, 1, other_ref, kernel_ref)


def per_device(kernel, slip_delta, block_list, live_count, direct_effect, load_rate, time_before):
    width = lax.axis_size("cols")
    height = lax.axis_size("rows")
    events_here, entries = block_list.shape
    events = events_here * width
    receivers, sources = kernel.shape
    blocks_here = sources // BLOCK

    share = receivers // width
    far_send, far_keep = [list(range(width // 2 + odd, width, 2)) for odd in (1, 0)]
    near_keep, near_send = [0, 1], list(range(2, width // 2))
    in_hbm = functools.partial(pltpu.with_memory_space_constraint, memory_space=pltpu.HBM)
    kernel = kernel.reshape(width, share, sources)
    packed = pl.pallas_call(
        pack_body,
        out_shape=f32(events_here + 1, SUB, BLOCK),
        in_specs=[HBM_SPEC] * 3,
        out_specs=VMEM_SPEC,
        scratch_shapes=[
            pltpu.VMEM(block_list.shape, jnp.int32),
            pltpu.SMEM(live_count.shape, jnp.int32),
            pltpu.VMEM((SUB, BLOCK), jnp.float32),
            pltpu.SemaphoreType.DMA((3,)),
        ],
        compiler_params=params(4),
        name="pack",
    )(in_hbm(slip_delta), in_hbm(block_list), in_hbm(live_count))
    others = sorted(range(1, height), key=lambda k: (k < 2, k))
    came = [send_xor(packed, "rows", k) for k in others]
    blocks_half = blocks_here // 2
    dense = pl.pallas_call(
        functools.partial(densify_body, entries, [0] + others),
        out_shape=f32(width, events_here, blocks_half, BLOCK),
        in_specs=[VMEM_SPEC] * height + [HBM_SPEC],
        out_specs=VMEM_SPEC,
        scratch_shapes=[pltpu.VMEM((events_here, height * entries, BLOCK), jnp.float32)],
        compiler_params=params(8),
        name="densify",
    )(packed, *came, in_hbm(kernel))
    mine = lax.all_to_all(dense, "cols", 0, 0, tiled=True)

    def call(body, targets, outs, *args):
        return pl.pallas_call(
            functools.partial(body, targets),
            out_shape=outs,
            in_specs=[VMEM_SPEC] * len(args),
            out_specs=jax.tree.map(lambda _: VMEM_SPEC, outs),
            compiler_params=params(8),
            cost_estimate=pl.CostEstimate(
                flops=3 * receivers * sources * events // 2,
                bytes_accessed=receivers * sources,
                transcendentals=0,
            ),
            name=body.__name__.removesuffix("_body") + "_stress",
        )(*args)

    slips = bf16(2 * events, blocks_half * BLOCK)

    def sums(targets):
        return f32(len(targets), events, share)

    came = send_xor(mine, "rows", 1)
    own, far_own, near_own = call(
        own_body, (far_send, near_send), [slips, sums(far_send), sums(near_send)], mine, kernel
    )
    other, far_sent = call(other_body, far_send, [slips, sums(far_send)], came, kernel, far_own)
    near_sent = call(rest_body, near_send, sums(near_send), other, kernel, near_own)

    def later(targets):
        return call(both_body, targets, sums(targets), own, other, kernel)

    far_came = send_xor(far_sent, "cols", 1)
    near_came = [send_xor(near_sent[j : j + 2], "cols", near_send[j]) for j in range(0, len(near_send), 2)]
    far = later(far_keep) + far_came
    near = sum(near_came, later(near_keep))
    parts = [send_xor(far[j], "cols", k) for j, k in reversed(list(enumerate(far_keep)))]
    parts.append(send_xor(near[1], "cols", 1))
    stress_change = sum(parts, near[0])
    scale = direct_effect[None, :]
    growth = jnp.expm1(load_rate * time_before / direct_effect)[None, :]
    log_time = jnp.log(scale / load_rate[None, :]) + jnp.log(
        jnp.log1p(jnp.exp(-stress_change / scale) * growth)
    )
    return (stress_change.T, log_time.T)


def solution(mesh):
    in_specs = (
        P("rows", "cols"),
        P("cols", "rows", None),
        P("cols", "rows"),
        P("cols"),
        P(("rows", "cols")),
        P(("rows", "cols")),
        P(("rows", "cols")),
    )
    out_specs = (P(("rows", "cols"), None), P(("rows", "cols"), None))
    return jax.shard_map(
        per_device, mesh=mesh, in_specs=in_specs, out_specs=out_specs, check_vma=False
    )
```

```python
import functools

import jax
import jax.numpy as jnp
from jax import lax
from jax.experimental import pallas as pl
from jax.experimental.pallas import tpu as pltpu
from jax.sharding import PartitionSpec as P

BLOCK = 128
SUB = 8
CHUNK = 256
VMEM_SPEC = pl.BlockSpec(memory_space=pltpu.VMEM)
HBM_SPEC = pl.BlockSpec(memory_space=pltpu.HBM)
MIB = 1024 * 1024
NT = (((1,), (1,)), ((), ()))


def f32(*shape):
    return jax.ShapeDtypeStruct(shape, jnp.float32)


def bf16(*shape):
    return jax.ShapeDtypeStruct(shape, jnp.bfloat16)


def params(mib):
    return pltpu.CompilerParams(vmem_limit_bytes=mib * MIB)


def send_xor(block, axis, k):
    return lax.ppermute(block, axis, [(r, r ^ k) for r in range(lax.axis_size(axis))])


def pack_body(slip_hbm, list_hbm, count_hbm, out_ref, list_ref, count_ref, ids, sems):
    events, entries = list_ref.shape
    slips = out_ref.at[pl.ds(0, events), pl.ds(0, entries)]
    copies = [
        pltpu.make_async_copy(src, dst, sems.at[j])
        for j, (src, dst) in enumerate(((list_hbm, list_ref), (count_hbm, count_ref), (slip_hbm, slips)))
    ]
    for copy in copies:
        copy.start()
    row = lax.axis_index("rows")
    entry = lax.broadcasted_iota(jnp.int32, (events, entries), 1) + row * entries
    ids[...] = jnp.full(ids.shape, -1.0, jnp.float32)
    for copy in copies[:2]:
        copy.wait()
    counts = jnp.broadcast_to(count_ref[...].reshape(1, events), (events, events))
    diagonal = lax.broadcasted_iota(jnp.int32, counts.shape, 0) == lax.broadcasted_iota(jnp.int32, counts.shape, 1)
    count = jnp.sum(jnp.where(diagonal, counts, 0), axis=1, keepdims=True)
    ids[0:events, 0:entries] = jnp.where(entry < count, list_ref[...], -1).astype(jnp.float32)
    out_ref[events] = pltpu.roll(ids[...], row * entries, 1)
    copies[2].wait()


def densify_body(entries, sources, *refs):
    ins, (_, out_ref, slips) = refs[:-3], refs[-3:]
    events = ins[0].shape[0] - 1
    width, _, blocks, _ = out_ref.shape
    live = len(ins) * entries
    row = lax.axis_index("rows")
    line = lax.broadcasted_iota(jnp.int32, (width * blocks, live), 0)
    number = ((line // blocks * 2 + row % 2) * blocks + line % blocks).astype(jnp.float32)
    for e in range(events):
        ids = jnp.full((1, BLOCK), -1.0, jnp.float32)
        for ref in ins:
            ids = jnp.maximum(ids, ref[events, e : e + 1, :])
        ids = jnp.broadcast_to(ids, (width * blocks, BLOCK))[:, :live]
        onehot = (ids == number).astype(jnp.bfloat16)
        for k, ref in zip(sources, ins):
            where = pl.ds(pl.multiple_of((row ^ k) * entries, entries), entries)
            slips[e, where, :] = ref[e, 0:entries, :]
        slip = slips[e]
        total = jnp.zeros((width * blocks, BLOCK), jnp.float32)
        for _ in range(2):
            piece = slip.astype(jnp.bfloat16)
            slip = slip - piece.astype(jnp.float32)
            total = total + jnp.dot(onehot, piece, preferred_element_type=jnp.float32)
        out_ref[:, e] = total.reshape(width, blocks, BLOCK)


def assemble(dense_ref, out_ref):
    events, blocks = out_ref.shape[0] // 2, dense_ref.shape[2]
    flat = dense_ref.reshape(events * blocks, BLOCK)
    for t in range(events // (2 * SUB)):
        for b in range(blocks):
            rows = [flat[pl.ds((2 * t + u) * SUB * blocks + b, SUB, stride=blocks), :] for u in range(2)]
            slip = jnp.concatenate(rows, axis=0)
            hi = slip.astype(jnp.bfloat16)
            lo = (slip - hi.astype(jnp.float32)).astype(jnp.bfloat16)
            where = slice(b * BLOCK, (b + 1) * BLOCK)
            out_ref[2 * t * SUB : 2 * (t + 1) * SUB, where] = hi
            out_ref[events + 2 * t * SUB : events + 2 * (t + 1) * SUB, where] = lo


def stress(k, other, slip_ref, kernel_ref):
    core = lax.axis_index("rows") % 2 ^ other
    events, patches = slip_ref.shape[0] // 2, slip_ref.shape[1]
    rows = kernel_ref.at[lax.axis_index("cols") ^ k]
    both = low = 0.0
    for t in range(0, patches, CHUNK):
        block = rows[:, pl.ds(pl.multiple_of(core * patches + t, CHUNK), CHUNK)]
        hi = block.astype(jnp.bfloat16)
        lo = (block - hi.astype(jnp.float32)).astype(jnp.bfloat16)
        both += lax.dot_general(slip_ref[:, t : t + CHUNK], hi, NT, preferred_element_type=jnp.float32)
        low += lax.dot_general(slip_ref[:events, t : t + CHUNK], lo, NT, preferred_element_type=jnp.float32)
    return both[:events] + both[events:] + low


def own_body(targets, dense_ref, kernel_ref, slip_ref, *out_refs):
    assemble(dense_ref, slip_ref)
    for group, out_ref in zip(targets, out_refs):
        for j, k in enumerate(group):
            out_ref[j] = stress(k, 0, slip_ref, kernel_ref)


def other_body(targets, dense_ref, kernel_ref, sum_ref, slip_ref, out_ref):
    assemble(dense_ref, slip_ref)
    rest_body(targets, slip_ref, kernel_ref, sum_ref, out_ref)


def rest_body(targets, slip_ref, kernel_ref, sum_ref, out_ref):
    for j, k in enumerate(targets):
        out_ref[j] = sum_ref[j] + stress(k, 1, slip_ref, kernel_ref)


def both_body(targets, own_ref, other_ref, kernel_ref, out_ref):
    for j, k in enumerate(targets):
        out_ref[j] = stress(k, 0, own_ref, kernel_ref) + stress(k, 1, other_ref, kernel_ref)


def per_device(kernel, slip_delta, block_list, live_count, direct_effect, load_rate, time_before):
    width = lax.axis_size("cols")
    height = lax.axis_size("rows")
    events_here, entries = block_list.shape
    events = events_here * width
    receivers, sources = kernel.shape
    blocks_here = sources // BLOCK

    share = receivers // width
    far_send, far_keep = [list(range(width // 2 + odd, width, 2)) for odd in (1, 0)]
    near_keep, near_send = [0, 1], list(range(2, width // 2))
    in_hbm = functools.partial(pltpu.with_memory_space_constraint, memory_space=pltpu.HBM)
    kernel = kernel.reshape(width, share, sources)
    packed = pl.pallas_call(
        pack_body,
        out_shape=f32(events_here + 1, SUB, BLOCK),
        in_specs=[HBM_SPEC] * 3,
        out_specs=VMEM_SPEC,
        scratch_shapes=[
            pltpu.VMEM(block_list.shape, jnp.int32),
            pltpu.VMEM(live_count.shape, jnp.int32),
            pltpu.VMEM((SUB, BLOCK), jnp.float32),
            pltpu.SemaphoreType.DMA((3,)),
        ],
        compiler_params=params(4),
        name="pack",
    )(in_hbm(slip_delta), in_hbm(block_list), in_hbm(live_count))
    others = sorted(range(1, height), key=lambda k: (k < 2, k))
    came = [send_xor(packed, "rows", k) for k in others]
    blocks_half = blocks_here // 2
    dense = pl.pallas_call(
        functools.partial(densify_body, entries, [0] + others),
        out_shape=f32(width, events_here, blocks_half, BLOCK),
        in_specs=[VMEM_SPEC] * height + [HBM_SPEC],
        out_specs=VMEM_SPEC,
        scratch_shapes=[pltpu.VMEM((events_here, height * entries, BLOCK), jnp.float32)],
        compiler_params=params(8),
        name="densify",
    )(packed, *came, in_hbm(kernel))
    mine = lax.all_to_all(dense, "cols", 0, 0, tiled=True)

    def call(body, targets, outs, *args):
        return pl.pallas_call(
            functools.partial(body, targets),
            out_shape=outs,
            in_specs=[VMEM_SPEC] * len(args),
            out_specs=jax.tree.map(lambda _: VMEM_SPEC, outs),
            compiler_params=params(8),
            cost_estimate=pl.CostEstimate(
                flops=3 * receivers * sources * events // 2,
                bytes_accessed=receivers * sources,
                transcendentals=0,
            ),
            name=body.__name__.removesuffix("_body") + "_stress",
        )(*args)

    slips = bf16(2 * events, blocks_half * BLOCK)

    def sums(targets):
        return f32(len(targets), events, share)

    came = send_xor(mine, "rows", 1)
    own, far_own, near_own = call(
        own_body, (far_send, near_send), [slips, sums(far_send), sums(near_send)], mine, kernel
    )
    other, far_sent = call(other_body, far_send, [slips, sums(far_send)], came, kernel, far_own)
    near_sent = call(rest_body, near_send, sums(near_send), other, kernel, near_own)

    def later(targets):
        return call(both_body, targets, sums(targets), own, other, kernel)

    far_came = send_xor(far_sent, "cols", 1)
    near_came = [send_xor(near_sent[j : j + 2], "cols", near_send[j]) for j in range(0, len(near_send), 2)]
    far = later(far_keep) + far_came
    near = sum(near_came, later(near_keep))
    parts = [send_xor(far[j], "cols", k) for j, k in reversed(list(enumerate(far_keep)))]
    parts.append(send_xor(near[1], "cols", 1))
    stress_change = sum(parts, near[0])
    scale = direct_effect[None, :]
    growth = jnp.expm1(load_rate * time_before / direct_effect)[None, :]
    log_time = jnp.log(scale / load_rate[None, :]) + jnp.log(
        jnp.log1p(jnp.exp(-stress_change / scale) * growth)
    )
    return (stress_change.T, log_time.T)


def solution(mesh):
    in_specs = (
        P("rows", "cols"),
        P("cols", "rows", None),
        P("cols", "rows"),
        P("cols"),
        P(("rows", "cols")),
        P(("rows", "cols")),
        P(("rows", "cols")),
    )
    out_specs = (P(("rows", "cols"), None), P(("rows", "cols"), None))
    return jax.shard_map(
        per_device, mesh=mesh, in_specs=in_specs, out_specs=out_specs, check_vma=False
    )
```

```python
import functools

import jax
import jax.numpy as jnp
from jax import lax
from jax.experimental import pallas as pl
from jax.experimental.pallas import tpu as pltpu
from jax.sharding import PartitionSpec as P

BLOCK = 128
SUB = 8
CHUNK = 256
SLOTS = 24
STRIDE = 32
VMEM_SPEC = pl.BlockSpec(memory_space=pltpu.VMEM)
HBM_SPEC = pl.BlockSpec(memory_space=pltpu.HBM)
MIB = 1024 * 1024
NT = (((1,), (1,)), ((), ()))


def f32(*shape):
    return jax.ShapeDtypeStruct(shape, jnp.float32)


def bf16(*shape):
    return jax.ShapeDtypeStruct(shape, jnp.bfloat16)


def params(mib):
    return pltpu.CompilerParams(vmem_limit_bytes=mib * MIB)


def send_xor(block, axis, k):
    return lax.ppermute(block, axis, [(r, r ^ k) for r in range(lax.axis_size(axis))])


def pack_body(slip_hbm, list_hbm, count_hbm, out_ref, list_ref, count_ref, ids, sems):
    events, entries = list_ref.shape
    slips = out_ref.at[pl.ds(0, events), pl.ds(0, entries)]
    copies = [
        pltpu.make_async_copy(src, dst, sems.at[j])
        for j, (src, dst) in enumerate(((list_hbm, list_ref), (count_hbm, count_ref), (slip_hbm, slips)))
    ]
    for copy in copies:
        copy.start()
    row = lax.axis_index("rows")
    entry = lax.broadcasted_iota(jnp.int32, (events, entries), 1) + row * entries
    event = lax.broadcasted_iota(jnp.int32, (events, entries), 0)
    ids[...] = jnp.full(ids.shape, -1.0, jnp.float32)
    for copy in copies[:2]:
        copy.wait()
    count = jnp.zeros((events, entries), jnp.int32)
    for e in range(events):
        count = jnp.where(event == e, count_ref[e], count)
    ids[0:events, 0:entries] = jnp.where(entry < count, list_ref[...], -1).astype(jnp.float32)
    out_ref[events] = pltpu.roll(ids[...], row * entries, 1)
    copies[2].wait()


def place_slips(sources, ins, slips):
    row = lax.axis_index("rows")
    events, entries, _ = slips.shape
    entries //= len(ins)
    for k, ref in zip(sources, ins):
        where = pl.ds(pl.multiple_of((row ^ k) * entries, entries), entries)
        for e in range(events):
            slips[e, where, :] = ref[e, 0:entries, :]


def compact_body(sources, width, blocks, *refs):
    ins, (_, out_ref, left_ref, slips) = refs[:-4], refs[-4:]
    events, live, _ = slips.shape
    place_slips(sources, ins, slips)
    core = lax.axis_index("rows") % 2
    ids = ins[0][events]
    for ref in ins[1:]:
        ids = jnp.maximum(ids, ref[events])
    mine = []
    for h in range(2):
        for c in range(width):
            low = ((2 * c + (core ^ h)) * blocks).astype(jnp.float32)
            mine.append((ids >= low) & (ids < low + blocks))
    rows = 2 * width * SUB
    member = jnp.concatenate([m.astype(jnp.float32) for m in mine], axis=0)
    i, j = (lax.broadcasted_iota(jnp.int32, (BLOCK, BLOCK), d) for d in (0, 1))
    before = jnp.dot(member.astype(jnp.bfloat16), (i < j).astype(jnp.bfloat16), preferred_element_type=jnp.float32)
    count = jnp.dot(member.astype(jnp.bfloat16), jnp.ones((BLOCK, BLOCK), jnp.bfloat16), preferred_element_type=jnp.float32)
    i, j = (lax.broadcasted_iota(jnp.int32, (rows, rows), d) for d in (0, 1))
    earlier = ((i // SUB == j // SUB) & (j % SUB < i % SUB)).astype(jnp.bfloat16)
    offset = jnp.dot(earlier, count.astype(jnp.bfloat16), preferred_element_type=jnp.float32)
    over = jnp.max(offset + count) > SLOTS
    mark = jnp.where(over, 1.0, 0.0)
    rank = jnp.where(member > 0, before + offset, -1.0)
    left = jnp.zeros(ids.shape, jnp.bool_)
    for c in range(width):
        left = left | (rank[c * SUB : (c + 1) * SUB] >= SLOTS)
    left_ref[...] = jnp.where(left, ids, -1.0)

    group = BLOCK // live
    groups = -(-events // group)
    event = lax.broadcasted_iota(jnp.int32, ids.shape, 0)
    code = jnp.maximum(ids, 0.0) - jnp.floor(jnp.maximum(ids, 0.0) / blocks) * blocks + 1.0
    code = code + (event * blocks).astype(jnp.float32)

    def rows_of(tile):
        tile = [pltpu.roll(tile[e : e + 1], (e % group) * live, 1) if e % group else tile[e : e + 1] for e in range(events)]
        lane = lax.broadcasted_iota(jnp.int32, (1, BLOCK), 1) // live
        out = []
        for g in range(groups):
            line = jnp.full((1, BLOCK), -1.0, jnp.float32)
            for e in range(g * group, min((g + 1) * group, events)):
                line = jnp.where(lane == e % group, tile[e], line)
            out.append(line)
        return out

    codes = rows_of(code)
    slot = lax.broadcasted_iota(jnp.int32, (STRIDE, BLOCK), 0).astype(jnp.float32)
    picks = [[] for _ in range(groups)]
    for c in range(width):
        for g, line in enumerate(rows_of(rank[c * SUB : (c + 1) * SUB])):
            line = jnp.where(line < SLOTS, line, -1.0)
            picks[g].append((slot == jnp.broadcast_to(line, slot.shape)).astype(jnp.bfloat16))
    data = numbers = 0.0
    for g in range(groups):
        pick = jnp.concatenate(picks[g], axis=0)
        size = min(group, events - g * group) * live
        slip = slips[g * group : min((g + 1) * group, events)].reshape(size, BLOCK)
        hi = slip.astype(jnp.bfloat16)
        lo = (slip - hi.astype(jnp.float32)).astype(jnp.bfloat16)
        data += jnp.dot(pick[:, :size], hi, preferred_element_type=jnp.float32)
        data += jnp.dot(pick[:, :size], lo, preferred_element_type=jnp.float32)
        line = jnp.broadcast_to(codes[g], (SUB, BLOCK)).astype(jnp.bfloat16)
        numbers += lax.dot_general(line, pick, NT, preferred_element_type=jnp.float32)
    lane = lax.broadcasted_iota(jnp.int32, (SUB, BLOCK), 1)
    for c in range(width):
        out_ref[c, 0:SLOTS, :] = data[c * STRIDE : c * STRIDE + SLOTS]
        start = c * STRIDE // BLOCK * BLOCK
        tile = numbers[:, start : start + BLOCK]
        shift = c * STRIDE - start
        tile = pltpu.roll(tile, BLOCK - shift, 1) if shift else tile
        out_ref[c, SLOTS : SLOTS + SUB, :] = jnp.where(lane < STRIDE, tile, mark)


def expand_body(in_ref, out_ref, mark_ref):
    width, events, blocks, _ = out_ref.shape
    mark = in_ref[0, SLOTS : SLOTS + SUB, :]
    for c in range(width):
        info = in_ref[c, SLOTS : SLOTS + SUB, :]
        mark = jnp.maximum(mark, info)
        numbers = jnp.broadcast_to(info[0:1, :], (events * blocks, BLOCK))[:, :STRIDE]
        place = lax.broadcasted_iota(jnp.int32, numbers.shape, 0).astype(jnp.float32) + 1.0
        pick = (numbers == place).astype(jnp.bfloat16)
        slip = in_ref[c]
        hi = slip.astype(jnp.bfloat16)
        lo = (slip - hi.astype(jnp.float32)).astype(jnp.bfloat16)
        total = jnp.dot(pick, hi, preferred_element_type=jnp.float32)
        total += jnp.dot(pick, lo, preferred_element_type=jnp.float32)
        out_ref[c] = total.reshape(events, blocks, BLOCK)
    mark_ref[...] = mark


def densify_body(sources, *refs):
    ins, (ids_ref, out_ref, slips) = refs[:-3], refs[-3:]
    width, events, blocks, _ = out_ref.shape
    live = slips.shape[1]
    place_slips(sources, ins, slips)
    line = lax.broadcasted_iota(jnp.int32, (width * blocks, live), 0)
    number = ((line // blocks * 2 + lax.axis_index("rows") % 2) * blocks + line % blocks).astype(jnp.float32)
    for e in range(events):
        ids = jnp.broadcast_to(ids_ref[e : e + 1, :], (width * blocks, BLOCK))[:, :live]
        onehot = (ids == number).astype(jnp.bfloat16)
        slip = slips[e]
        hi = slip.astype(jnp.bfloat16)
        lo = (slip - hi.astype(jnp.float32)).astype(jnp.bfloat16)
        total = jnp.dot(onehot, hi, preferred_element_type=jnp.float32)
        total += jnp.dot(onehot, lo, preferred_element_type=jnp.float32)
        out_ref[:, e] = total.reshape(width, blocks, BLOCK)


def assemble(dense_ref, out_ref):
    events, blocks = out_ref.shape[0] // 2, dense_ref.shape[2]
    flat = dense_ref.reshape(events * blocks, BLOCK)
    for t in range(events // (2 * SUB)):
        for b in range(blocks):
            rows = [flat[pl.ds((2 * t + u) * SUB * blocks + b, SUB, stride=blocks), :] for u in range(2)]
            slip = jnp.concatenate(rows, axis=0)
            hi = slip.astype(jnp.bfloat16)
            lo = (slip - hi.astype(jnp.float32)).astype(jnp.bfloat16)
            where = slice(b * BLOCK, (b + 1) * BLOCK)
            out_ref[2 * t * SUB : 2 * (t + 1) * SUB, where] = hi
            out_ref[events + 2 * t * SUB : events + 2 * (t + 1) * SUB, where] = lo


def stress(k, other, slip_ref, kernel_ref):
    core = lax.axis_index("rows") % 2 ^ other
    events, patches = slip_ref.shape[0] // 2, slip_ref.shape[1]
    rows = kernel_ref.at[lax.axis_index("cols") ^ k]
    both = low = 0.0
    for t in range(0, patches, CHUNK):
        block = rows[:, pl.ds(pl.multiple_of(core * patches + t, CHUNK), CHUNK)]
        hi = block.astype(jnp.bfloat16)
        lo = (block - hi.astype(jnp.float32)).astype(jnp.bfloat16)
        both += lax.dot_general(slip_ref[:, t : t + CHUNK], hi, NT, preferred_element_type=jnp.float32)
        low += lax.dot_general(slip_ref[:events, t : t + CHUNK], lo, NT, preferred_element_type=jnp.float32)
    return both[:events] + both[events:] + low


def own_body(targets, dense_ref, kernel_ref, slip_ref, *out_refs):
    assemble(dense_ref, slip_ref)
    for group, out_ref in zip(targets, out_refs):
        for j, k in enumerate(group):
            out_ref[j] = stress(k, 0, slip_ref, kernel_ref)


def other_body(targets, dense_ref, kernel_ref, sum_ref, slip_ref, out_ref):
    assemble(dense_ref, slip_ref)
    rest_body(targets, slip_ref, kernel_ref, sum_ref, out_ref)


def rest_body(targets, slip_ref, kernel_ref, sum_ref, out_ref):
    for j, k in enumerate(targets):
        out_ref[j] = sum_ref[j] + stress(k, 1, slip_ref, kernel_ref)


def both_body(targets, own_ref, other_ref, kernel_ref, out_ref):
    for j, k in enumerate(targets):
        out_ref[j] = stress(k, 0, own_ref, kernel_ref) + stress(k, 1, other_ref, kernel_ref)


def per_device(kernel, slip_delta, block_list, live_count, direct_effect, load_rate, time_before):
    width = lax.axis_size("cols")
    height = lax.axis_size("rows")
    events_here, entries = block_list.shape
    events = events_here * width
    receivers, sources = kernel.shape
    blocks_here = sources // BLOCK

    share = receivers // width
    far_send, far_keep = [list(range(width // 2 + odd, width, 2)) for odd in (1, 0)]
    near_keep, near_send = [0, 1], list(range(2, width // 2))
    in_hbm = functools.partial(pltpu.with_memory_space_constraint, memory_space=pltpu.HBM)
    kernel = kernel.reshape(width, share, sources)
    packed = pl.pallas_call(
        pack_body,
        out_shape=f32(events_here + 1, SUB, BLOCK),
        in_specs=[HBM_SPEC] * 3,
        out_specs=VMEM_SPEC,
        scratch_shapes=[
            pltpu.VMEM(block_list.shape, jnp.int32),
            pltpu.SMEM(live_count.shape, jnp.int32),
            pltpu.VMEM((SUB, BLOCK), jnp.float32),
            pltpu.SemaphoreType.DMA((3,)),
        ],
        compiler_params=params(4),
        name="pack",
    )(in_hbm(slip_delta), in_hbm(block_list), in_hbm(live_count))
    others = sorted(range(1, height), key=lambda k: (k < 2, k))
    came = [send_xor(packed, "rows", k) for k in others]
    blocks_half = blocks_here // 2
    sources_of = [0] + others
    blocks_of = [packed, *came]
    live = height * entries
    slips_held = pltpu.VMEM((events_here, live, BLOCK), jnp.float32)
    message, left = pl.pallas_call(
        functools.partial(compact_body, sources_of, width, blocks_half),
        out_shape=[f32(width, SLOTS + SUB, BLOCK), f32(SUB, BLOCK)],
        in_specs=[VMEM_SPEC] * height + [HBM_SPEC],
        out_specs=[VMEM_SPEC] * 2,
        scratch_shapes=[slips_held],
        compiler_params=params(16),
        name="compact",
    )(*blocks_of, in_hbm(kernel))
    mine, mark = pl.pallas_call(
        expand_body,
        out_shape=[f32(width, events_here, blocks_half, BLOCK), f32(SUB, BLOCK)],
        in_specs=[VMEM_SPEC],
        out_specs=[VMEM_SPEC] * 2,
        compiler_params=params(8),
        name="expand",
    )(lax.all_to_all(message, "cols", 0, 0, tiled=True))

    def all_left(kernel, left, *blocks_of):
        dense = pl.pallas_call(
            functools.partial(densify_body, sources_of),
            out_shape=f32(width, events_here, blocks_half, BLOCK),
            in_specs=[VMEM_SPEC] * (height + 1),
            out_specs=VMEM_SPEC,
            scratch_shapes=[slips_held],
            compiler_params=params(8),
            name="densify",
        )(*blocks_of, left)
        return stress_of(kernel, lax.all_to_all(dense, "cols", 0, 0, tiled=True))

    def call(body, targets, outs, *args):
        return pl.pallas_call(
            functools.partial(body, targets),
            out_shape=outs,
            in_specs=[VMEM_SPEC] * len(args),
            out_specs=jax.tree.map(lambda _: VMEM_SPEC, outs),
            compiler_params=params(24),
            cost_estimate=pl.CostEstimate(
                flops=3 * receivers * sources * events // 2,
                bytes_accessed=receivers * sources,
                transcendentals=0,
            ),
            name=body.__name__.removesuffix("_body") + "_stress",
        )(*args)

    slips = bf16(2 * events, blocks_half * BLOCK)

    def sums(targets):
        return f32(len(targets), events, share)

    def stress_of(kernel, mine):
        came = send_xor(mine, "rows", 1)
        own, far_own, near_own = call(
            own_body, (far_send, near_send), [slips, sums(far_send), sums(near_send)], mine, kernel
        )
        other, far_sent = call(other_body, far_send, [slips, sums(far_send)], came, kernel, far_own)
        near_sent = call(rest_body, near_send, sums(near_send), other, kernel, near_own)

        def later(targets):
            return call(both_body, targets, sums(targets), own, other, kernel)

        far_came = send_xor(far_sent, "cols", 1)
        near_came = [send_xor(near_sent[j : j + 2], "cols", near_send[j]) for j in range(0, len(near_send), 2)]
        far = later(far_keep) + far_came
        near = sum(near_came, later(near_keep))
        parts = [send_xor(far[j], "cols", k) for j, k in reversed(list(enumerate(far_keep)))]
        parts.append(send_xor(near[1], "cols", 1))
        return sum(parts, near[0])

    stress_change = stress_of(kernel, mine)
    stress_change += lax.cond(
        jnp.any(mark[0, STRIDE:] > 0), all_left, lambda *_: jnp.zeros_like(stress_change), kernel, left, *blocks_of
    )
    scale = direct_effect[None, :]
    growth = jnp.expm1(load_rate * time_before / direct_effect)[None, :]
    log_time = jnp.log(scale / load_rate[None, :]) + jnp.log(
        jnp.log1p(jnp.exp(-stress_change / scale) * growth)
    )
    return (stress_change.T, log_time.T)


def solution(mesh):
    in_specs = (
        P("rows", "cols"),
        P("cols", "rows", None),
        P("cols", "rows"),
        P("cols"),
        P(("rows", "cols")),
        P(("rows", "cols")),
        P(("rows", "cols")),
    )
    out_specs = (P(("rows", "cols"), None), P(("rows", "cols"), None))
    return jax.shard_map(
        per_device, mesh=mesh, in_specs=in_specs, out_specs=out_specs, check_vma=False
    )
```

```python
import functools

import jax
import jax.numpy as jnp
from jax import lax
from jax.experimental import pallas as pl
from jax.experimental.pallas import tpu as pltpu
from jax.sharding import PartitionSpec as P

BLOCK = 128
SUB = 8
CHUNK = 256
SLOTS = 24
STRIDE = 32
VMEM_SPEC = pl.BlockSpec(memory_space=pltpu.VMEM)
HBM_SPEC = pl.BlockSpec(memory_space=pltpu.HBM)
MIB = 1024 * 1024
NT = (((1,), (1,)), ((), ()))


def f32(*shape):
    return jax.ShapeDtypeStruct(shape, jnp.float32)


def bf16(*shape):
    return jax.ShapeDtypeStruct(shape, jnp.bfloat16)


def params(mib):
    return pltpu.CompilerParams(vmem_limit_bytes=mib * MIB)


def send_xor(block, axis, k):
    return lax.ppermute(block, axis, [(r, r ^ k) for r in range(lax.axis_size(axis))])


def pack_body(slip_hbm, list_hbm, count_hbm, out_ref, list_ref, count_ref, ids, sems):
    events, entries = list_ref.shape
    slips = out_ref.at[pl.ds(0, events), pl.ds(0, entries)]
    copies = [
        pltpu.make_async_copy(src, dst, sems.at[j])
        for j, (src, dst) in enumerate(((list_hbm, list_ref), (count_hbm, count_ref), (slip_hbm, slips)))
    ]
    for copy in copies:
        copy.start()
    row = lax.axis_index("rows")
    entry = lax.broadcasted_iota(jnp.int32, (events, entries), 1) + row * entries
    event = lax.broadcasted_iota(jnp.int32, (events, entries), 0)
    ids[...] = jnp.full(ids.shape, -1.0, jnp.float32)
    for copy in copies[:2]:
        copy.wait()
    count = jnp.zeros((events, entries), jnp.int32)
    for e in range(events):
        count = jnp.where(event == e, count_ref[e], count)
    ids[0:events, 0:entries] = jnp.where(entry < count, list_ref[...], -1).astype(jnp.float32)
    out_ref[events] = pltpu.roll(ids[...], row * entries, 1)
    copies[2].wait()


def place_slips(sources, ins, slips):
    row = lax.axis_index("rows")
    events, entries, _ = slips.shape
    entries //= len(ins)
    for k, ref in zip(sources, ins):
        where = pl.ds(pl.multiple_of((row ^ k) * entries, entries), entries)
        for e in range(events):
            slips[e, where, :] = ref[e, 0:entries, :]


def compact_body(sources, width, blocks, *refs):
    ins, (_, out_ref, left_ref, slips) = refs[:-4], refs[-4:]
    events, live, _ = slips.shape
    place_slips(sources, ins, slips)
    core = lax.axis_index("rows") % 2
    ids = ins[0][events]
    for ref in ins[1:]:
        ids = jnp.maximum(ids, ref[events])
    mine = []
    for h in range(2):
        for c in range(width):
            low = ((2 * c + (core ^ h)) * blocks).astype(jnp.float32)
            mine.append((ids >= low) & (ids < low + blocks))
    rows = 2 * width * SUB
    member = jnp.concatenate([m.astype(jnp.float32) for m in mine], axis=0)
    i, j = (lax.broadcasted_iota(jnp.int32, (BLOCK, BLOCK), d) for d in (0, 1))
    before = jnp.dot(member.astype(jnp.bfloat16), (i < j).astype(jnp.bfloat16), preferred_element_type=jnp.float32)
    count = jnp.dot(member.astype(jnp.bfloat16), jnp.ones((BLOCK, BLOCK), jnp.bfloat16), preferred_element_type=jnp.float32)
    i, j = (lax.broadcasted_iota(jnp.int32, (rows, rows), d) for d in (0, 1))
    earlier = ((i // SUB == j // SUB) & (j % SUB < i % SUB)).astype(jnp.bfloat16)
    offset = jnp.dot(earlier, count.astype(jnp.bfloat16), preferred_element_type=jnp.float32)
    over = jnp.max(offset + count) > SLOTS
    mark = jnp.where(over, 1.0, 0.0)
    rank = jnp.where(member > 0, before + offset, -1.0)
    left = jnp.zeros(ids.shape, jnp.bool_)
    for c in range(width):
        left = left | (rank[c * SUB : (c + 1) * SUB] >= SLOTS)
    left_ref[...] = jnp.where(left, ids, -1.0)

    group = BLOCK // live
    groups = -(-events // group)
    event = lax.broadcasted_iota(jnp.int32, ids.shape, 0)
    code = jnp.maximum(ids, 0.0) - jnp.floor(jnp.maximum(ids, 0.0) / blocks) * blocks + 1.0
    code = code + (event * blocks).astype(jnp.float32)

    def rows_of(tile):
        tile = [pltpu.roll(tile[e : e + 1], (e % group) * live, 1) if e % group else tile[e : e + 1] for e in range(events)]
        lane = lax.broadcasted_iota(jnp.int32, (1, BLOCK), 1) // live
        out = []
        for g in range(groups):
            line = jnp.full((1, BLOCK), -1.0, jnp.float32)
            for e in range(g * group, min((g + 1) * group, events)):
                line = jnp.where(lane == e % group, tile[e], line)
            out.append(line)
        return out

    codes = rows_of(code)
    slot = lax.broadcasted_iota(jnp.int32, (STRIDE, BLOCK), 0).astype(jnp.float32)
    picks = [[] for _ in range(groups)]
    for c in range(width):
        for g, line in enumerate(rows_of(rank[c * SUB : (c + 1) * SUB])):
            line = jnp.where(line < SLOTS, line, -1.0)
            picks[g].append((slot == jnp.broadcast_to(line, slot.shape)).astype(jnp.bfloat16))
    data = numbers = 0.0
    for g in range(groups):
        pick = jnp.concatenate(picks[g], axis=0)
        size = min(group, events - g * group) * live
        slip = slips[g * group : min((g + 1) * group, events)].reshape(size, BLOCK)
        hi = slip.astype(jnp.bfloat16)
        lo = (slip - hi.astype(jnp.float32)).astype(jnp.bfloat16)
        data += jnp.dot(pick[:, :size], hi, preferred_element_type=jnp.float32)
        data += jnp.dot(pick[:, :size], lo, preferred_element_type=jnp.float32)
        line = jnp.broadcast_to(codes[g], (SUB, BLOCK)).astype(jnp.bfloat16)
        numbers += lax.dot_general(line, pick, NT, preferred_element_type=jnp.float32)
    lane = lax.broadcasted_iota(jnp.int32, (SUB, BLOCK), 1)
    for c in range(width):
        out_ref[c, 0:SLOTS, :] = data[c * STRIDE : c * STRIDE + SLOTS]
        start = c * STRIDE // BLOCK * BLOCK
        tile = numbers[:, start : start + BLOCK]
        shift = c * STRIDE - start
        tile = pltpu.roll(tile, BLOCK - shift, 1) if shift else tile
        out_ref[c, SLOTS : SLOTS + SUB, :] = jnp.where(lane < STRIDE, tile, mark)


def expand_body(in_ref, out_ref, mark_ref):
    width, events, blocks, _ = out_ref.shape
    mark = in_ref[0, SLOTS : SLOTS + SUB, :]
    for c in range(width):
        info = in_ref[c, SLOTS : SLOTS + SUB, :]
        mark = jnp.maximum(mark, info)
        numbers = jnp.broadcast_to(info[0:1, :], (events * blocks, BLOCK))[:, :STRIDE]
        place = lax.broadcasted_iota(jnp.int32, numbers.shape, 0).astype(jnp.float32) + 1.0
        pick = (numbers == place).astype(jnp.bfloat16)
        slip = in_ref[c]
        hi = slip.astype(jnp.bfloat16)
        lo = (slip - hi.astype(jnp.float32)).astype(jnp.bfloat16)
        total = jnp.dot(pick, hi, preferred_element_type=jnp.float32)
        total += jnp.dot(pick, lo, preferred_element_type=jnp.float32)
        out_ref[c] = total.reshape(events, blocks, BLOCK)
    mark_ref[...] = mark


def densify_body(sources, *refs):
    ins, (ids_ref, out_ref, slips) = refs[:-3], refs[-3:]
    width, events, blocks, _ = out_ref.shape
    live = slips.shape[1]
    place_slips(sources, ins, slips)
    line = lax.broadcasted_iota(jnp.int32, (width * blocks, live), 0)
    number = ((line // blocks * 2 + lax.axis_index("rows") % 2) * blocks + line % blocks).astype(jnp.float32)
    for e in range(events):
        ids = jnp.broadcast_to(ids_ref[e : e + 1, :], (width * blocks, BLOCK))[:, :live]
        onehot = (ids == number).astype(jnp.bfloat16)
        slip = slips[e]
        hi = slip.astype(jnp.bfloat16)
        lo = (slip - hi.astype(jnp.float32)).astype(jnp.bfloat16)
        total = jnp.dot(onehot, hi, preferred_element_type=jnp.float32)
        total += jnp.dot(onehot, lo, preferred_element_type=jnp.float32)
        out_ref[:, e] = total.reshape(width, blocks, BLOCK)


def assemble(dense_ref, out_ref):
    events, blocks = out_ref.shape[0] // 2, dense_ref.shape[2]
    flat = dense_ref.reshape(events * blocks, BLOCK)
    for t in range(events // (2 * SUB)):
        for b in range(blocks):
            rows = [flat[pl.ds((2 * t + u) * SUB * blocks + b, SUB, stride=blocks), :] for u in range(2)]
            slip = jnp.concatenate(rows, axis=0)
            hi = slip.astype(jnp.bfloat16)
            lo = (slip - hi.astype(jnp.float32)).astype(jnp.bfloat16)
            where = slice(b * BLOCK, (b + 1) * BLOCK)
            out_ref[2 * t * SUB : 2 * (t + 1) * SUB, where] = hi
            out_ref[events + 2 * t * SUB : events + 2 * (t + 1) * SUB, where] = lo


def stress(k, other, slip_ref, kernel_ref):
    core = lax.axis_index("rows") % 2 ^ other
    events, patches = slip_ref.shape[0] // 2, slip_ref.shape[1]
    rows = kernel_ref.at[lax.axis_index("cols") ^ k]
    both = low = 0.0
    for t in range(0, patches, CHUNK):
        block = rows[:, pl.ds(pl.multiple_of(core * patches + t, CHUNK), CHUNK)]
        hi = block.astype(jnp.bfloat16)
        lo = (block - hi.astype(jnp.float32)).astype(jnp.bfloat16)
        both += lax.dot_general(slip_ref[:, t : t + CHUNK], hi, NT, preferred_element_type=jnp.float32)
        low += lax.dot_general(slip_ref[:events, t : t + CHUNK], lo, NT, preferred_element_type=jnp.float32)
    return both[:events] + both[events:] + low


def own_body(targets, dense_ref, kernel_ref, slip_ref, *out_refs):
    assemble(dense_ref, slip_ref)
    for group, out_ref in zip(targets, out_refs):
        for j, k in enumerate(group):
            out_ref[j] = stress(k, 0, slip_ref, kernel_ref)


def other_body(targets, dense_ref, kernel_ref, sum_ref, slip_ref, out_ref):
    assemble(dense_ref, slip_ref)
    rest_body(targets, slip_ref, kernel_ref, sum_ref, out_ref)


def rest_body(targets, slip_ref, kernel_ref, sum_ref, out_ref):
    for j, k in enumerate(targets):
        out_ref[j] = sum_ref[j] + stress(k, 1, slip_ref, kernel_ref)


def both_body(targets, own_ref, other_ref, kernel_ref, out_ref):
    for j, k in enumerate(targets):
        out_ref[j] = stress(k, 0, own_ref, kernel_ref) + stress(k, 1, other_ref, kernel_ref)


def per_device(kernel, slip_delta, block_list, live_count, direct_effect, load_rate, time_before):
    width = lax.axis_size("cols")
    height = lax.axis_size("rows")
    events_here, entries = block_list.shape
    events = events_here * width
    receivers, sources = kernel.shape
    blocks_here = sources // BLOCK

    share = receivers // width
    far_send, far_keep = [list(range(width // 2 + odd, width, 2)) for odd in (1, 0)]
    near_keep, near_send = [0, 1], list(range(2, width // 2))
    in_hbm = functools.partial(pltpu.with_memory_space_constraint, memory_space=pltpu.HBM)
    kernel = kernel.reshape(width, share, sources)
    packed = pl.pallas_call(
        pack_body,
        out_shape=f32(events_here + 1, SUB, BLOCK),
        in_specs=[HBM_SPEC] * 3,
        out_specs=VMEM_SPEC,
        scratch_shapes=[
            pltpu.VMEM(block_list.shape, jnp.int32),
            pltpu.SMEM(live_count.shape, jnp.int32),
            pltpu.VMEM((SUB, BLOCK), jnp.float32),
            pltpu.SemaphoreType.DMA((3,)),
        ],
        compiler_params=params(4),
        name="pack",
    )(in_hbm(slip_delta), in_hbm(block_list), in_hbm(live_count))
    others = sorted(range(1, height), key=lambda k: (k < 2, k))
    came = [send_xor(packed, "rows", k) for k in others]
    blocks_half = blocks_here // 2
    sources_of = [0] + others
    blocks_of = [packed, *came]
    live = height * entries
    slips_held = pltpu.VMEM((events_here, live, BLOCK), jnp.float32)
    message, left = pl.pallas_call(
        functools.partial(compact_body, sources_of, width, blocks_half),
        out_shape=[f32(width, SLOTS + SUB, BLOCK), f32(SUB, BLOCK)],
        in_specs=[VMEM_SPEC] * height + [HBM_SPEC],
        out_specs=[VMEM_SPEC] * 2,
        scratch_shapes=[slips_held],
        compiler_params=params(16),
        name="compact",
    )(*blocks_of, in_hbm(kernel))
    mine, mark = pl.pallas_call(
        expand_body,
        out_shape=[f32(width, events_here, blocks_half, BLOCK), f32(SUB, BLOCK)],
        in_specs=[VMEM_SPEC],
        out_specs=[VMEM_SPEC] * 2,
        compiler_params=params(8),
        name="expand",
    )(lax.all_to_all(message, "cols", 0, 0, tiled=True))

    def all_left(kernel, left, *blocks_of):
        dense = pl.pallas_call(
            functools.partial(densify_body, sources_of),
            out_shape=f32(width, events_here, blocks_half, BLOCK),
            in_specs=[VMEM_SPEC] * (height + 1),
            out_specs=VMEM_SPEC,
            scratch_shapes=[slips_held],
            compiler_params=params(8),
            name="densify",
        )(*blocks_of, left)
        return sum(stress_of(kernel, lax.all_to_all(dense, "cols", 0, 0, tiled=True)))

    def call(body, targets, outs, *args):
        return pl.pallas_call(
            functools.partial(body, targets),
            out_shape=outs,
            in_specs=[VMEM_SPEC] * len(args),
            out_specs=jax.tree.map(lambda _: VMEM_SPEC, outs),
            compiler_params=params(24),
            cost_estimate=pl.CostEstimate(
                flops=3 * receivers * sources * events // 2,
                bytes_accessed=receivers * sources,
                transcendentals=0,
            ),
            name=body.__name__.removesuffix("_body") + "_stress",
        )(*args)

    slips = bf16(2 * events, blocks_half * BLOCK)

    def sums(targets):
        return f32(len(targets), events, share)

    def stress_of(kernel, mine):
        came = send_xor(mine, "rows", 1)
        own, far_own, near_own = call(
            own_body, (far_send, near_send), [slips, sums(far_send), sums(near_send)], mine, kernel
        )
        other, far_sent = call(other_body, far_send, [slips, sums(far_send)], came, kernel, far_own)
        near_sent = call(rest_body, near_send, sums(near_send), other, kernel, near_own)

        def later(targets):
            return call(both_body, targets, sums(targets), own, other, kernel)

        far_came = send_xor(far_sent, "cols", 1)
        near_came = [send_xor(near_sent[j : j + 2], "cols", near_send[j]) for j in range(0, len(near_send), 2)]
        far = later(far_keep) + far_came
        near = sum(near_came, later(near_keep))
        parts = [send_xor(far[j], "cols", k) for j, k in reversed(list(enumerate(far_keep)))]
        parts.append(send_xor(near[1], "cols", 1))
        return [*parts, near[0]]

    first, *parts = stress_of(kernel, mine)
    first, left, *blocks_of = lax.optimization_barrier((first, left, *blocks_of))
    parts.append(
        lax.cond(jnp.any(mark[0, STRIDE:] > 0), all_left, lambda *_: jnp.zeros_like(first), kernel, left, *blocks_of)
    )
    stress_change = sum(parts, first)
    scale = direct_effect[None, :]
    growth = jnp.expm1(load_rate * time_before / direct_effect)[None, :]
    log_time = jnp.log(scale / load_rate[None, :]) + jnp.log(
        jnp.log1p(jnp.exp(-stress_change / scale) * growth)
    )
    return (stress_change.T, log_time.T)


def solution(mesh):
    in_specs = (
        P("rows", "cols"),
        P("cols", "rows", None),
        P("cols", "rows"),
        P("cols"),
        P(("rows", "cols")),
        P(("rows", "cols")),
        P(("rows", "cols")),
    )
    out_specs = (P(("rows", "cols"), None), P(("rows", "cols"), None))
    return jax.shard_map(
        per_device, mesh=mesh, in_specs=in_specs, out_specs=out_specs, check_vma=False
    )
```

```python
import functools

import jax
import jax.numpy as jnp
from jax import lax
from jax.experimental import pallas as pl
from jax.experimental.pallas import tpu as pltpu
from jax.sharding import PartitionSpec as P

BLOCK = 128
SUB = 8
CHUNK = 256
SLOTS = 24
STRIDE = 32
VMEM_SPEC = pl.BlockSpec(memory_space=pltpu.VMEM)
HBM_SPEC = pl.BlockSpec(memory_space=pltpu.HBM)
MIB = 1024 * 1024
NT = (((1,), (1,)), ((), ()))


def f32(*shape):
    return jax.ShapeDtypeStruct(shape, jnp.float32)


def bf16(*shape):
    return jax.ShapeDtypeStruct(shape, jnp.bfloat16)


def params(mib):
    return pltpu.CompilerParams(vmem_limit_bytes=mib * MIB)


def send_xor(block, axis, k):
    return lax.ppermute(block, axis, [(r, r ^ k) for r in range(lax.axis_size(axis))])


def pack_body(slip_hbm, list_hbm, count_hbm, out_ref, list_ref, count_ref, ids, sems):
    events, entries = list_ref.shape
    slips = out_ref.at[pl.ds(0, events), pl.ds(0, entries)]
    copies = [
        pltpu.make_async_copy(src, dst, sems.at[j])
        for j, (src, dst) in enumerate(((list_hbm, list_ref), (count_hbm, count_ref), (slip_hbm, slips)))
    ]
    for copy in copies:
        copy.start()
    row = lax.axis_index("rows")
    entry = lax.broadcasted_iota(jnp.int32, (events, entries), 1) + row * entries
    event = lax.broadcasted_iota(jnp.int32, (events, entries), 0)
    ids[...] = jnp.full(ids.shape, -1.0, jnp.float32)
    for copy in copies[:2]:
        copy.wait()
    count = jnp.zeros((events, entries), jnp.int32)
    for e in range(events):
        count = jnp.where(event == e, count_ref[e], count)
    ids[0:events, 0:entries] = jnp.where(entry < count, list_ref[...], -1).astype(jnp.float32)
    out_ref[events] = pltpu.roll(ids[...], row * entries, 1)
    copies[2].wait()


def place_slips(sources, ins, slips):
    row = lax.axis_index("rows")
    events, entries, _ = slips.shape
    entries //= len(ins)
    for k, ref in zip(sources, ins):
        where = pl.ds(pl.multiple_of((row ^ k) * entries, entries), entries)
        for e in range(events):
            slips[e, where, :] = ref[e, 0:entries, :]


def compact_body(sources, width, blocks, *refs):
    ins, (_, out_ref, left_ref, slips) = refs[:-4], refs[-4:]
    events, live, _ = slips.shape
    place_slips(sources, ins, slips)
    core = lax.axis_index("rows") % 2
    ids = ins[0][events]
    for ref in ins[1:]:
        ids = jnp.maximum(ids, ref[events])
    mine = []
    for h in range(2):
        for c in range(width):
            low = ((2 * c + (core ^ h)) * blocks).astype(jnp.float32)
            mine.append((ids >= low) & (ids < low + blocks))
    rows = 2 * width * SUB
    member = jnp.concatenate([m.astype(jnp.float32) for m in mine], axis=0)
    i, j = (lax.broadcasted_iota(jnp.int32, (BLOCK, BLOCK), d) for d in (0, 1))
    before = jnp.dot(member.astype(jnp.bfloat16), (i < j).astype(jnp.bfloat16), preferred_element_type=jnp.float32)
    count = jnp.dot(member.astype(jnp.bfloat16), jnp.ones((BLOCK, BLOCK), jnp.bfloat16), preferred_element_type=jnp.float32)
    i, j = (lax.broadcasted_iota(jnp.int32, (rows, rows), d) for d in (0, 1))
    earlier = ((i // SUB == j // SUB) & (j % SUB < i % SUB)).astype(jnp.bfloat16)
    offset = jnp.dot(earlier, count.astype(jnp.bfloat16), preferred_element_type=jnp.float32)
    over = jnp.max(offset + count) > SLOTS
    mark = jnp.where(over, 1.0, 0.0)
    rank = jnp.where(member > 0, before + offset, -1.0)
    left = jnp.zeros(ids.shape, jnp.bool_)
    for c in range(width):
        left = left | (rank[c * SUB : (c + 1) * SUB] >= SLOTS)
    left_ref[...] = jnp.where(left, ids, -1.0)

    group = BLOCK // live
    groups = -(-events // group)
    event = lax.broadcasted_iota(jnp.int32, ids.shape, 0)
    code = jnp.maximum(ids, 0.0) - jnp.floor(jnp.maximum(ids, 0.0) / blocks) * blocks + 1.0
    code = code + (event * blocks).astype(jnp.float32)

    def rows_of(tile):
        tile = [pltpu.roll(tile[e : e + 1], (e % group) * live, 1) if e % group else tile[e : e + 1] for e in range(events)]
        lane = lax.broadcasted_iota(jnp.int32, (1, BLOCK), 1) // live
        out = []
        for g in range(groups):
            line = jnp.full((1, BLOCK), -1.0, jnp.float32)
            for e in range(g * group, min((g + 1) * group, events)):
                line = jnp.where(lane == e % group, tile[e], line)
            out.append(line)
        return out

    codes = rows_of(code)
    slot = lax.broadcasted_iota(jnp.int32, (STRIDE, BLOCK), 0).astype(jnp.float32)
    picks = [[] for _ in range(groups)]
    for c in range(width):
        for g, line in enumerate(rows_of(rank[c * SUB : (c + 1) * SUB])):
            line = jnp.where(line < SLOTS, line, -1.0)
            picks[g].append((slot == jnp.broadcast_to(line, slot.shape)).astype(jnp.bfloat16))
    data = numbers = 0.0
    for g in range(groups):
        pick = jnp.concatenate(picks[g], axis=0)
        size = min(group, events - g * group) * live
        slip = slips[g * group : min((g + 1) * group, events)].reshape(size, BLOCK)
        hi = slip.astype(jnp.bfloat16)
        lo = (slip - hi.astype(jnp.float32)).astype(jnp.bfloat16)
        data += jnp.dot(pick[:, :size], hi, preferred_element_type=jnp.float32)
        data += jnp.dot(pick[:, :size], lo, preferred_element_type=jnp.float32)
        line = jnp.broadcast_to(codes[g], (SUB, BLOCK)).astype(jnp.bfloat16)
        numbers += lax.dot_general(line, pick, NT, preferred_element_type=jnp.float32)
    lane = lax.broadcasted_iota(jnp.int32, (SUB, BLOCK), 1)
    for c in range(width):
        out_ref[c, 0:SLOTS, :] = data[c * STRIDE : c * STRIDE + SLOTS]
        start = c * STRIDE // BLOCK * BLOCK
        tile = numbers[:, start : start + BLOCK]
        shift = c * STRIDE - start
        tile = pltpu.roll(tile, BLOCK - shift, 1) if shift else tile
        out_ref[c, SLOTS : SLOTS + SUB, :] = jnp.where(lane < STRIDE, tile, mark)


def expand_body(in_ref, out_ref, mark_ref):
    width, events, blocks, _ = out_ref.shape
    mark = in_ref[0, SLOTS : SLOTS + SUB, :]
    for c in range(width):
        info = in_ref[c, SLOTS : SLOTS + SUB, :]
        mark = jnp.maximum(mark, info)
        numbers = jnp.broadcast_to(info[0:1, :], (events * blocks, BLOCK))[:, :STRIDE]
        place = lax.broadcasted_iota(jnp.int32, numbers.shape, 0).astype(jnp.float32) + 1.0
        pick = (numbers == place).astype(jnp.bfloat16)
        slip = in_ref[c]
        hi = slip.astype(jnp.bfloat16)
        lo = (slip - hi.astype(jnp.float32)).astype(jnp.bfloat16)
        total = jnp.dot(pick, hi, preferred_element_type=jnp.float32)
        total += jnp.dot(pick, lo, preferred_element_type=jnp.float32)
        out_ref[c] = total.reshape(events, blocks, BLOCK)
    mark_ref[...] = mark


def densify_body(sources, *refs):
    ins, (ids_ref, out_ref, slips) = refs[:-3], refs[-3:]
    width, events, blocks, _ = out_ref.shape
    live = slips.shape[1]
    place_slips(sources, ins, slips)
    line = lax.broadcasted_iota(jnp.int32, (width * blocks, live), 0)
    number = ((line // blocks * 2 + lax.axis_index("rows") % 2) * blocks + line % blocks).astype(jnp.float32)
    for e in range(events):
        ids = jnp.broadcast_to(ids_ref[e : e + 1, :], (width * blocks, BLOCK))[:, :live]
        onehot = (ids == number).astype(jnp.bfloat16)
        slip = slips[e]
        hi = slip.astype(jnp.bfloat16)
        lo = (slip - hi.astype(jnp.float32)).astype(jnp.bfloat16)
        total = jnp.dot(onehot, hi, preferred_element_type=jnp.float32)
        total += jnp.dot(onehot, lo, preferred_element_type=jnp.float32)
        out_ref[:, e] = total.reshape(width, blocks, BLOCK)


def assemble(dense_ref, out_ref):
    events, blocks = out_ref.shape[0] // 2, dense_ref.shape[2]
    flat = dense_ref.reshape(events * blocks, BLOCK)
    for t in range(events // (2 * SUB)):
        for b in range(blocks):
            rows = [flat[pl.ds((2 * t + u) * SUB * blocks + b, SUB, stride=blocks), :] for u in range(2)]
            slip = jnp.concatenate(rows, axis=0)
            hi = slip.astype(jnp.bfloat16)
            lo = (slip - hi.astype(jnp.float32)).astype(jnp.bfloat16)
            where = slice(b * BLOCK, (b + 1) * BLOCK)
            out_ref[2 * t * SUB : 2 * (t + 1) * SUB, where] = hi
            out_ref[events + 2 * t * SUB : events + 2 * (t + 1) * SUB, where] = lo


def stress(k, other, slip_ref, kernel_ref):
    core = lax.axis_index("rows") % 2 ^ other
    events, patches = slip_ref.shape[0] // 2, slip_ref.shape[1]
    rows = kernel_ref.at[lax.axis_index("cols") ^ k]
    both = low = 0.0
    for t in range(0, patches, CHUNK):
        block = rows[:, pl.ds(pl.multiple_of(core * patches + t, CHUNK), CHUNK)]
        hi = block.astype(jnp.bfloat16)
        lo = (block - hi.astype(jnp.float32)).astype(jnp.bfloat16)
        both += lax.dot_general(slip_ref[:, t : t + CHUNK], hi, NT, preferred_element_type=jnp.float32)
        low += lax.dot_general(slip_ref[:events, t : t + CHUNK], lo, NT, preferred_element_type=jnp.float32)
    return both[:events] + both[events:] + low


def own_body(targets, dense_ref, kernel_ref, slip_ref, *out_refs):
    assemble(dense_ref, slip_ref)
    for group, out_ref in zip(targets, out_refs):
        for j, k in enumerate(group):
            out_ref[j] = stress(k, 0, slip_ref, kernel_ref)


def other_body(targets, dense_ref, kernel_ref, sum_ref, slip_ref, out_ref):
    assemble(dense_ref, slip_ref)
    rest_body(targets, slip_ref, kernel_ref, sum_ref, out_ref)


def rest_body(targets, slip_ref, kernel_ref, sum_ref, out_ref):
    for j, k in enumerate(targets):
        out_ref[j] = sum_ref[j] + stress(k, 1, slip_ref, kernel_ref)


def both_body(targets, own_ref, other_ref, kernel_ref, out_ref):
    for j, k in enumerate(targets):
        out_ref[j] = stress(k, 0, own_ref, kernel_ref) + stress(k, 1, other_ref, kernel_ref)


def per_device(kernel, slip_delta, block_list, live_count, direct_effect, load_rate, time_before):
    width = lax.axis_size("cols")
    height = lax.axis_size("rows")
    events_here, entries = block_list.shape
    events = events_here * width
    receivers, sources = kernel.shape
    blocks_here = sources // BLOCK

    share = receivers // width
    far_send, far_keep = [list(range(width // 2 + odd, width, 2)) for odd in (1, 0)]
    near_keep, near_send = [0, 1], list(range(2, width // 2))
    in_hbm = functools.partial(pltpu.with_memory_space_constraint, memory_space=pltpu.HBM)
    kernel = kernel.reshape(width, share, sources)
    packed = pl.pallas_call(
        pack_body,
        out_shape=f32(events_here + 1, SUB, BLOCK),
        in_specs=[HBM_SPEC] * 3,
        out_specs=VMEM_SPEC,
        scratch_shapes=[
            pltpu.VMEM(block_list.shape, jnp.int32),
            pltpu.SMEM(live_count.shape, jnp.int32),
            pltpu.VMEM((SUB, BLOCK), jnp.float32),
            pltpu.SemaphoreType.DMA((3,)),
        ],
        compiler_params=params(4),
        name="pack",
    )(in_hbm(slip_delta), in_hbm(block_list), in_hbm(live_count))
    others = sorted(range(1, height), key=lambda k: (k < 2, k))
    came = [send_xor(packed, "rows", k) for k in others]
    blocks_half = blocks_here // 2
    sources_of = [0] + others
    blocks_of = [packed, *came]
    live = height * entries
    slips_held = pltpu.VMEM((events_here, live, BLOCK), jnp.float32)
    message, left = pl.pallas_call(
        functools.partial(compact_body, sources_of, width, blocks_half),
        out_shape=[f32(width, SLOTS + SUB, BLOCK), f32(SUB, BLOCK)],
        in_specs=[VMEM_SPEC] * height + [HBM_SPEC],
        out_specs=[VMEM_SPEC] * 2,
        scratch_shapes=[slips_held],
        compiler_params=params(16),
        name="compact",
    )(*blocks_of, in_hbm(kernel))
    mine, mark = pl.pallas_call(
        expand_body,
        out_shape=[f32(width, events_here, blocks_half, BLOCK), f32(SUB, BLOCK)],
        in_specs=[VMEM_SPEC],
        out_specs=[VMEM_SPEC] * 2,
        compiler_params=params(8),
        name="expand",
    )(lax.all_to_all(message, "cols", 0, 0, tiled=True))

    def all_left(kernel, left, *blocks_of):
        dense = pl.pallas_call(
            functools.partial(densify_body, sources_of),
            out_shape=f32(width, events_here, blocks_half, BLOCK),
            in_specs=[VMEM_SPEC] * (height + 1),
            out_specs=VMEM_SPEC,
            scratch_shapes=[slips_held],
            compiler_params=params(8),
            name="densify",
        )(*blocks_of, left)
        return sum(stress_of(kernel, lax.all_to_all(dense, "cols", 0, 0, tiled=True)))

    def call(body, targets, outs, *args):
        return pl.pallas_call(
            functools.partial(body, targets),
            out_shape=outs,
            in_specs=[VMEM_SPEC] * len(args),
            out_specs=jax.tree.map(lambda _: VMEM_SPEC, outs),
            compiler_params=params(24),
            cost_estimate=pl.CostEstimate(
                flops=3 * receivers * sources * events // 2,
                bytes_accessed=receivers * sources,
                transcendentals=0,
            ),
            name=body.__name__.removesuffix("_body") + "_stress",
        )(*args)

    slips = bf16(2 * events, blocks_half * BLOCK)

    def sums(targets):
        return f32(len(targets), events, share)

    def stress_of(kernel, mine):
        came = send_xor(mine, "rows", 1)
        own, far_own, near_own = call(
            own_body, (far_send, near_send), [slips, sums(far_send), sums(near_send)], mine, kernel
        )
        other, far_sent = call(other_body, far_send, [slips, sums(far_send)], came, kernel, far_own)
        near_sent = call(rest_body, near_send, sums(near_send), other, kernel, near_own)

        def later(targets):
            return call(both_body, targets, sums(targets), own, other, kernel)

        far_came = send_xor(far_sent, "cols", 1)
        near_came = [send_xor(near_sent[j : j + 2], "cols", near_send[j]) for j in range(0, len(near_send), 2)]
        far = later(far_keep) + far_came
        near = sum(near_came, later(near_keep))
        parts = [send_xor(far[j], "cols", k) for j, k in reversed(list(enumerate(far_keep)))]
        parts.append(send_xor(near[1], "cols", 1))
        return [*parts, near[0]]

    *parts, first, mine_part = stress_of(kernel, mine)
    parts.append(mine_part)
    first, left, *blocks_of = lax.optimization_barrier((first, left, *blocks_of))
    parts.append(
        lax.cond(jnp.any(mark[0, STRIDE:] > 0), all_left, lambda *_: jnp.zeros_like(first), kernel, left, *blocks_of)
    )
    stress_change = sum(parts, first)
    scale = direct_effect[None, :]
    growth = jnp.expm1(load_rate * time_before / direct_effect)[None, :]
    log_time = jnp.log(scale / load_rate[None, :]) + jnp.log(
        jnp.log1p(jnp.exp(-stress_change / scale) * growth)
    )
    return (stress_change.T, log_time.T)


def solution(mesh):
    in_specs = (
        P("rows", "cols"),
        P("cols", "rows", None),
        P("cols", "rows"),
        P("cols"),
        P(("rows", "cols")),
        P(("rows", "cols")),
        P(("rows", "cols")),
    )
    out_specs = (P(("rows", "cols"), None), P(("rows", "cols"), None))
    return jax.shard_map(
        per_device, mesh=mesh, in_specs=in_specs, out_specs=out_specs, check_vma=False
    )
```

```python
import functools

import jax
import jax.numpy as jnp
from jax import lax
from jax.experimental import pallas as pl
from jax.experimental.pallas import tpu as pltpu
from jax.sharding import PartitionSpec as P

BLOCK = 128
SUB = 8
CHUNK = 256
SLOTS = 15
STRIDE = 16
VMEM_SPEC = pl.BlockSpec(memory_space=pltpu.VMEM)
HBM_SPEC = pl.BlockSpec(memory_space=pltpu.HBM)
MIB = 1024 * 1024
NT = (((1,), (1,)), ((), ()))


def f32(*shape):
    return jax.ShapeDtypeStruct(shape, jnp.float32)


def bf16(*shape):
    return jax.ShapeDtypeStruct(shape, jnp.bfloat16)


def params(mib):
    return pltpu.CompilerParams(vmem_limit_bytes=mib * MIB)


def send_xor(block, axis, k):
    return lax.ppermute(block, axis, [(r, r ^ k) for r in range(lax.axis_size(axis))])


def compact_body(
    width, blocks, slip_hbm, list_hbm, count_hbm, _, out_ref, left_ref, list_ref, count_ref, number, sems
):
    events, entries = list_ref.shape
    slips = left_ref.at[pl.ds(0, events), pl.ds(0, entries)]
    copies = [
        pltpu.make_async_copy(src, dst, sems.at[j])
        for j, (src, dst) in enumerate(((list_hbm, list_ref), (count_hbm, count_ref), (slip_hbm, slips)))
    ]
    for copy in copies:
        copy.start()
    row = lax.axis_index("rows")
    entry = lax.broadcasted_iota(jnp.int32, (events, entries), 1) + row * entries
    event = lax.broadcasted_iota(jnp.int32, (events, entries), 0)
    number[...] = jnp.full(number.shape, -1.0, jnp.float32)
    pieces = 2 * width
    rows = pieces * SUB
    i, j = (lax.broadcasted_iota(jnp.int32, (BLOCK, BLOCK), d) for d in (0, 1))
    lanes = jnp.concatenate([i < j, i >= 0], axis=1).astype(jnp.bfloat16)
    i, j = (lax.broadcasted_iota(jnp.int32, (rows, rows), d) for d in (0, 1))
    earlier = ((i // SUB == j // SUB) & (j % SUB < i % SUB)).astype(jnp.bfloat16)
    for copy in copies[:2]:
        copy.wait()
    count = jnp.zeros((events, entries), jnp.int32)
    for e in range(events):
        count = jnp.where(event == e, count_ref[e], count)
    number[0:events, 0:entries] = jnp.where(entry < count, list_ref[...], -1).astype(jnp.float32)
    ids = number[...]
    member = []
    for core in range(2):
        for c in range(width):
            low = float((2 * c + core) * blocks)
            member.append(((ids >= low) & (ids < low + blocks)).astype(jnp.float32))
    member = jnp.concatenate(member, axis=0)
    within = jnp.dot(member.astype(jnp.bfloat16), lanes, preferred_element_type=jnp.float32)
    total = within[:, BLOCK:]
    offset = jnp.dot(earlier, total.astype(jnp.bfloat16), preferred_element_type=jnp.float32)
    mark = jnp.where(jnp.max(offset + total) > SLOTS, 1.0, 0.0)
    rank = jnp.where(member > 0, within[:, :BLOCK] + offset, -1.0)
    left = jnp.zeros(ids.shape, jnp.bool_)
    for p in range(pieces):
        left = left | (rank[p * SUB : (p + 1) * SUB] >= SLOTS)
    left_ref[events] = pltpu.roll(jnp.where(left, ids, -1.0), row * entries, 1)

    lane = lax.broadcasted_iota(jnp.int32, (1, BLOCK), 1) // entries

    def line_of(tile):
        line = jnp.full((1, BLOCK), -1.0, jnp.float32)
        for e in range(events):
            part = pltpu.roll(tile[e : e + 1], e * entries, 1) if e else tile[0:1]
            line = jnp.where(lane == e, part, line)
        return line

    known = jnp.maximum(ids, 0.0)
    code = known - jnp.floor(known / blocks) * blocks + 1.0
    code += (lax.broadcasted_iota(jnp.int32, ids.shape, 0) * blocks).astype(jnp.float32)
    codes = jnp.broadcast_to(line_of(code), (SUB, BLOCK)).astype(jnp.bfloat16)
    slot = lax.broadcasted_iota(jnp.int32, (STRIDE, BLOCK), 0).astype(jnp.float32)
    picks = []
    for p in range(pieces):
        line = line_of(rank[p * SUB : (p + 1) * SUB])
        line = jnp.where(line < SLOTS, line, -1.0)
        picks.append((slot == jnp.broadcast_to(line, slot.shape)).astype(jnp.bfloat16))
    pick = jnp.concatenate(picks, axis=0)
    numbers = lax.dot_general(codes, pick, NT, preferred_element_type=jnp.float32)
    copies[2].wait()
    slip = jnp.concatenate([left_ref[e, 0:entries, :] for e in range(events)], axis=0)
    hi = slip.astype(jnp.bfloat16)
    lo = (slip - hi.astype(jnp.float32)).astype(jnp.bfloat16)
    size = events * entries
    data = jnp.dot(pick[:, :size], hi, preferred_element_type=jnp.float32)
    data += jnp.dot(pick[:, :size], lo, preferred_element_type=jnp.float32)
    last = lax.broadcasted_iota(jnp.int32, (STRIDE, BLOCK), 0) == SLOTS
    lane = lax.broadcasted_iota(jnp.int32, (1, BLOCK), 1)
    for p in range(pieces):
        start = p * STRIDE // BLOCK * BLOCK
        tile = numbers[0:1, start : start + BLOCK]
        shift = p * STRIDE - start
        tile = pltpu.roll(tile, BLOCK - shift, 1) if shift else tile
        tile = jnp.broadcast_to(jnp.where(lane < STRIDE, tile, mark), (STRIDE, BLOCK))
        piece = jnp.where(last, tile, data[p * STRIDE : (p + 1) * STRIDE])
        for other in range(out_ref.shape[0] // pieces):
            out_ref[other * pieces + p] = piece


def expand_body(in_ref, out_ref, mark_ref):
    width, events, blocks, _ = out_ref.shape
    height = in_ref.shape[0] // width
    lane = lax.broadcasted_iota(jnp.int32, (1, BLOCK), 1)
    mark = jnp.zeros((1, BLOCK), jnp.float32)
    for c in range(width):
        numbers = jnp.zeros((1, BLOCK), jnp.float32)
        slip = []
        for r in range(height):
            piece = in_ref[r * width + c]
            info = piece[SLOTS : SLOTS + 1, :]
            mark = jnp.maximum(mark, jnp.where(lane >= STRIDE, info, 0.0))
            info = pltpu.roll(info, r * STRIDE, 1) if r else info
            numbers = jnp.where(lane // STRIDE == r, info, numbers)
            slip.append(piece)
        slip = jnp.concatenate(slip, axis=0)
        numbers = jnp.broadcast_to(numbers, (events * blocks, BLOCK))[:, : height * STRIDE]
        place = lax.broadcasted_iota(jnp.int32, numbers.shape, 0).astype(jnp.float32) + 1.0
        pick = (numbers == place).astype(jnp.bfloat16)
        hi = slip.astype(jnp.bfloat16)
        lo = (slip - hi.astype(jnp.float32)).astype(jnp.bfloat16)
        total = jnp.dot(pick, hi, preferred_element_type=jnp.float32)
        total += jnp.dot(pick, lo, preferred_element_type=jnp.float32)
        out_ref[c] = total.reshape(events, blocks, BLOCK)
    mark_ref[...] = jnp.broadcast_to(mark, mark_ref.shape)


def densify_body(sources, *refs):
    ins, (out_ref, slips) = refs[:-2], refs[-2:]
    width, events, blocks, _ = out_ref.shape
    live = slips.shape[1]
    entries = live // len(ins)
    row = lax.axis_index("rows")
    line = lax.broadcasted_iota(jnp.int32, (width * blocks, live), 0)
    number = ((line // blocks * 2 + row % 2) * blocks + line % blocks).astype(jnp.float32)
    for e in range(events):
        ids = jnp.full((1, BLOCK), -1.0, jnp.float32)
        for k, ref in zip(sources, ins):
            ids = jnp.maximum(ids, ref[events, e : e + 1, :])
            where = pl.ds(pl.multiple_of((row ^ k) * entries, entries), entries)
            slips[e, where, :] = ref[e, 0:entries, :]
        ids = jnp.broadcast_to(ids, (width * blocks, BLOCK))[:, :live]
        onehot = (ids == number).astype(jnp.bfloat16)
        slip = slips[e]
        hi = slip.astype(jnp.bfloat16)
        lo = (slip - hi.astype(jnp.float32)).astype(jnp.bfloat16)
        total = jnp.dot(onehot, hi, preferred_element_type=jnp.float32)
        total += jnp.dot(onehot, lo, preferred_element_type=jnp.float32)
        out_ref[:, e] = total.reshape(width, blocks, BLOCK)


def assemble(dense_ref, out_ref):
    events, blocks = out_ref.shape[0] // 2, dense_ref.shape[2]
    flat = dense_ref.reshape(events * blocks, BLOCK)
    for t in range(events // (2 * SUB)):
        for b in range(blocks):
            rows = [flat[pl.ds((2 * t + u) * SUB * blocks + b, SUB, stride=blocks), :] for u in range(2)]
            slip = jnp.concatenate(rows, axis=0)
            hi = slip.astype(jnp.bfloat16)
            lo = (slip - hi.astype(jnp.float32)).astype(jnp.bfloat16)
            where = slice(b * BLOCK, (b + 1) * BLOCK)
            out_ref[2 * t * SUB : 2 * (t + 1) * SUB, where] = hi
            out_ref[events + 2 * t * SUB : events + 2 * (t + 1) * SUB, where] = lo


def stress(k, other, slip_ref, kernel_ref):
    core = lax.axis_index("rows") % 2 ^ other
    events, patches = slip_ref.shape[0] // 2, slip_ref.shape[1]
    rows = kernel_ref.at[lax.axis_index("cols") ^ k]
    both = low = 0.0
    for t in range(0, patches, CHUNK):
        block = rows[:, pl.ds(pl.multiple_of(core * patches + t, CHUNK), CHUNK)]
        hi = block.astype(jnp.bfloat16)
        lo = (block - hi.astype(jnp.float32)).astype(jnp.bfloat16)
        both += lax.dot_general(slip_ref[:, t : t + CHUNK], hi, NT, preferred_element_type=jnp.float32)
        low += lax.dot_general(slip_ref[:events, t : t + CHUNK], lo, NT, preferred_element_type=jnp.float32)
    return both[:events] + both[events:] + low


def own_body(targets, dense_ref, kernel_ref, slip_ref, *out_refs):
    assemble(dense_ref, slip_ref)
    for group, out_ref in zip(targets, out_refs):
        for j, k in enumerate(group):
            out_ref[j] = stress(k, 0, slip_ref, kernel_ref)


def other_body(targets, dense_ref, kernel_ref, sum_ref, slip_ref, out_ref):
    assemble(dense_ref, slip_ref)
    rest_body(targets, slip_ref, kernel_ref, sum_ref, out_ref)


def rest_body(targets, slip_ref, kernel_ref, sum_ref, out_ref):
    for j, k in enumerate(targets):
        out_ref[j] = sum_ref[j] + stress(k, 1, slip_ref, kernel_ref)


def both_body(targets, own_ref, other_ref, kernel_ref, out_ref):
    for j, k in enumerate(targets):
        out_ref[j] = stress(k, 0, own_ref, kernel_ref) + stress(k, 1, other_ref, kernel_ref)


def per_device(kernel, slip_delta, block_list, live_count, direct_effect, load_rate, time_before):
    width = lax.axis_size("cols")
    height = lax.axis_size("rows")
    events_here, entries = block_list.shape
    events = events_here * width
    receivers, sources = kernel.shape
    blocks_here = sources // BLOCK

    share = receivers // width
    far_send, far_keep = [list(range(width // 2 + odd, width, 2)) for odd in (1, 0)]
    near_keep, near_send = [0, 1], list(range(2, width // 2))
    in_hbm = functools.partial(pltpu.with_memory_space_constraint, memory_space=pltpu.HBM)
    kernel = kernel.reshape(width, share, sources)
    blocks_half = blocks_here // 2
    message, left = pl.pallas_call(
        functools.partial(compact_body, width, blocks_half),
        out_shape=[f32(height * width, STRIDE, BLOCK), f32(events_here + 1, SUB, BLOCK)],
        in_specs=[HBM_SPEC] * 4,
        out_specs=[VMEM_SPEC] * 2,
        scratch_shapes=[
            pltpu.VMEM(block_list.shape, jnp.int32),
            pltpu.SMEM(live_count.shape, jnp.int32),
            pltpu.VMEM((SUB, BLOCK), jnp.float32),
            pltpu.SemaphoreType.DMA((3,)),
        ],
        compiler_params=params(16),
        name="compact",
    )(in_hbm(slip_delta), in_hbm(block_list), in_hbm(live_count), in_hbm(kernel))
    mine, mark = pl.pallas_call(
        expand_body,
        out_shape=[f32(width, events_here, blocks_half, BLOCK), f32(SUB, BLOCK)],
        in_specs=[VMEM_SPEC],
        out_specs=[VMEM_SPEC] * 2,
        compiler_params=params(16),
        name="expand",
    )(lax.all_to_all(message, ("rows", "cols"), 0, 0, tiled=True))

    def all_left(kernel, left):
        others = sorted(range(1, height), key=lambda k: (k < 2, k))
        dense = pl.pallas_call(
            functools.partial(densify_body, [0] + others),
            out_shape=f32(width, events_here, blocks_half, BLOCK),
            in_specs=[VMEM_SPEC] * height,
            out_specs=VMEM_SPEC,
            scratch_shapes=[pltpu.VMEM((events_here, height * entries, BLOCK), jnp.float32)],
            compiler_params=params(8),
            name="densify",
        )(left, *(send_xor(left, "rows", k) for k in others))
        return sum(stress_of(kernel, lax.all_to_all(dense, "cols", 0, 0, tiled=True)))

    def call(body, targets, outs, *args):
        return pl.pallas_call(
            functools.partial(body, targets),
            out_shape=outs,
            in_specs=[VMEM_SPEC] * len(args),
            out_specs=jax.tree.map(lambda _: VMEM_SPEC, outs),
            compiler_params=params(24),
            cost_estimate=pl.CostEstimate(
                flops=3 * receivers * sources * events // 2,
                bytes_accessed=receivers * sources,
                transcendentals=0,
            ),
            name=body.__name__.removesuffix("_body") + "_stress",
        )(*args)

    slips = bf16(2 * events, blocks_half * BLOCK)

    def sums(targets):
        return f32(len(targets), events, share)

    def stress_of(kernel, mine):
        came = send_xor(mine, "rows", 1)
        own, far_own, near_own = call(
            own_body, (far_send, near_send), [slips, sums(far_send), sums(near_send)], mine, kernel
        )
        other, far_sent = call(other_body, far_send, [slips, sums(far_send)], came, kernel, far_own)
        near_sent = call(rest_body, near_send, sums(near_send), other, kernel, near_own)

        def later(targets):
            return call(both_body, targets, sums(targets), own, other, kernel)

        far_came = send_xor(far_sent, "cols", 1)
        near_came = [send_xor(near_sent[j : j + 2], "cols", near_send[j]) for j in range(0, len(near_send), 2)]
        far = later(far_keep) + far_came
        near = sum(near_came, later(near_keep))
        parts = [send_xor(far[j], "cols", k) for j, k in reversed(list(enumerate(far_keep)))]
        parts.append(send_xor(near[1], "cols", 1))
        return [*parts, near[0]]

    *parts, first, mine_part = stress_of(kernel, mine)
    parts.append(mine_part)
    first, left = lax.optimization_barrier((first, left))
    parts.append(lax.cond(jnp.any(mark[0, STRIDE:] > 0), all_left, lambda *_: jnp.zeros_like(first), kernel, left))
    stress_change = sum(parts, first)
    scale = direct_effect[None, :]
    growth = jnp.expm1(load_rate * time_before / direct_effect)[None, :]
    log_time = jnp.log(scale / load_rate[None, :]) + jnp.log(
        jnp.log1p(jnp.exp(-stress_change / scale) * growth)
    )
    return (stress_change.T, log_time.T)


def solution(mesh):
    in_specs = (
        P("rows", "cols"),
        P("cols", "rows", None),
        P("cols", "rows"),
        P("cols"),
        P(("rows", "cols")),
        P(("rows", "cols")),
        P(("rows", "cols")),
    )
    out_specs = (P(("rows", "cols"), None), P(("rows", "cols"), None))
    return jax.shard_map(
        per_device, mesh=mesh, in_specs=in_specs, out_specs=out_specs, check_vma=False
    )
```

```python
import functools

import jax
import jax.numpy as jnp
from jax import lax
from jax.experimental import pallas as pl
from jax.experimental.pallas import tpu as pltpu
from jax.sharding import PartitionSpec as P

BLOCK = 128
SUB = 8
CHUNK = 256
SLOTS = 15
STRIDE = 16
VMEM_SPEC = pl.BlockSpec(memory_space=pltpu.VMEM)
HBM_SPEC = pl.BlockSpec(memory_space=pltpu.HBM)
MIB = 1024 * 1024
NT = (((1,), (1,)), ((), ()))


def f32(*shape):
    return jax.ShapeDtypeStruct(shape, jnp.float32)


def bf16(*shape):
    return jax.ShapeDtypeStruct(shape, jnp.bfloat16)


def params(mib):
    return pltpu.CompilerParams(vmem_limit_bytes=mib * MIB)


def send_xor(block, axis, k):
    return lax.ppermute(block, axis, [(r, r ^ k) for r in range(lax.axis_size(axis))])


def compact_body(
    width, blocks, slip_hbm, list_hbm, count_hbm, _, out_ref, left_ref, list_ref, count_ref, number, sems
):
    events, entries = list_ref.shape
    slips = left_ref.at[pl.ds(0, events), pl.ds(0, entries)]
    copies = [
        pltpu.make_async_copy(src, dst, sems.at[j])
        for j, (src, dst) in enumerate(((list_hbm, list_ref), (count_hbm, count_ref), (slip_hbm, slips)))
    ]
    for copy in copies:
        copy.start()
    row = lax.axis_index("rows")
    entry = lax.broadcasted_iota(jnp.int32, (events, entries), 1) + row * entries
    event = lax.broadcasted_iota(jnp.int32, (events, entries), 0)
    number[...] = jnp.full(number.shape, -1.0, jnp.float32)
    pieces = 2 * width
    rows = pieces * SUB
    i, j = (lax.broadcasted_iota(jnp.int32, (BLOCK, BLOCK), d) for d in (0, 1))
    lanes = jnp.concatenate([i < j, i >= 0], axis=1).astype(jnp.bfloat16)
    i, j = (lax.broadcasted_iota(jnp.int32, (rows, rows), d) for d in (0, 1))
    earlier = ((i // SUB == j // SUB) & (j % SUB < i % SUB)).astype(jnp.bfloat16)
    for copy in copies[:2]:
        copy.wait()
    count = jnp.zeros((events, entries), jnp.int32)
    for e in range(events):
        count = jnp.where(event == e, count_ref[e], count)
    number[0:events, 0:entries] = jnp.where(entry < count, list_ref[...], -1).astype(jnp.float32)
    ids = number[...]
    member = []
    for core in range(2):
        for c in range(width):
            low = float((2 * c + core) * blocks)
            member.append(((ids >= low) & (ids < low + blocks)).astype(jnp.float32))
    member = jnp.concatenate(member, axis=0)
    within = jnp.dot(member.astype(jnp.bfloat16), lanes, preferred_element_type=jnp.float32)
    total = within[:, BLOCK:]
    offset = jnp.dot(earlier, total.astype(jnp.bfloat16), preferred_element_type=jnp.float32)
    mark = jnp.where(jnp.max(offset + total) > SLOTS, 1.0, 0.0)
    rank = jnp.where(member > 0, within[:, :BLOCK] + offset, -1.0)
    left = jnp.zeros(ids.shape, jnp.bool_)
    for p in range(pieces):
        left = left | (rank[p * SUB : (p + 1) * SUB] >= SLOTS)
    left_ref[events] = pltpu.roll(jnp.where(left, ids, -1.0), row * entries, 1)

    i, j = (lax.broadcasted_iota(jnp.int32, (SUB, BLOCK), d) for d in (0, 1))
    here = j // entries == i

    def line_of(tile):
        moved = pltpu.roll(tile, 0, 1, stride=entries, stride_axis=0)
        return jnp.max(jnp.where(here, moved, -1.0), axis=0, keepdims=True)

    known = jnp.maximum(ids, 0.0)
    code = known - jnp.floor(known / blocks) * blocks + 1.0
    code += (lax.broadcasted_iota(jnp.int32, ids.shape, 0) * blocks).astype(jnp.float32)
    codes = jnp.broadcast_to(line_of(code), (SUB, BLOCK)).astype(jnp.bfloat16)
    slot = lax.broadcasted_iota(jnp.int32, (STRIDE, BLOCK), 0).astype(jnp.float32)
    picks = []
    for p in range(pieces):
        line = line_of(rank[p * SUB : (p + 1) * SUB])
        line = jnp.where(line < SLOTS, line, -1.0)
        picks.append((slot == jnp.broadcast_to(line, slot.shape)).astype(jnp.bfloat16))
    pick = jnp.concatenate(picks, axis=0)
    numbers = lax.dot_general(codes, pick, NT, preferred_element_type=jnp.float32)
    copies[2].wait()
    slip = jnp.concatenate([left_ref[e, 0:entries, :] for e in range(events)], axis=0)
    hi = slip.astype(jnp.bfloat16)
    lo = (slip - hi.astype(jnp.float32)).astype(jnp.bfloat16)
    size = events * entries
    data = jnp.dot(pick[:, :size], hi, preferred_element_type=jnp.float32)
    data += jnp.dot(pick[:, :size], lo, preferred_element_type=jnp.float32)
    last = lax.broadcasted_iota(jnp.int32, (STRIDE, BLOCK), 0) == SLOTS
    lane = lax.broadcasted_iota(jnp.int32, (1, BLOCK), 1)
    for p in range(pieces):
        start = p * STRIDE // BLOCK * BLOCK
        tile = numbers[0:1, start : start + BLOCK]
        shift = p * STRIDE - start
        tile = pltpu.roll(tile, BLOCK - shift, 1) if shift else tile
        tile = jnp.broadcast_to(jnp.where(lane < STRIDE, tile, mark), (STRIDE, BLOCK))
        piece = jnp.where(last, tile, data[p * STRIDE : (p + 1) * STRIDE])
        core, c = p // width, p % width
        height = out_ref.shape[0] // width
        for r in range(core, height, 2):
            out_ref[c * height + r] = piece


def expand_body(in_ref, out_ref, mark_ref):
    width, events, blocks, _ = out_ref.shape
    height = in_ref.shape[0] // width
    lane = lax.broadcasted_iota(jnp.int32, (1, BLOCK), 1)
    mark = jnp.zeros((1, BLOCK), jnp.float32)
    for c in range(width):
        numbers = jnp.zeros((1, BLOCK), jnp.float32)
        slip = []
        for r in range(height):
            piece = in_ref[c * height + r]
            info = piece[SLOTS : SLOTS + 1, :]
            mark = jnp.maximum(mark, jnp.where(lane >= STRIDE, info, 0.0))
            info = pltpu.roll(info, r * STRIDE, 1) if r else info
            numbers = jnp.where(lane // STRIDE == r, info, numbers)
            slip.append(piece)
        slip = jnp.concatenate(slip, axis=0)
        numbers = jnp.broadcast_to(numbers, (events * blocks, BLOCK))[:, : height * STRIDE]
        place = lax.broadcasted_iota(jnp.int32, numbers.shape, 0).astype(jnp.float32) + 1.0
        pick = (numbers == place).astype(jnp.bfloat16)
        hi = slip.astype(jnp.bfloat16)
        lo = (slip - hi.astype(jnp.float32)).astype(jnp.bfloat16)
        total = jnp.dot(pick, hi, preferred_element_type=jnp.float32)
        total += jnp.dot(pick, lo, preferred_element_type=jnp.float32)
        out_ref[c] = total.reshape(events, blocks, BLOCK)
    mark_ref[...] = jnp.broadcast_to(mark, mark_ref.shape)


def densify_body(sources, *refs):
    ins, (out_ref, slips) = refs[:-2], refs[-2:]
    width, events, blocks, _ = out_ref.shape
    live = slips.shape[1]
    entries = live // len(ins)
    row = lax.axis_index("rows")
    line = lax.broadcasted_iota(jnp.int32, (width * blocks, live), 0)
    number = ((line // blocks * 2 + row % 2) * blocks + line % blocks).astype(jnp.float32)
    for e in range(events):
        ids = jnp.full((1, BLOCK), -1.0, jnp.float32)
        for k, ref in zip(sources, ins):
            ids = jnp.maximum(ids, ref[events, e : e + 1, :])
            where = pl.ds(pl.multiple_of((row ^ k) * entries, entries), entries)
            slips[e, where, :] = ref[e, 0:entries, :]
        ids = jnp.broadcast_to(ids, (width * blocks, BLOCK))[:, :live]
        onehot = (ids == number).astype(jnp.bfloat16)
        slip = slips[e]
        hi = slip.astype(jnp.bfloat16)
        lo = (slip - hi.astype(jnp.float32)).astype(jnp.bfloat16)
        total = jnp.dot(onehot, hi, preferred_element_type=jnp.float32)
        total += jnp.dot(onehot, lo, preferred_element_type=jnp.float32)
        out_ref[:, e] = total.reshape(width, blocks, BLOCK)


def assemble(dense_ref, out_ref):
    events, blocks = out_ref.shape[0] // 2, dense_ref.shape[2]
    flat = dense_ref.reshape(events * blocks, BLOCK)
    for t in range(events // (2 * SUB)):
        for b in range(blocks):
            rows = [flat[pl.ds((2 * t + u) * SUB * blocks + b, SUB, stride=blocks), :] for u in range(2)]
            slip = jnp.concatenate(rows, axis=0)
            hi = slip.astype(jnp.bfloat16)
            lo = (slip - hi.astype(jnp.float32)).astype(jnp.bfloat16)
            where = slice(b * BLOCK, (b + 1) * BLOCK)
            out_ref[2 * t * SUB : 2 * (t + 1) * SUB, where] = hi
            out_ref[events + 2 * t * SUB : events + 2 * (t + 1) * SUB, where] = lo


def stress(k, other, slip_ref, kernel_ref):
    core = lax.axis_index("rows") % 2 ^ other
    events, patches = slip_ref.shape[0] // 2, slip_ref.shape[1]
    rows = kernel_ref.at[lax.axis_index("cols") ^ k]
    both = low = 0.0
    for t in range(0, patches, CHUNK):
        block = rows[:, pl.ds(pl.multiple_of(core * patches + t, CHUNK), CHUNK)]
        hi = block.astype(jnp.bfloat16)
        lo = (block - hi.astype(jnp.float32)).astype(jnp.bfloat16)
        both += lax.dot_general(slip_ref[:, t : t + CHUNK], hi, NT, preferred_element_type=jnp.float32)
        low += lax.dot_general(slip_ref[:events, t : t + CHUNK], lo, NT, preferred_element_type=jnp.float32)
    return both[:events] + both[events:] + low


def own_body(targets, dense_ref, kernel_ref, slip_ref, *out_refs):
    assemble(dense_ref, slip_ref)
    for group, out_ref in zip(targets, out_refs):
        for j, k in enumerate(group):
            out_ref[j] = stress(k, 0, slip_ref, kernel_ref)


def other_body(targets, dense_ref, kernel_ref, sum_ref, slip_ref, out_ref):
    assemble(dense_ref, slip_ref)
    rest_body(targets, slip_ref, kernel_ref, sum_ref, out_ref)


def rest_body(targets, slip_ref, kernel_ref, sum_ref, out_ref):
    for j, k in enumerate(targets):
        out_ref[j] = sum_ref[j] + stress(k, 1, slip_ref, kernel_ref)


def both_body(targets, own_ref, other_ref, kernel_ref, out_ref):
    for j, k in enumerate(targets):
        out_ref[j] = stress(k, 0, own_ref, kernel_ref) + stress(k, 1, other_ref, kernel_ref)


def per_device(kernel, slip_delta, block_list, live_count, direct_effect, load_rate, time_before):
    width = lax.axis_size("cols")
    height = lax.axis_size("rows")
    events_here, entries = block_list.shape
    events = events_here * width
    receivers, sources = kernel.shape
    blocks_here = sources // BLOCK

    share = receivers // width
    far_send, far_keep = [list(range(width // 2 + odd, width, 2)) for odd in (1, 0)]
    near_keep, near_send = [0, 1], list(range(2, width // 2))
    in_hbm = functools.partial(pltpu.with_memory_space_constraint, memory_space=pltpu.HBM)
    kernel = kernel.reshape(width, share, sources)
    blocks_half = blocks_here // 2
    message, left = pl.pallas_call(
        functools.partial(compact_body, width, blocks_half),
        out_shape=[f32(height * width, STRIDE, BLOCK), f32(events_here + 1, SUB, BLOCK)],
        in_specs=[HBM_SPEC] * 4,
        out_specs=[VMEM_SPEC] * 2,
        scratch_shapes=[
            pltpu.VMEM(block_list.shape, jnp.int32),
            pltpu.SMEM(live_count.shape, jnp.int32),
            pltpu.VMEM((SUB, BLOCK), jnp.float32),
            pltpu.SemaphoreType.DMA((3,)),
        ],
        compiler_params=params(16),
        name="compact",
    )(in_hbm(slip_delta), in_hbm(block_list), in_hbm(live_count), in_hbm(kernel))
    mine, mark = pl.pallas_call(
        expand_body,
        out_shape=[f32(width, events_here, blocks_half, BLOCK), f32(SUB, BLOCK)],
        in_specs=[VMEM_SPEC],
        out_specs=[VMEM_SPEC] * 2,
        compiler_params=params(16),
        name="expand",
    )(lax.all_to_all(message, ("cols", "rows"), 0, 0, tiled=True))

    def all_left(kernel, left):
        others = sorted(range(1, height), key=lambda k: (k < 2, k))
        dense = pl.pallas_call(
            functools.partial(densify_body, [0] + others),
            out_shape=f32(width, events_here, blocks_half, BLOCK),
            in_specs=[VMEM_SPEC] * height,
            out_specs=VMEM_SPEC,
            scratch_shapes=[pltpu.VMEM((events_here, height * entries, BLOCK), jnp.float32)],
            compiler_params=params(8),
            name="densify",
        )(left, *(send_xor(left, "rows", k) for k in others))
        return sum(stress_of(kernel, lax.all_to_all(dense, "cols", 0, 0, tiled=True)))

    def call(body, targets, outs, *args):
        return pl.pallas_call(
            functools.partial(body, targets),
            out_shape=outs,
            in_specs=[VMEM_SPEC] * len(args),
            out_specs=jax.tree.map(lambda _: VMEM_SPEC, outs),
            compiler_params=params(24),
            cost_estimate=pl.CostEstimate(
                flops=3 * receivers * sources * events // 2,
                bytes_accessed=receivers * sources,
                transcendentals=0,
            ),
            name=body.__name__.removesuffix("_body") + "_stress",
        )(*args)

    slips = bf16(2 * events, blocks_half * BLOCK)

    def sums(targets):
        return f32(len(targets), events, share)

    def stress_of(kernel, mine):
        came = send_xor(mine, "rows", 1)
        own, far_own, near_own = call(
            own_body, (far_send, near_send), [slips, sums(far_send), sums(near_send)], mine, kernel
        )
        other, far_sent = call(other_body, far_send, [slips, sums(far_send)], came, kernel, far_own)
        near_sent = call(rest_body, near_send, sums(near_send), other, kernel, near_own)

        def later(targets):
            return call(both_body, targets, sums(targets), own, other, kernel)

        far_came = send_xor(far_sent, "cols", 1)
        near_came = [send_xor(near_sent[j : j + 2], "cols", near_send[j]) for j in range(0, len(near_send), 2)]
        far = later(far_keep) + far_came
        near = sum(near_came, later(near_keep))
        parts = [send_xor(far[j], "cols", k) for j, k in reversed(list(enumerate(far_keep)))]
        parts.append(send_xor(near[1], "cols", 1))
        return [*parts, near[0]]

    *parts, first, mine_part = stress_of(kernel, mine)
    parts.append(mine_part)
    first, left = lax.optimization_barrier((first, left))
    parts.append(lax.cond(jnp.any(mark[0, STRIDE:] > 0), all_left, lambda *_: jnp.zeros_like(first), kernel, left))
    stress_change = sum(parts, first)
    scale = direct_effect[None, :]
    growth = jnp.expm1(load_rate * time_before / direct_effect)[None, :]
    log_time = jnp.log(scale / load_rate[None, :]) + jnp.log(
        jnp.log1p(jnp.exp(-stress_change / scale) * growth)
    )
    return (stress_change.T, log_time.T)


def solution(mesh):
    in_specs = (
        P("rows", "cols"),
        P("cols", "rows", None),
        P("cols", "rows"),
        P("cols"),
        P(("rows", "cols")),
        P(("rows", "cols")),
        P(("rows", "cols")),
    )
    out_specs = (P(("rows", "cols"), None), P(("rows", "cols"), None))
    return jax.shard_map(
        per_device, mesh=mesh, in_specs=in_specs, out_specs=out_specs, check_vma=False
    )
```

```python
import functools

import jax
import jax.numpy as jnp
from jax import lax
from jax.experimental import pallas as pl
from jax.experimental.pallas import tpu as pltpu
from jax.sharding import PartitionSpec as P

BLOCK = 128
SUB = 8
CHUNK = 256
SLOTS = 15
STRIDE = 16
VMEM_SPEC = pl.BlockSpec(memory_space=pltpu.VMEM)
HBM_SPEC = pl.BlockSpec(memory_space=pltpu.HBM)
MIB = 1024 * 1024
NT = (((1,), (1,)), ((), ()))


def f32(*shape):
    return jax.ShapeDtypeStruct(shape, jnp.float32)


def bf16(*shape):
    return jax.ShapeDtypeStruct(shape, jnp.bfloat16)


def params(mib):
    return pltpu.CompilerParams(vmem_limit_bytes=mib * MIB)


def send_xor(block, axis, k):
    return lax.ppermute(block, axis, [(r, r ^ k) for r in range(lax.axis_size(axis))])


def compact_body(
    width, blocks, slip_hbm, list_hbm, count_hbm, _, out_ref, left_ref, list_ref, count_ref, number, sems
):
    events, entries = list_ref.shape
    slips = left_ref.at[pl.ds(0, events), pl.ds(0, entries)]
    copies = [
        pltpu.make_async_copy(src, dst, sems.at[j])
        for j, (src, dst) in enumerate(((list_hbm, list_ref), (count_hbm, count_ref), (slip_hbm, slips)))
    ]
    for copy in copies:
        copy.start()
    row = lax.axis_index("rows")
    entry = lax.broadcasted_iota(jnp.int32, (events, entries), 1) + row * entries
    event = lax.broadcasted_iota(jnp.int32, (events, entries), 0)
    number[...] = jnp.full(number.shape, -1.0, jnp.float32)
    pieces = 2 * width
    rows = pieces * SUB
    i, j = (lax.broadcasted_iota(jnp.int32, (BLOCK, BLOCK), d) for d in (0, 1))
    lanes = jnp.concatenate([i < j, i >= 0], axis=1).astype(jnp.bfloat16)
    i, j = (lax.broadcasted_iota(jnp.int32, (rows, rows), d) for d in (0, 1))
    earlier = ((i // SUB == j // SUB) & (j % SUB < i % SUB)).astype(jnp.bfloat16)
    for copy in copies[:2]:
        copy.wait()
    count = jnp.zeros((events, entries), jnp.int32)
    for e in range(events):
        count = jnp.where(event == e, count_ref[e], count)
    number[0:events, 0:entries] = jnp.where(entry < count, list_ref[...], -1).astype(jnp.float32)
    ids = number[...]
    member = []
    for core in range(2):
        for c in range(width):
            low = float((2 * c + core) * blocks)
            member.append(((ids >= low) & (ids < low + blocks)).astype(jnp.float32))
    member = jnp.concatenate(member, axis=0)
    within = jnp.dot(member.astype(jnp.bfloat16), lanes, preferred_element_type=jnp.float32)
    total = within[:, BLOCK:]
    offset = jnp.dot(earlier, total.astype(jnp.bfloat16), preferred_element_type=jnp.float32)
    mark = jnp.where(jnp.max(offset + total) > SLOTS, 1.0, 0.0)
    rank = jnp.where(member > 0, within[:, :BLOCK] + offset, -1.0)
    left = jnp.zeros(ids.shape, jnp.bool_)
    for p in range(pieces):
        left = left | (rank[p * SUB : (p + 1) * SUB] >= SLOTS)
    left_ref[events] = pltpu.roll(jnp.where(left, ids, -1.0), row * entries, 1)

    i, j = (lax.broadcasted_iota(jnp.int32, (SUB, BLOCK), d) for d in (0, 1))
    here = j // entries == i

    def line_of(tile):
        moved = pltpu.roll(tile, 0, 1, stride=entries, stride_axis=0)
        return jnp.max(jnp.where(here, moved, -1.0), axis=0, keepdims=True)

    known = jnp.maximum(ids, 0.0)
    code = known - jnp.floor(known / blocks) * blocks + 1.0
    code += (lax.broadcasted_iota(jnp.int32, ids.shape, 0) * blocks).astype(jnp.float32)
    codes = jnp.broadcast_to(line_of(code), (SUB, BLOCK)).astype(jnp.bfloat16)
    slot = lax.broadcasted_iota(jnp.int32, (STRIDE, BLOCK), 0).astype(jnp.float32)
    picks = []
    for p in range(pieces):
        line = line_of(rank[p * SUB : (p + 1) * SUB])
        line = jnp.where(line < SLOTS, line, -1.0)
        picks.append((slot == jnp.broadcast_to(line, slot.shape)).astype(jnp.bfloat16))
    pick = jnp.concatenate(picks, axis=0)
    numbers = lax.dot_general(codes, pick, NT, preferred_element_type=jnp.float32)
    copies[2].wait()
    slip = jnp.concatenate([left_ref[e, 0:entries, :] for e in range(events)], axis=0)
    hi = slip.astype(jnp.bfloat16)
    lo = (slip - hi.astype(jnp.float32)).astype(jnp.bfloat16)
    size = events * entries
    data = jnp.dot(pick[:, :size], hi, preferred_element_type=jnp.float32)
    data += jnp.dot(pick[:, :size], lo, preferred_element_type=jnp.float32)
    last = lax.broadcasted_iota(jnp.int32, (STRIDE, BLOCK), 0) == SLOTS
    lane = lax.broadcasted_iota(jnp.int32, (1, BLOCK), 1)
    for p in range(pieces):
        start = p * STRIDE // BLOCK * BLOCK
        tile = numbers[0:1, start : start + BLOCK]
        shift = p * STRIDE - start
        tile = pltpu.roll(tile, BLOCK - shift, 1) if shift else tile
        tile = jnp.broadcast_to(jnp.where(lane < STRIDE, tile, mark), (STRIDE, BLOCK))
        piece = jnp.where(last, tile, data[p * STRIDE : (p + 1) * STRIDE])
        core, c = p // width, p % width
        height = out_ref.shape[0] // width
        for r in range(core, height, 2):
            out_ref[c * height + r] = piece


def expand_body(in_ref, out_ref, mark_ref):
    width, events, blocks, _ = out_ref.shape
    height = in_ref.shape[0] // width
    lane = lax.broadcasted_iota(jnp.int32, (1, BLOCK), 1)
    mark = jnp.zeros((1, BLOCK), jnp.float32)
    for c in range(width):
        numbers = jnp.zeros((1, BLOCK), jnp.float32)
        slip = []
        for r in range(height):
            piece = in_ref[c * height + r]
            info = piece[SLOTS : SLOTS + 1, :]
            mark = jnp.maximum(mark, jnp.where(lane >= STRIDE, info, 0.0))
            info = pltpu.roll(info, r * STRIDE, 1) if r else info
            numbers = jnp.where(lane // STRIDE == r, info, numbers)
            slip.append(piece)
        slip = jnp.concatenate(slip, axis=0)
        numbers = jnp.broadcast_to(numbers, (events * blocks, BLOCK))[:, : height * STRIDE]
        place = lax.broadcasted_iota(jnp.int32, numbers.shape, 0).astype(jnp.float32) + 1.0
        pick = (numbers == place).astype(jnp.bfloat16)
        hi = slip.astype(jnp.bfloat16)
        lo = (slip - hi.astype(jnp.float32)).astype(jnp.bfloat16)
        total = jnp.dot(pick, hi, preferred_element_type=jnp.float32)
        total += jnp.dot(pick, lo, preferred_element_type=jnp.float32)
        out_ref[c] = total.reshape(events, blocks, BLOCK)
    mark_ref[...] = jnp.broadcast_to(mark, mark_ref.shape)


def densify_body(sources, *refs):
    ins, (out_ref, slips) = refs[:-2], refs[-2:]
    width, events, blocks, _ = out_ref.shape
    live = slips.shape[1]
    entries = live // len(ins)
    row = lax.axis_index("rows")
    line = lax.broadcasted_iota(jnp.int32, (width * blocks, live), 0)
    number = ((line // blocks * 2 + row % 2) * blocks + line % blocks).astype(jnp.float32)
    for e in range(events):
        ids = jnp.full((1, BLOCK), -1.0, jnp.float32)
        for k, ref in zip(sources, ins):
            ids = jnp.maximum(ids, ref[events, e : e + 1, :])
            where = pl.ds(pl.multiple_of((row ^ k) * entries, entries), entries)
            slips[e, where, :] = ref[e, 0:entries, :]
        ids = jnp.broadcast_to(ids, (width * blocks, BLOCK))[:, :live]
        onehot = (ids == number).astype(jnp.bfloat16)
        slip = slips[e]
        hi = slip.astype(jnp.bfloat16)
        lo = (slip - hi.astype(jnp.float32)).astype(jnp.bfloat16)
        total = jnp.dot(onehot, hi, preferred_element_type=jnp.float32)
        total += jnp.dot(onehot, lo, preferred_element_type=jnp.float32)
        out_ref[:, e] = total.reshape(width, blocks, BLOCK)


def assemble(dense_ref, out_ref):
    events, blocks = out_ref.shape[0] // 2, dense_ref.shape[2]
    flat = dense_ref.reshape(events * blocks, BLOCK)
    for t in range(events // (2 * SUB)):
        for b in range(blocks):
            rows = [flat[pl.ds((2 * t + u) * SUB * blocks + b, SUB, stride=blocks), :] for u in range(2)]
            slip = jnp.concatenate(rows, axis=0)
            hi = slip.astype(jnp.bfloat16)
            lo = (slip - hi.astype(jnp.float32)).astype(jnp.bfloat16)
            where = slice(b * BLOCK, (b + 1) * BLOCK)
            out_ref[2 * t * SUB : 2 * (t + 1) * SUB, where] = hi
            out_ref[events + 2 * t * SUB : events + 2 * (t + 1) * SUB, where] = lo


def stress(k, other, slip_ref, kernel_ref):
    core = lax.axis_index("rows") % 2 ^ other
    events, patches = slip_ref.shape[0] // 2, slip_ref.shape[1]
    rows = kernel_ref.at[lax.axis_index("cols") ^ k]
    both = low = 0.0
    for t in range(0, patches, CHUNK):
        block = rows[:, pl.ds(pl.multiple_of(core * patches + t, CHUNK), CHUNK)]
        hi = block.astype(jnp.bfloat16)
        lo = (block - hi.astype(jnp.float32)).astype(jnp.bfloat16)
        both += lax.dot_general(slip_ref[:, t : t + CHUNK], hi, NT, preferred_element_type=jnp.float32)
        low += lax.dot_general(slip_ref[:events, t : t + CHUNK], lo, NT, preferred_element_type=jnp.float32)
    return both[:events] + both[events:] + low


def own_body(targets, dense_ref, kernel_ref, slip_ref, *out_refs):
    assemble(dense_ref, slip_ref)
    for group, out_ref in zip(targets, out_refs):
        for j, k in enumerate(group):
            out_ref[j] = stress(k, 0, slip_ref, kernel_ref)


def other_body(targets, dense_ref, kernel_ref, sum_ref, slip_ref, out_ref):
    assemble(dense_ref, slip_ref)
    rest_body(targets, slip_ref, kernel_ref, sum_ref, out_ref)


def rest_body(targets, slip_ref, kernel_ref, sum_ref, out_ref):
    for j, k in enumerate(targets):
        out_ref[j] = sum_ref[j] + stress(k, 1, slip_ref, kernel_ref)


def both_body(targets, own_ref, other_ref, kernel_ref, out_ref):
    for j, k in enumerate(targets):
        out_ref[j] = stress(k, 0, own_ref, kernel_ref) + stress(k, 1, other_ref, kernel_ref)


def per_device(kernel, slip_delta, block_list, live_count, direct_effect, load_rate, time_before):
    width = lax.axis_size("cols")
    height = lax.axis_size("rows")
    events_here, entries = block_list.shape
    events = events_here * width
    receivers, sources = kernel.shape
    blocks_here = sources // BLOCK

    share = receivers // width
    far_send, far_keep = [list(range(width // 2 + odd, width, 2)) for odd in (1, 0)]
    near_keep, near_send = [0, 1], list(range(2, width // 2))
    in_hbm = functools.partial(pltpu.with_memory_space_constraint, memory_space=pltpu.HBM)
    kernel = kernel.reshape(width, share, sources)
    blocks_half = blocks_here // 2
    message, left = pl.pallas_call(
        functools.partial(compact_body, width, blocks_half),
        out_shape=[f32(height * width, STRIDE, BLOCK), f32(events_here + 1, SUB, BLOCK)],
        in_specs=[HBM_SPEC] * 4,
        out_specs=[VMEM_SPEC] * 2,
        scratch_shapes=[
            pltpu.VMEM(block_list.shape, jnp.int32),
            pltpu.SMEM(live_count.shape, jnp.int32),
            pltpu.VMEM((SUB, BLOCK), jnp.float32),
            pltpu.SemaphoreType.DMA((3,)),
        ],
        compiler_params=params(16),
        name="compact",
    )(in_hbm(slip_delta), in_hbm(block_list), in_hbm(live_count), in_hbm(kernel))
    mine, mark = pl.pallas_call(
        expand_body,
        out_shape=[f32(width, events_here, blocks_half, BLOCK), f32(SUB, BLOCK)],
        in_specs=[VMEM_SPEC],
        out_specs=[VMEM_SPEC] * 2,
        compiler_params=params(16),
        name="expand",
    )(lax.all_to_all(message, ("cols", "rows"), 0, 0, tiled=True))

    def all_left(kernel, left):
        others = sorted(range(1, height), key=lambda k: (k < 2, k))
        dense = pl.pallas_call(
            functools.partial(densify_body, [0] + others),
            out_shape=f32(width, events_here, blocks_half, BLOCK),
            in_specs=[VMEM_SPEC] * height,
            out_specs=VMEM_SPEC,
            scratch_shapes=[pltpu.VMEM((events_here, height * entries, BLOCK), jnp.float32)],
            compiler_params=params(8),
            name="densify",
        )(left, *(send_xor(left, "rows", k) for k in others))
        return sum(stress_of(kernel, lax.all_to_all(dense, "cols", 0, 0, tiled=True)))

    def call(body, targets, outs, *args):
        return pl.pallas_call(
            functools.partial(body, targets),
            out_shape=outs,
            in_specs=[VMEM_SPEC] * len(args),
            out_specs=jax.tree.map(lambda _: VMEM_SPEC, outs),
            compiler_params=params(24),
            cost_estimate=pl.CostEstimate(
                flops=3 * receivers * sources * events // 2,
                bytes_accessed=receivers * sources,
                transcendentals=0,
            ),
            name=body.__name__.removesuffix("_body") + "_stress",
        )(*args)

    slips = bf16(2 * events, blocks_half * BLOCK)

    def sums(targets):
        return f32(len(targets), events, share)

    def stress_of(kernel, mine):
        came = send_xor(mine, "rows", 1)
        groups = (far_send, near_send, far_keep)
        own, far_own, near_own, kept_own = call(own_body, groups, [slips, *map(sums, groups)], mine, kernel)
        other, far_sent = call(other_body, far_send, [slips, sums(far_send)], came, kernel, far_own)
        near_sent = call(rest_body, near_send, sums(near_send), other, kernel, near_own)

        def later(targets):
            return call(both_body, targets, sums(targets), own, other, kernel)

        far_came = send_xor(far_sent, "cols", 1)
        near_came = [send_xor(near_sent[j : j + 2], "cols", near_send[j]) for j in range(0, len(near_send), 2)]
        far = call(rest_body, far_keep, sums(far_keep), other, kernel, kept_own) + far_came
        near = sum(near_came, later(near_keep))
        parts = [send_xor(far[j], "cols", k) for j, k in reversed(list(enumerate(far_keep)))]
        parts.append(send_xor(near[1], "cols", 1))
        return [*parts, near[0]]

    *parts, first, mine_part = stress_of(kernel, mine)
    parts.append(mine_part)
    first, left = lax.optimization_barrier((first, left))
    parts.append(lax.cond(jnp.any(mark[0, STRIDE:] > 0), all_left, lambda *_: jnp.zeros_like(first), kernel, left))
    stress_change = sum(parts, first)
    scale = direct_effect[None, :]
    growth = jnp.expm1(load_rate * time_before / direct_effect)[None, :]
    log_time = jnp.log(scale / load_rate[None, :]) + jnp.log(
        jnp.log1p(jnp.exp(-stress_change / scale) * growth)
    )
    return (stress_change.T, log_time.T)


def solution(mesh):
    in_specs = (
        P("rows", "cols"),
        P("cols", "rows", None),
        P("cols", "rows"),
        P("cols"),
        P(("rows", "cols")),
        P(("rows", "cols")),
        P(("rows", "cols")),
    )
    out_specs = (P(("rows", "cols"), None), P(("rows", "cols"), None))
    return jax.shard_map(
        per_device, mesh=mesh, in_specs=in_specs, out_specs=out_specs, check_vma=False
    )
```
